32 devices in a mesh: dp: 4 (over y, core), ctx: 8 (over z, x).
Axes of the slice: x: 2, y: 2, z: 4, core: 2. Of those that a mesh axis runs over, the one named last changes fastest.
Arguments:
- inputs: bfloat16 [8, 1024, 2048], P('dp', 'ctx'), may hold values from -6 to 6
- norm_gain: bfloat16 [2048], P(('dp', 'ctx')), may hold values from 0.25 to 1.75
- norm_bias: bfloat16 [2048], P(('dp', 'ctx')), may hold values from -3 to 3
- joined_weight: bfloat16 [2048, 6144], P(('dp', 'ctx')), may hold values from -0.125 to 0.125
- gate_weight: bfloat16 [2048, 5632], P(('dp', 'ctx')), may hold values from -0.125 to 0.125
- up_weight: bfloat16 [2048, 5632], P(('dp', 'ctx')), may hold values from -0.125 to 0.125
- out_weight: bfloat16 [2048, 2048], P(('dp', 'ctx')), may hold values from -3 to 3
- down_weight: bfloat16 [2048, 5632], P(('dp', 'ctx')), may hold values from -0.078125 to 0.078125
- cotangent: bfloat16 [8, 1024, 2048], P('dp', 'ctx'), may hold values from -6 to 6
- lengths: int32 [8], P('dp'), may hold values from 128 to 1024, as said below
Outputs:
- output: bfloat16 [8, 1024, 2048], P('dp', 'ctx')
- input_grad: bfloat16 [8, 1024, 2048], P('dp', 'ctx')
- gain_grad: float32 [2048], P(('dp', 'ctx'))
- bias_grad: float32 [2048], P(('dp', 'ctx'))
- joined_grad: float32 [2048, 6144], P(('dp', 'ctx'))
- gate_grad: float32 [2048, 5632], P(('dp', 'ctx'))
- up_grad: float32 [2048, 5632], P(('dp', 'ctx'))
- out_grad: float32 [2048, 2048], P(('dp', 'ctx'))
- down_grad: float32 [2048, 5632], P(('dp', 'ctx'))
The draws below stay inside these ranges and needn't reach their ends.
Inputs may be any that keep to these rules, and one draw needn't show every extreme that they name: `lengths`: of the 2 sequences on each index of dp, one drawn from the seed has all 1024 tokens; each other one has from 128 to 512 real tokens.
All inputs are finite; a program needn't handle non-finite values.
Results may differ from the reference program's by a relative error of at most 0.011.
Values may be sent and summed in bfloat16 or wider, within the bound.
No kernel may reach another device: no remote copies, remote signals or barrier semaphores. Data moves between devices by JAX's collectives and lax.ppermute only.
A program may use at most 640 MiB of HBM per device.

```python
import jax
import jax.numpy as jnp
from jax import lax

D = 2048
H = 32
HD = 64
ROT = 16
FF = 5632
SEQ_GROUP = 2
LENGTH = 1024
SEQS = 8


def draw_lengths(key, part):
    key = jax.random.fold_in(key, 7)
    short_key, pick_key = jax.random.split(key)
    groups = SEQS // SEQ_GROUP
    shorter = jax.random.randint(short_key, (groups, SEQ_GROUP), LENGTH // 8, LENGTH // 2 + 1)
    chosen = jax.random.randint(pick_key, (groups,), 0, SEQ_GROUP)
    select = jnp.arange(SEQ_GROUP)[None, :] == chosen[:, None]
    return jnp.where(select, LENGTH, shorter).reshape(SEQS).astype(jnp.int32)


def block_levels(own_key, extent, pieces, least, largest):
    def one(dim, blocks):
        heights = jax.random.uniform(jax.random.fold_in(jax.random.fold_in(own_key, 6), dim), (blocks,), jnp.float32, least / len(pieces), largest / len(pieces))
        return jnp.repeat(jnp.exp(heights), extent[dim] // blocks).reshape((-1,) + (1,) * (len(extent) - dim - 1))

    factor_of = one(*pieces[0])
    for cut in pieces[1:]:
        factor_of = factor_of * one(*cut)
    return factor_of


def normal_values(key, extent, spread, most, cuts=(), held_as=jnp.bfloat16):
    level = block_levels(key, extent, cuts, -0.22, 0.18) if cuts else 1.0
    array = jax.random.normal(key, extent, jnp.float32) * spread * level
    return jnp.minimum(jnp.maximum(array, -most), most).astype(held_as)


def setup_inputs(seed: int = 0) -> dict:
    splits = jax.random.split(jax.random.key(seed), 11)
    return {
        "inputs": normal_values(splits[0], (SEQS, LENGTH, D), 1.0, 6.0, ((0, 4), (1, 8))),
        "norm_gain": jnp.clip(1.0 + 0.15 * jax.random.normal(splits[1], (D,), jnp.float32), 0.25, 1.75).astype(jnp.bfloat16),
        "norm_bias": normal_values(splits[2], (D,), 0.5, 3.0, ((0, 32),)),
        "joined_weight": normal_values(splits[3], (D, 3 * D), D ** -0.5, 0.125, ((0, 32),)),
        "gate_weight": normal_values(splits[4], (D, FF), D ** -0.5, 0.125, ((0, 32),)),
        "up_weight": normal_values(splits[5], (D, FF), D ** -0.5, 0.125, ((0, 32),)),
        "out_weight": normal_values(splits[6], (D, D), (max(2, D // 512)) ** -0.5, 3.0, ((0, 32),)),
        "down_weight": normal_values(splits[7], (D, FF), FF ** -0.5, 0.078125, ((0, 32),)),
        "cotangent": normal_values(splits[8], (SEQS, LENGTH, D), 1.0, 6.0, ((0, 4), (1, 8))),
        "lengths": draw_lengths(jax.random.fold_in(splits[10], 71), 0),
    }


EPSILON = 1e-05
THETA = 10000.0
NEGATIVE = -1e+30
HIGHEST = lax.Precision.HIGHEST

@jax.custom_vjp
def low(v):
    return lax.optimization_barrier(v.astype(jnp.bfloat16)).astype(jnp.float32)

@jax.custom_vjp
def low_back(v):
    return v

def low_keep(v):
    return (low(v), None)

def low_pass(kept, grad):
    return (grad,)

def back_keep(v):
    return (v, None)

def back_low(kept, grad):
    return (low(grad),)
low.defvjp(low_keep, low_pass)
low_back.defvjp(back_keep, back_low)

def rotary_tables(positions):
    halfway = ROT // 2
    frequency = THETA ** (-(2.0 * jnp.arange(halfway, dtype=jnp.float32)) / ROT)
    angles = positions.astype(jnp.float32)[:, None] * frequency[None, :]
    return (jnp.cos(angles)[:, None, :], jnp.sin(angles)[:, None, :])

def rotate(tensor, cosine_table, sine_table):
    halfway = ROT // 2
    first = tensor[..., :halfway]
    second = tensor[..., halfway:ROT]
    return jnp.concatenate([first * cosine_table - second * sine_table, second * cosine_table + first * sine_table, tensor[..., ROT:]], axis=-1)

def attend_block(queries, keys, values, query_pos, length):
    key_pos = jnp.arange(keys.shape[0], dtype=jnp.int32)
    scores = low_back(jnp.einsum('qhd,khd->hqk', queries, keys, precision=HIGHEST) * 0.125)
    alive_rows = query_pos < length
    allowed = (key_pos[None, :] <= query_pos[:, None]) & alive_rows[:, None]
    masked = jnp.where(allowed[None], scores, NEGATIVE)
    row_max = lax.optimization_barrier(jnp.max(masked, axis=-1, keepdims=True))
    exponent = jnp.where(allowed[None], jnp.exp(masked - row_max), 0.0)
    totals = lax.optimization_barrier(jnp.sum(exponent, axis=-1, keepdims=True))
    probs = exponent / jnp.where(alive_rows[None, :, None], totals, 1.0)
    attended = jnp.einsum('hqk,khd->qhd', probs, values, precision=HIGHEST)
    return attended * alive_rows[:, None, None].astype(jnp.float32)

def one_sequence(hidden_in, norm_gain, norm_bias, joined_weight, gate_weight, up_weight, out_weight, down_weight, length):
    seq_len, features = hidden_in.shape
    center = hidden_in - lax.optimization_barrier(jnp.mean(hidden_in, axis=-1, keepdims=True))
    variance = lax.optimization_barrier(jnp.mean(center * center, axis=-1, keepdims=True))
    standard = center * lax.rsqrt(variance + EPSILON)
    normed = low(standard * norm_gain + norm_bias)
    projected = low_back(jnp.dot(normed, joined_weight, precision=HIGHEST))
    queries = projected[:, :features].reshape(seq_len, H, HD)
    keys = projected[:, features:2 * features].reshape(seq_len, H, HD)
    values = projected[:, 2 * features:].reshape(seq_len, H, HD)
    positions = jnp.arange(seq_len, dtype=jnp.int32)
    cosine_table, sine_table = rotary_tables(positions)
    queries_rot = low(rotate(queries, cosine_table, sine_table))
    keys_rot = low(rotate(keys, cosine_table, sine_table))
    values_low = low(values)
    gate_proj = low_back(jnp.dot(normed, gate_weight, precision=HIGHEST))
    up_proj = low_back(jnp.dot(normed, up_weight, precision=HIGHEST))
    hidden = low(jax.nn.silu(gate_proj) * up_proj)
    block_rows = min(512, seq_len)
    blocks = seq_len // block_rows

    def per_block(pair):
        return attend_block(pair[0], keys_rot, values_low, pair[1], length)
    attended = lax.map(jax.checkpoint(per_block), (queries_rot.reshape(blocks, block_rows, H, HD), positions.reshape(blocks, block_rows)))
    attn_rows = low(low_back(attended.reshape(seq_len, features)))
    branch_attn = jnp.dot(attn_rows, out_weight.T, precision=HIGHEST)
    branch_mlp = jnp.dot(hidden, down_weight.T, precision=HIGHEST)
    return hidden_in + branch_attn + branch_mlp

def reference(inputs, norm_gain, norm_bias, joined_weight, gate_weight, up_weight, out_weight, down_weight, cotangent, lengths):
    params = (norm_gain.astype(jnp.float32), norm_bias.astype(jnp.float32), joined_weight.astype(jnp.float32), gate_weight.astype(jnp.float32), up_weight.astype(jnp.float32), out_weight.astype(jnp.float32), down_weight.astype(jnp.float32))

    def step(totals, slices):
        seq_in, seq_cot, length = slices

        def forward(hidden_in, norm_g, norm_b, joined_w, gate_w, up_w, out_w, down_w):
            return one_sequence(hidden_in, norm_g, norm_b, joined_w, gate_w, up_w, out_w, down_w, length)
        result, pullback = jax.vjp(forward, seq_in.astype(jnp.float32), *params)
        grads = pullback(seq_cot.astype(jnp.float32))
        new_totals = tuple((total + grad for total, grad in zip(totals, grads[1:])))
        return (new_totals, (result.astype(jnp.bfloat16), grads[0].astype(jnp.bfloat16)))
    start_totals = tuple((jnp.zeros(param.shape, jnp.float32) for param in params))
    totals, (output, input_grad) = lax.scan(step, start_totals, (inputs, cotangent, lengths))
    return (output, input_grad, totals[0], totals[1], totals[2], totals[3], totals[4], totals[5], totals[6])
```

```python
import functools

import jax
import jax.numpy as jnp
from jax import lax
from jax.experimental import pallas as pl
from jax.experimental.pallas import tpu as pltpu
from jax.sharding import PartitionSpec as P

HD = 64
ROT = 16
EPSILON = 1e-05
THETA = 10000.0
NEGATIVE = -1e30
BF = jnp.bfloat16
F32 = jnp.float32
LAST = (((1,), (1,)), ((), ()))
FIRST = (((0,), (0,)), ((), ()))


def dot(left, right):
    return jnp.dot(left, right, preferred_element_type=F32)


def dot_last(left, right):
    return lax.dot_general(left, right, LAST, preferred_element_type=F32)


def dot_first(left, right):
    return lax.dot_general(left, right, FIRST, preferred_element_type=F32)


def rotary_tables(length, width):
    half = ROT // 2
    lane = jnp.arange(width, dtype=jnp.int32) % HD
    frequency = THETA ** (-(2.0 * (lane % half).astype(F32)) / ROT)
    angles = jnp.arange(length, dtype=jnp.int32).astype(F32)[:, None] * frequency[None, :]
    cosine = jnp.where(lane[None, :] < ROT, jnp.cos(angles), 1.0)
    sine = jnp.sin(angles)
    sine = jnp.where(lane[None, :] < half, -sine, jnp.where(lane[None, :] < ROT, sine, 0.0))
    return cosine, sine


def partner(x):
    half = ROT // 2
    lane = lax.broadcasted_iota(jnp.int32, x.shape, 1) % HD
    down = jnp.concatenate([x[:, half:], x[:, :half]], axis=1)
    up = jnp.concatenate([x[:, -half:], x[:, :-half]], axis=1)
    return jnp.where(lane < half, down, up)


def attend_forward(length_ref, joined_ref, cos_ref, sin_ref, rot_ref, attn_ref, lse_ref, total):
    parts, _, rows, triple = joined_ref.shape
    width = triple // 3
    length = parts * rows
    seq = pl.program_id(0)
    head = pl.program_id(1)
    alive_count = length_ref[seq]
    block = min(256, length)
    lane = lax.broadcasted_iota(jnp.int32, (1, width), 1)
    mine = (lane // HD) == head

    @pl.when(head == 0)
    def _():
        def rotated(start, scale):
            x = joined_ref[:, 0, :, start : start + width].reshape(length, width)
            x = x * cos_ref[...] + partner(x) * sin_ref[...]
            return (x.astype(BF) * scale).reshape(parts, rows, width)

        rot_ref[:, 0, :, :width] = rotated(0, 0.125)
        rot_ref[:, 0, :, width : 2 * width] = rotated(width, 1.0)
        rot_ref[:, 0, :, 2 * width :] = joined_ref[:, 0, :, 2 * width :].astype(BF)
        total[...] = jnp.zeros_like(total)
        lse_ref[...] = jnp.zeros_like(lse_ref)

    per = block // rows if block >= rows else 1
    block = per * rows
    for step in range(length // block):
        begin, end = step * per, (step + 1) * per
        stop = end * rows

        @pl.when(begin * rows < alive_count)
        def _(begin=begin, end=end, stop=stop):
            q = rot_ref[begin:end, 0, :, :width].reshape(block, width)
            q = jnp.where(mine, q, jnp.zeros_like(q))
            k = rot_ref[:end, 0, :, width : 2 * width].reshape(stop, width)
            v = rot_ref[:end, 0, :, 2 * width :].reshape(stop, width)
            scores = dot_last(q, k)
            q_pos = begin * rows + lax.broadcasted_iota(jnp.int32, (block, 1), 0)
            k_pos = lax.broadcasted_iota(jnp.int32, (block, stop), 1)
            scores = jnp.where(k_pos <= q_pos, scores, NEGATIVE)
            top = jnp.max(scores, axis=1, keepdims=True)
            expo = jnp.exp(scores - top)
            weight = jnp.sum(expo, axis=1, keepdims=True)
            out = dot(expo.astype(BF), v) / weight
            alive = q_pos < alive_count
            here = slice(begin * rows, stop)
            total[here, :] += jnp.where(mine & alive, out, 0.0)
            lse = jnp.where(alive, top + jnp.log(weight), 0.0)
            spot = lax.broadcasted_iota(jnp.int32, (1, lse_ref.shape[3]), 1) == head
            held = lse_ref[begin:end, 0].reshape(block, lse_ref.shape[3])
            lse_ref[begin:end, 0] = jnp.where(spot, lse, held).reshape(per, rows, -1)

    @pl.when(head == pl.num_programs(1) - 1)
    def _():
        attn_ref[:, 0] = total[...].astype(BF).reshape(parts, rows, width)


def attend_backward(
    length_ref, rot_ref, attn_ref, grad_ref, lse_ref, cos_ref, sin_ref, out_ref, dq, dk, dv
):
    parts, _, rows, triple = rot_ref.shape
    width = triple // 3
    length = parts * rows
    seq = pl.program_id(0)
    head = pl.program_id(1)
    alive_count = length_ref[seq]
    per = max(1, min(256, length) // rows)
    block = per * rows
    lane = lax.broadcasted_iota(jnp.int32, (1, width), 1)
    mine = (lane // HD) == head

    @pl.when(head == 0)
    def _():
        dq[...] = jnp.zeros_like(dq)
        dk[...] = jnp.zeros_like(dk)
        dv[...] = jnp.zeros_like(dv)

    for step in range(length // block):
        begin, end = step * per, (step + 1) * per
        stop = end * rows

        @pl.when(begin * rows < alive_count)
        def _(begin=begin, end=end, stop=stop):
            q_pos = begin * rows + lax.broadcasted_iota(jnp.int32, (block, 1), 0)
            alive = q_pos < alive_count
            q = rot_ref[begin:end, 0, :, :width].reshape(block, width)
            q = jnp.where(mine, q, jnp.zeros_like(q))
            k = rot_ref[:end, 0, :, width : 2 * width].reshape(stop, width)
            v = rot_ref[:end, 0, :, 2 * width :].reshape(stop, width)
            g = grad_ref[begin:end, 0].reshape(block, width)
            g = jnp.where(mine & alive, g, jnp.zeros_like(g))
            o = attn_ref[begin:end, 0].reshape(block, width)
            delta = jnp.sum(g.astype(F32) * o.astype(F32), axis=1, keepdims=True)
            held = lse_ref[begin:end, 0].reshape(block, lse_ref.shape[3])
            spot = lax.broadcasted_iota(jnp.int32, (1, lse_ref.shape[3]), 1) == head
            lse = jnp.sum(jnp.where(spot, held, 0.0), axis=1, keepdims=True)
            scores = dot_last(q, k)
            k_pos = lax.broadcasted_iota(jnp.int32, (block, stop), 1)
            probs = jnp.where((k_pos <= q_pos) & alive, jnp.exp(scores - lse), 0.0)
            d_probs = dot_last(g, v)
            d_scores = (probs * (d_probs - delta)).astype(BF)
            here = slice(begin * rows, stop)
            dq[here, :] += jnp.where(mine, dot(d_scores, k), 0.0)
            dk[:stop, :] += dot_first(d_scores, q)
            dv[:stop, :] += dot_first(probs.astype(BF), g)

    @pl.when(head == pl.num_programs(1) - 1)
    def _():
        def unrotated(x):
            return (x * cos_ref[...] - partner(x) * sin_ref[...]).astype(BF)

        shape = (parts, rows, width)
        out_ref[:, 0, :, :width] = unrotated(dq[...] * 0.125).reshape(shape)
        out_ref[:, 0, :, width : 2 * width] = unrotated(dk[...]).reshape(shape)
        out_ref[:, 0, :, 2 * width :] = dv[...].astype(BF).reshape(shape)


def attention_calls(parts, groups, rows, width, heads):
    length = parts * rows
    smem = pl.BlockSpec(memory_space=pltpu.SMEM)

    def spec(last):
        return pl.BlockSpec((parts, 1, rows, last), lambda s, h: (0, s, 0, 0))

    table = pl.BlockSpec((length, width), lambda s, h: (0, 0))

    def shape(last, dtype):
        return jax.ShapeDtypeStruct((parts, groups, rows, last), dtype)

    pairs = groups * heads * length * length // 2
    params = pltpu.CompilerParams(vmem_limit_bytes=48 * 1024 * 1024)
    forward = pl.pallas_call(
        attend_forward,
        grid=(groups, heads),
        in_specs=[smem, spec(3 * width), table, table],
        out_specs=[spec(3 * width), spec(width), spec(heads)],
        out_shape=[shape(3 * width, BF), shape(width, BF), shape(heads, F32)],
        scratch_shapes=[pltpu.VMEM((length, width), F32)],
        compiler_params=params,
        cost_estimate=pl.CostEstimate(
            flops=pairs * 1024, bytes_accessed=16 * length * width, transcendentals=pairs
        ),
        name="attend_forward",
    )
    backward = pl.pallas_call(
        attend_backward,
        grid=(groups, heads),
        in_specs=[smem, spec(3 * width), spec(width), spec(width), spec(heads), table, table],
        out_specs=spec(3 * width),
        out_shape=shape(3 * width, BF),
        scratch_shapes=[pltpu.VMEM((length, width), F32)] * 3,
        compiler_params=params,
        cost_estimate=pl.CostEstimate(
            flops=pairs * 2560, bytes_accessed=16 * length * width, transcendentals=pairs
        ),
        name="attend_backward",
    )
    return forward, backward


def on_device(
    n_ctx,
    n_dp,
    inputs,
    norm_gain,
    norm_bias,
    joined_weight,
    gate_weight,
    up_weight,
    out_weight,
    down_weight,
    cotangent,
    lengths,
):
    groups, rows, features = inputs.shape
    tokens = groups * rows
    own = norm_gain.shape[0]
    hidden_units = gate_weight.shape[1]
    width = features // n_ctx
    units = hidden_units // n_ctx
    heads = width // HD
    length = n_ctx * rows
    both = ("dp", "ctx")

    def split_columns(weight, last):
        return weight.reshape(own, -1, n_ctx, last).transpose(2, 1, 0, 3)

    narrow = jnp.concatenate(
        [split_columns(joined_weight, width), split_columns(out_weight, width)], axis=1
    )
    wide = jnp.concatenate(
        [split_columns(w, units) for w in (gate_weight, up_weight, down_weight)], axis=1
    )
    narrow = lax.all_to_all(narrow, "ctx", split_axis=0, concat_axis=0, tiled=True)
    wide = lax.all_to_all(wide, "ctx", split_axis=0, concat_axis=0, tiled=True)
    joined_part = narrow[:, :3].transpose(0, 2, 1, 3).reshape(n_ctx * own, 3 * width)

    def gather_rows(part):
        return lax.all_gather(part.reshape(n_ctx * own, -1), "dp", axis=0, tiled=True)

    w_joined = gather_rows(joined_part)
    w_gate, w_up = gather_rows(wide[:, 0]), gather_rows(wide[:, 1])
    w_out, w_down = gather_rows(narrow[:, 3]), gather_rows(wide[:, 2])

    scales = jnp.concatenate([norm_gain, norm_bias]).reshape(1, 2 * own)
    scales = lax.all_gather(scales, both, axis=0, tiled=True).astype(F32)
    gain = scales[:, :own].reshape(1, features)
    bias = scales[:, own:].reshape(1, features)
    flat_in = inputs.reshape(tokens, features).astype(F32)
    center = flat_in - jnp.mean(flat_in, axis=-1, keepdims=True)
    variance = jnp.mean(center * center, axis=-1, keepdims=True)
    inverse = lax.rsqrt(variance + EPSILON)
    standard = center * inverse
    normed_own = (standard * gain + bias).astype(BF)
    cot_own = cotangent.reshape(tokens, features)

    def gather_tokens(part):
        return lax.all_gather(part, "ctx", axis=0, tiled=True)

    def scatter_tokens(total):
        return lax.psum_scatter(total, "ctx", scatter_dimension=0, tiled=True)

    normed = gather_tokens(normed_own)
    cot = gather_tokens(cot_own)
    all_tokens = n_ctx * tokens

    forward, backward = attention_calls(n_ctx, groups, rows, width, heads)
    cosine, sine = rotary_tables(length, width)
    blocks = (n_ctx, groups, rows)
    joined = dot(normed, w_joined)
    rotated, attn, lse = forward(lengths, joined.reshape(*blocks, 3 * width), cosine, sine)
    attn_rows = attn.reshape(all_tokens, width)
    gate = dot(normed, w_gate)
    up = dot(normed, w_up)
    sigmoid = jax.nn.sigmoid(gate)
    silu = gate * sigmoid
    hidden = (silu * up).astype(BF)
    partial = (dot_last(attn_rows, w_out) + dot_last(hidden, w_down)).astype(BF)
    output = (flat_in + scatter_tokens(partial).astype(F32)).astype(BF)

    d_attn = dot(cot, w_out).astype(BF)
    d_hidden = dot(cot, w_down)
    d_gate = (d_hidden * up * sigmoid * (1.0 + gate * (1.0 - sigmoid))).astype(BF)
    d_up = (d_hidden * silu).astype(BF)
    d_joined = backward(
        lengths, rotated, attn, d_attn.reshape(*blocks, width), lse, cosine, sine
    ).reshape(all_tokens, 3 * width)

    normed_partial = (
        dot_last(d_gate, w_gate) + dot_last(d_up, w_up) + dot_last(d_joined, w_joined)
    ).astype(BF)
    d_normed = scatter_tokens(normed_partial).astype(F32)
    standard_grad = d_normed * gain
    centered = (
        standard_grad
        - jnp.mean(standard_grad, axis=-1, keepdims=True)
        - standard * jnp.mean(standard_grad * standard, axis=-1, keepdims=True)
    )
    input_grad = (cot_own.astype(F32) + inverse * centered).astype(BF)

    def reduce_rows(left, right):
        total = dot_first(left, right).astype(BF)
        total = lax.psum_scatter(total, "dp", scatter_dimension=0, tiled=True)
        return total.reshape(n_ctx, own, -1)

    g_down = reduce_rows(cot, hidden)
    g_gate = reduce_rows(normed, d_gate)
    g_up = reduce_rows(normed, d_up)
    g_out = reduce_rows(cot, attn_rows)
    g_joined = reduce_rows(normed, d_joined)
    g_wide = jnp.stack([g_gate, g_up, g_down], axis=1)
    g_narrow = jnp.concatenate(
        [
            g_joined.reshape(n_ctx, own, 3, width).transpose(0, 2, 1, 3),
            g_out.reshape(n_ctx, 1, own, width),
        ],
        axis=1,
    )
    g_wide = lax.all_to_all(g_wide, "ctx", split_axis=0, concat_axis=0, tiled=True)
    g_narrow = lax.all_to_all(g_narrow, "ctx", split_axis=0, concat_axis=0, tiled=True)

    def own_rows(pieces):
        return pieces.transpose(2, 1, 0, 3).reshape(own, -1).astype(F32)

    norm_sums = jnp.stack([jnp.sum(d_normed * standard, axis=0), jnp.sum(d_normed, axis=0)])
    norm_sums = norm_sums.reshape(2, n_ctx * n_dp, own).transpose(1, 0, 2).reshape(-1, 2 * own)
    norm_sums = lax.psum_scatter(norm_sums, both, scatter_dimension=0, tiled=True)
    return (
        output.reshape(inputs.shape),
        input_grad.reshape(inputs.shape),
        norm_sums[0, :own],
        norm_sums[0, own:],
        own_rows(g_narrow[:, :3]),
        own_rows(g_wide[:, :1]),
        own_rows(g_wide[:, 1:2]),
        own_rows(g_narrow[:, 3:]),
        own_rows(g_wide[:, 2:]),
    )


def solution(mesh):
    rows = P(("dp", "ctx"), None)
    vector = P(("dp", "ctx"))
    tokens = P("dp", "ctx", None)
    return jax.shard_map(
        functools.partial(on_device, mesh.shape["ctx"], mesh.shape["dp"]),
        mesh=mesh,
        in_specs=(tokens, vector, vector, rows, rows, rows, rows, rows, tokens, P("dp")),
        out_specs=(tokens, tokens, vector, vector, rows, rows, rows, rows, rows),
        check_vma=False,
    )
```

```python
import functools

import jax
import jax.numpy as jnp
from jax import lax
from jax.experimental import pallas as pl
from jax.experimental.pallas import tpu as pltpu
from jax.sharding import PartitionSpec as P

HD = 64
ROT = 16
EPSILON = 1e-05
THETA = 10000.0
NEGATIVE = -1e30
BF = jnp.bfloat16
F32 = jnp.float32
LAST = (((1,), (1,)), ((), ()))
FIRST = (((0,), (0,)), ((), ()))


def dot(left, right):
    return jnp.dot(left, right, preferred_element_type=F32)


def dot_last(left, right):
    return lax.dot_general(left, right, LAST, preferred_element_type=F32)


def dot_first(left, right):
    return lax.dot_general(left, right, FIRST, preferred_element_type=F32)


def rotary_tables(length, width):
    half = ROT // 2
    lane = jnp.arange(width, dtype=jnp.int32) % HD
    frequency = THETA ** (-(2.0 * (lane % half).astype(F32)) / ROT)
    angles = jnp.arange(length, dtype=jnp.int32).astype(F32)[:, None] * frequency[None, :]
    cosine = jnp.where(lane[None, :] < ROT, jnp.cos(angles), 1.0)
    sine = jnp.sin(angles)
    sine = jnp.where(lane[None, :] < half, -sine, jnp.where(lane[None, :] < ROT, sine, 0.0))
    return cosine, sine


def partner(x):
    half = ROT // 2
    lane = lax.broadcasted_iota(jnp.int32, x.shape, 1) % HD
    down = jnp.concatenate([x[:, half:], x[:, :half]], axis=1)
    up = jnp.concatenate([x[:, -half:], x[:, :-half]], axis=1)
    return jnp.where(lane < half, down, up)


def attend_forward(length_ref, slot_ref, joined_ref, cos_ref, sin_ref, rot_ref, attn_ref, lse_ref, total):
    parts, _, rows, triple = joined_ref.shape
    width = triple // 3
    length = parts * rows
    seq = pl.program_id(0)
    head = pl.program_id(1)
    alive_count = length_ref[seq]
    block = min(256, length)
    lane = lax.broadcasted_iota(jnp.int32, (1, width), 1)
    mine = (lane // HD) == head

    @pl.when(head == 0)
    def _():
        for part in range(parts):
            slot = slot_ref[part]
            here = slice(part * rows, (part + 1) * rows)

            def rotated(start):
                x = joined_ref[slot, 0, :, start : start + width]
                return (x * cos_ref[here, :] + partner(x) * sin_ref[here, :]).astype(BF)

            rot_ref[part, 0, :, :width] = rotated(0) * 0.125
            rot_ref[part, 0, :, width : 2 * width] = rotated(width)
            rot_ref[part, 0, :, 2 * width :] = joined_ref[slot, 0, :, 2 * width :].astype(BF)
        total[...] = jnp.zeros_like(total)
        lse_ref[...] = jnp.zeros_like(lse_ref)

    per = block // rows if block >= rows else 1
    block = per * rows
    for step in range(length // block):
        begin, end = step * per, (step + 1) * per
        stop = end * rows

        @pl.when(begin * rows < alive_count)
        def _(begin=begin, end=end, stop=stop):
            q = rot_ref[begin:end, 0, :, :width].reshape(block, width)
            q = jnp.where(mine, q, jnp.zeros_like(q))
            k = rot_ref[:end, 0, :, width : 2 * width].reshape(stop, width)
            v = rot_ref[:end, 0, :, 2 * width :].reshape(stop, width)
            scores = dot_last(q, k)
            q_pos = begin * rows + lax.broadcasted_iota(jnp.int32, (block, 1), 0)
            k_pos = lax.broadcasted_iota(jnp.int32, (block, stop), 1)
            scores = jnp.where(k_pos <= q_pos, scores, NEGATIVE)
            top = jnp.max(scores, axis=1, keepdims=True)
            expo = jnp.exp(scores - top)
            weight = jnp.sum(expo, axis=1, keepdims=True)
            out = dot(expo.astype(BF), v) / weight
            alive = q_pos < alive_count
            here = slice(begin * rows, stop)
            total[here, :] += jnp.where(mine & alive, out, 0.0)
            lse = jnp.where(alive, top + jnp.log(weight), 0.0)
            spot = lax.broadcasted_iota(jnp.int32, (1, lse_ref.shape[3]), 1) == head
            held = lse_ref[begin:end, 0].reshape(block, lse_ref.shape[3])
            lse_ref[begin:end, 0] = jnp.where(spot, lse, held).reshape(per, rows, -1)

    @pl.when(head == pl.num_programs(1) - 1)
    def _():
        for part in range(parts):
            attn_ref[slot_ref[part], 0] = total[part * rows : (part + 1) * rows, :].astype(BF)


def attend_backward(
    length_ref, slot_ref, rot_ref, attn_ref, grad_ref, lse_ref, cos_ref, sin_ref, out_ref, dq, dk, dv
):
    parts, _, rows, triple = rot_ref.shape
    width = triple // 3
    length = parts * rows
    seq = pl.program_id(0)
    head = pl.program_id(1)
    alive_count = length_ref[seq]
    per = max(1, min(256, length) // rows)
    block = per * rows
    lane = lax.broadcasted_iota(jnp.int32, (1, width), 1)
    mine = (lane // HD) == head

    @pl.when(head == 0)
    def _():
        dq[...] = jnp.zeros_like(dq)
        dk[...] = jnp.zeros_like(dk)
        dv[...] = jnp.zeros_like(dv)

    for step in range(length // block):
        begin, end = step * per, (step + 1) * per
        stop = end * rows

        @pl.when(begin * rows < alive_count)
        def _(begin=begin, end=end, stop=stop):
            q_pos = begin * rows + lax.broadcasted_iota(jnp.int32, (block, 1), 0)
            alive = q_pos < alive_count
            q = rot_ref[begin:end, 0, :, :width].reshape(block, width)
            q = jnp.where(mine, q, jnp.zeros_like(q))
            k = rot_ref[:end, 0, :, width : 2 * width].reshape(stop, width)
            v = rot_ref[:end, 0, :, 2 * width :].reshape(stop, width)
            slots = [slot_ref[part] for part in range(begin, end)]
            g = jnp.concatenate([grad_ref[slot, 0] for slot in slots], axis=0)
            g = jnp.where(mine & alive, g, jnp.zeros_like(g))
            o = jnp.concatenate([attn_ref[slot, 0] for slot in slots], axis=0)
            delta = jnp.sum(g.astype(F32) * o.astype(F32), axis=1, keepdims=True)
            held = lse_ref[begin:end, 0].reshape(block, lse_ref.shape[3])
            spot = lax.broadcasted_iota(jnp.int32, (1, lse_ref.shape[3]), 1) == head
            lse = jnp.sum(jnp.where(spot, held, 0.0), axis=1, keepdims=True)
            scores = dot_last(q, k)
            k_pos = lax.broadcasted_iota(jnp.int32, (block, stop), 1)
            probs = jnp.where((k_pos <= q_pos) & alive, jnp.exp(scores - lse), 0.0)
            d_probs = dot_last(g, v)
            d_scores = (probs * (d_probs - delta)).astype(BF)
            here = slice(begin * rows, stop)
            dq[here, :] += jnp.where(mine, dot(d_scores, k), 0.0)
            dk[:stop, :] += dot_first(d_scores, q)
            dv[:stop, :] += dot_first(probs.astype(BF), g)

    @pl.when(head == pl.num_programs(1) - 1)
    def _():
        for part in range(parts):
            slot = slot_ref[part]
            here = slice(part * rows, (part + 1) * rows)

            def unrotated(x):
                return (x * cos_ref[here, :] - partner(x) * sin_ref[here, :]).astype(BF)

            out_ref[slot, 0, :, :width] = unrotated(dq[here, :] * 0.125)
            out_ref[slot, 0, :, width : 2 * width] = unrotated(dk[here, :])
            out_ref[slot, 0, :, 2 * width :] = dv[here, :].astype(BF)


def attention_calls(parts, groups, rows, width, heads):
    length = parts * rows
    smem = pl.BlockSpec(memory_space=pltpu.SMEM)

    def spec(last):
        return pl.BlockSpec((parts, 1, rows, last), lambda s, h: (0, s, 0, 0))

    table = pl.BlockSpec((length, width), lambda s, h: (0, 0))

    def shape(last, dtype):
        return jax.ShapeDtypeStruct((parts, groups, rows, last), dtype)

    pairs = groups * heads * length * length // 2
    params = pltpu.CompilerParams(vmem_limit_bytes=48 * 1024 * 1024)
    forward = pl.pallas_call(
        attend_forward,
        grid=(groups, heads),
        in_specs=[smem, smem, spec(3 * width), table, table],
        out_specs=[spec(3 * width), spec(width), spec(heads)],
        out_shape=[shape(3 * width, BF), shape(width, BF), shape(heads, F32)],
        scratch_shapes=[pltpu.VMEM((length, width), F32)],
        compiler_params=params,
        cost_estimate=pl.CostEstimate(
            flops=pairs * 1024, bytes_accessed=16 * length * width, transcendentals=pairs
        ),
        name="attend_forward",
    )
    backward = pl.pallas_call(
        attend_backward,
        grid=(groups, heads),
        in_specs=[smem, smem, spec(3 * width), spec(width), spec(width), spec(heads), table, table],
        out_specs=spec(3 * width),
        out_shape=shape(3 * width, BF),
        scratch_shapes=[pltpu.VMEM((length, width), F32)] * 3,
        compiler_params=params,
        cost_estimate=pl.CostEstimate(
            flops=pairs * 2560, bytes_accessed=16 * length * width, transcendentals=pairs
        ),
        name="attend_backward",
    )
    return forward, backward


def pack_kernel(specs, n, own, *refs):
    sources, out_ref = refs[:-1], refs[-1]
    offset = 0
    for source, (repeat, width) in zip(sources, specs):
        for part in range(repeat):
            for dest in range(n):
                start = (part * n + dest) * width
                out_ref[dest, :, offset : offset + width] = source[:, start : start + width]
            offset += width


def unpack_kernel(specs, n, own, in_ref, *outs):
    offset = 0
    for out, (repeat, width) in zip(outs, specs):
        span = repeat * width
        for source in range(n):
            out[source * own : (source + 1) * own, :] = in_ref[source, :, offset : offset + span]
        offset += span


def pack_rows_kernel(specs, n, own, me_ref, *refs):
    sources, outs = refs[: len(specs)], refs[len(specs) :]
    for step, out in enumerate(outs):
        row = pl.multiple_of((me_ref[0] ^ step) * own, own)
        offset = 0
        for source, (repeat, width) in zip(sources, specs):
            span = repeat * width
            out[:, offset : offset + span] = source[pl.ds(row, own), :]
            offset += span


def unpack_rows_kernel(specs, n, own, me_ref, *refs):
    pieces, outs, held = refs[:n], refs[n:-1], refs[-1]
    for step, piece in enumerate(pieces):
        held[me_ref[0] ^ step] = piece[...]
    offset = 0
    for out, (repeat, width) in zip(outs, specs):
        for part in range(repeat):
            for source in range(n):
                start = (part * n + source) * width
                block = held[source, :, offset : offset + width]
                out[:, start : start + width] = block.astype(F32)
            offset += width


def total_width(specs):
    return sum(repeat * width for repeat, width in specs)


def in_vmem(kernel, name, out_shape, scratch=(), scalars=0):
    def call(*operands):
        places = [pltpu.SMEM] * scalars + [pltpu.VMEM] * (len(operands) - scalars)
        outs = jax.tree.map(lambda _: pl.BlockSpec(memory_space=pltpu.VMEM), out_shape)
        moved = sum(o.size * o.dtype.itemsize for o in operands)
        return pl.pallas_call(
            kernel,
            in_specs=[pl.BlockSpec(memory_space=place) for place in places],
            out_specs=outs,
            out_shape=out_shape,
            scratch_shapes=list(scratch),
            compiler_params=pltpu.CompilerParams(vmem_limit_bytes=48 * 1024 * 1024),
            cost_estimate=pl.CostEstimate(flops=0, bytes_accessed=3 * moved, transcendentals=0),
            name=name,
        )(*operands)

    return call


def pack_columns(specs, n, own, weights):
    shape = jax.ShapeDtypeStruct((n, own, total_width(specs)), BF)
    return in_vmem(functools.partial(pack_kernel, specs, n, own), "pack_columns", shape)(*weights)


def unpack_columns(specs, n, own, packed):
    shapes = [jax.ShapeDtypeStruct((n * own, repeat * width), BF) for repeat, width in specs]
    return in_vmem(functools.partial(unpack_kernel, specs, n, own), "unpack_columns", shapes)(
        packed
    )


def pack_rows(specs, n, own, me, gradients):
    shapes = [jax.ShapeDtypeStruct((own, total_width(specs)), BF)] * n
    kernel = functools.partial(pack_rows_kernel, specs, n, own)
    return in_vmem(kernel, "pack_rows", shapes, scalars=1)(me.reshape(1), *gradients)


def unpack_rows(specs, n, own, me, pieces):
    shapes = [jax.ShapeDtypeStruct((own, repeat * n * width), F32) for repeat, width in specs]
    kernel = functools.partial(unpack_rows_kernel, specs, n, own)
    held = pltpu.VMEM((n, own, total_width(specs)), BF)
    return in_vmem(kernel, "unpack_rows", shapes, scratch=[held], scalars=1)(
        me.reshape(1), *pieces
    )


class Layer:
    def __init__(self, n_ctx, slots, inputs, norm_gain, cotangent, lengths):
        self.groups, self.rows, self.features = inputs.shape
        self.tokens = self.groups * self.rows
        self.n_ctx, self.slots, self.lengths = n_ctx, slots, lengths
        self.own = norm_gain.shape[0]
        self.width = self.features // n_ctx
        self.flat = inputs.reshape(self.tokens, self.features).astype(F32)
        self.cot = cotangent.reshape(self.tokens, self.features)
        self.forward, self.backward = attention_calls(
            n_ctx, self.groups, self.rows, self.width, self.width // HD
        )
        self.tables = rotary_tables(n_ctx * self.rows, self.width)
        self.blocks = (n_ctx, self.groups, self.rows)

    def norm(self, scales):
        self.gain = scales[:, : self.own].astype(F32).reshape(1, self.features)
        bias = scales[:, self.own :].astype(F32).reshape(1, self.features)
        center = self.flat - jnp.mean(self.flat, axis=-1, keepdims=True)
        variance = jnp.mean(center * center, axis=-1, keepdims=True)
        self.inverse = lax.rsqrt(variance + EPSILON)
        self.standard = center * self.inverse
        return (self.standard * self.gain + bias).astype(BF)

    def attend(self, joined):
        joined = joined.reshape(*self.blocks, 3 * self.width)
        rotated, attn, lse = self.forward(self.lengths, self.slots, joined, *self.tables)
        return rotated, attn.reshape(-1, self.width), lse

    def attend_back(self, rotated, attn, d_attn, lse):
        shape = (*self.blocks, self.width)
        return self.backward(
            self.lengths,
            self.slots,
            rotated,
            attn.reshape(shape),
            d_attn.reshape(shape),
            lse,
            *self.tables,
        ).reshape(-1, 3 * self.width)

    def hide(self, gate, up):
        return (gate * jax.nn.sigmoid(gate) * up).astype(BF)

    def hide_back(self, d_hidden, gate, up):
        sigmoid = jax.nn.sigmoid(gate)
        d_gate = d_hidden * up * sigmoid * (1.0 + gate * (1.0 - sigmoid))
        return d_gate.astype(BF), (d_hidden * (gate * sigmoid)).astype(BF)

    def finish_output(self, branches):
        return (self.flat + branches.astype(F32)).astype(BF)

    def norm_back(self, d_normed):
        d_normed = d_normed.astype(F32)
        grad = d_normed * self.gain
        centered = (
            grad
            - jnp.mean(grad, axis=-1, keepdims=True)
            - self.standard * jnp.mean(grad * self.standard, axis=-1, keepdims=True)
        )
        sums = [jnp.sum(d_normed * self.standard, axis=0), jnp.sum(d_normed, axis=0)]
        sums = jnp.concatenate([v.reshape(-1, self.own) for v in sums], axis=1)
        return (self.cot.astype(F32) + self.inverse * centered).astype(BF), sums


def on_any_mesh(layer, specs, weights, scales):
    n, own = layer.n_ctx, layer.own
    both = ("dp", "ctx")
    me = jnp.zeros((), jnp.int32)

    def swap(pieces):
        return lax.all_to_all(pieces, "ctx", split_axis=0, concat_axis=0, tiled=True)

    parts = unpack_columns(specs, n, own, swap(pack_columns(specs, n, own, weights)))
    w_joined, w_out, w_gate, w_up, w_down = (
        lax.all_gather(part, "dp", axis=0, tiled=True) for part in parts
    )
    normed = layer.norm(lax.all_gather(scales, both, axis=0, tiled=True))
    normed, cot = (lax.all_gather(v, "ctx", axis=0, tiled=True) for v in (normed, layer.cot))
    rotated, attn, lse = layer.attend(dot(normed, w_joined))
    gate, up = dot(normed, w_gate), dot(normed, w_up)
    hidden = layer.hide(gate, up)
    branches = (dot_last(attn, w_out) + dot_last(hidden, w_down)).astype(BF)
    branches = lax.psum_scatter(branches, "ctx", scatter_dimension=0, tiled=True)
    d_gate, d_up = layer.hide_back(dot(cot, w_down), gate, up)
    d_joined = layer.attend_back(rotated, attn, dot(cot, w_out).astype(BF), lse)
    d_normed = dot_last(d_gate, w_gate) + dot_last(d_up, w_up) + dot_last(d_joined, w_joined)
    d_normed = lax.psum_scatter(d_normed.astype(BF), "ctx", scatter_dimension=0, tiled=True)
    pairs = [(normed, d_joined), (cot, attn), (normed, d_gate), (normed, d_up), (cot, hidden)]
    sums = [
        lax.psum_scatter(dot_first(*pair).astype(BF), "dp", scatter_dimension=0, tiled=True)
        for pair in pairs
    ]
    pieces = swap(jnp.stack(pack_rows(specs, n, own, me, sums)))
    grads = unpack_rows(specs, n, own, me, [pieces[i] for i in range(n)])
    input_grad, norm_sums = layer.norm_back(d_normed)
    norm_sums = lax.psum_scatter(norm_sums, both, scatter_dimension=0, tiled=True)
    return layer.finish_output(branches), input_grad, norm_sums, grads


def swaps(bit, n):
    return [(i, i ^ bit) for i in range(n)]


class State:
    def __init__(self, **arrays):
        self.held = arrays

    def __getitem__(self, name):
        return self.held[name]

    def drop(self, *names):
        for name in names:
            del self.held[name]

    def tick(self, before=(), sends=(), work=()):
        for action in before:
            self.held.update(action(self.held))
        view = dict(self.held)
        for name, source, axis, pairs in sends:
            view[name] = lax.ppermute(self.held[source], axis, pairs)
        for action in work:
            view.update(action(view))
        self.held = lax.optimization_barrier(view)


def on_grid(layer, specs, weights, scales):
    n, own, features = layer.n_ctx, layer.own, layer.features
    ctx, dp = lax.axis_index("ctx"), lax.axis_index("dp")
    z = ctx // 2
    inner = (z == 1) | (z == 2)
    quarter = features // 4
    side, pair = ("ctx", swaps(1, n)), ("ctx", swaps(2, n))
    middle = ("ctx", [(2, 4), (3, 5), (4, 2), (5, 3)])
    outward = ("ctx", [(2, 0), (3, 1), (4, 6), (5, 7)])
    inward = ("ctx", [(b, a) for a, b in outward[1]])
    core, across = ("dp", swaps(1, 4)), ("dp", swaps(2, 4))

    def blocks_of(v, first, steps):
        blocks = [
            lax.dynamic_slice_in_dim(v, (first ^ step) * quarter, quarter, 1) for step in steps
        ]
        return jnp.concatenate(blocks, axis=1)

    def reorder(v):
        return blocks_of(v, dp, (0, 2, 1, 3))

    def unorder(v):
        return blocks_of(v, (dp % 2) * 2 + dp // 2, (0, 2, 1, 3))

    def all_scales(s):
        held = s["scales"]
        for axis, bit, size in [("ctx", b, n) for b in (1, 2, 4)] + [("dp", b, 4) for b in (1, 2)]:
            mine = lax.axis_index(axis) // bit % 2
            got = lax.ppermute(held, axis, swaps(bit, size))
            first, second = jnp.where(mine == 0, held, got), jnp.where(mine == 0, got, held)
            held = jnp.concatenate([first, second], axis=0)
        return {"n0": reorder(layer.norm(held))}

    def weights_in(s):
        packed = pack_columns(specs, n, own, weights)
        packed = lax.all_to_all(packed, "ctx", split_axis=0, concat_axis=0, tiled=True)
        names = ("joined0", "out0", "gate0", "up0", "down0")
        return dict(zip(names, unpack_columns(specs, n, own, packed)))

    def joint(name, keys):
        return lambda s: {name: jnp.concatenate([s[key] for key in keys], axis=0)}

    def whole(name):
        return joint("w_" + name, [name + i for i in "0213"])

    def gathered(letter):
        return joint(letter, [letter + i for i in ("0", "0x", "1", "1x", "2", "2x", "3", "3x")])

    def select(name):
        return lambda s: {name: jnp.where(inner, s[name + "i"], s[name + "o"])}

    def plus(name, *parts):
        return lambda s: {name: sum(s[part].astype(F32) for part in parts).astype(BF)}

    def project(s):
        return {"joined": dot(s["n"], s["w_joined"])}

    def attend(s):
        rotated, attn, lse = layer.attend(s["joined"])
        return {"rotated": rotated, "attn": attn, "lse": lse}

    def gate(s):
        return {"gate": dot(s["n"], s["w_gate"])}

    def up(s):
        up = dot(s["n"], s["w_up"])
        return {"up": up, "hidden": layer.hide(s["gate"], up)}

    def two_slots(name, total, place):
        rows = total.shape[0] // 2
        return {f"{name}{place}k": total[:rows], f"{name}{place}a": total[rows:]}

    def rows_of(array, place):
        rows = array.shape[0] // 4
        return array[place * rows : (place + 1) * rows]

    def output_part(place):
        def work(s):
            total = dot_last(rows_of(s["attn"], place), s["w_out"])
            total += dot_last(rows_of(s["hidden"], place), s["w_down"])
            return two_slots("o", total.astype(BF), place)

        return work

    def normed_part(place):
        def work(s):
            total = dot_last(rows_of(s["d_gate"], place), s["w_gate"])
            total += dot_last(rows_of(s["d_up"], place), s["w_up"])
            total += dot_last(rows_of(s["d_joined"], place), s["w_joined"])
            return two_slots("d", total.astype(BF), place)

        return work

    def attn_back(s):
        return {"d_attn": dot(s["c"], s["w_out"]).astype(BF)}

    def hidden_back(s):
        d_gate, d_up = layer.hide_back(dot(s["c"], s["w_down"]), s["gate"], s["up"])
        return {"d_gate": d_gate, "d_up": d_up}

    def attend_back(s):
        d_joined = layer.attend_back(s["rotated"], s["attn"], s["d_attn"], s["lse"])
        return {"d_joined": d_joined}

    factors = {
        "joined": ("n", "d_joined"),
        "out": ("c", "attn"),
        "gate": ("n", "d_gate"),
        "up": ("n", "d_up"),
        "down": ("c", "hidden"),
    }

    def product(s, name, begin, end):
        left, right = factors[name]
        return dot_first(s[left][:, begin * quarter : end * quarter], s[right])

    def grad_a(name):
        return lambda s: {name + "A": product(s, name, 2, 4).astype(BF)}

    def grad_b(name):
        def work(s):
            total = product(s, name, 1, 2) + s[name + "Ar"][quarter:].astype(F32)
            return {name + "B": total.astype(BF)}

        return work

    def grad_c(name):
        def work(s):
            total = product(s, name, 0, 1) + s[name + "Ar"][:quarter].astype(F32)
            return {name + "C": (total + s[name + "Br"].astype(F32)).astype(BF)}

        return work

    def send_a(name):
        return (name + "Ar", name + "A", *core)

    def send_b(name):
        return (name + "Br", name + "B", *across)

    def swap_rows(names, chosen):
        def work(s):
            pieces = pack_rows(chosen, n, own, ctx, [s[name + "C"] for name in names])
            pieces = [
                lax.ppermute(piece, "ctx", swaps(step, n)) if step else piece
                for step, piece in enumerate(pieces)
            ]
            grads = unpack_rows(chosen, n, own, ctx, pieces)
            return {"g_" + name: grad for name, grad in zip(names, grads)}

        return work

    def norm_back(s):
        input_grad, sums = layer.norm_back(unorder(s["d"]))
        for axis, bit, size in [("dp", b, 4) for b in (2, 1)] + [("ctx", b, n) for b in (4, 2, 1)]:
            mine = lax.axis_index(axis) // bit % 2
            halves = sums.reshape(2, -1, sums.shape[1])
            first, second = halves[0], halves[1]
            give = jnp.where(mine == 0, second, first)
            keep = jnp.where(mine == 0, first, second)
            sums = keep + lax.ppermute(give, axis, swaps(bit, size))
        return {"input_grad": input_grad, "norm_sums": sums}

    def to(name, source, way):
        return (name, source, *way)

    def y(name):
        return (name + "2", name + "0", *across)

    def near(name):
        return (name + "1", name + "0", *core)

    def far(name):
        return (name + "3", name + "2", *core)

    st = State(scales=scales, c0=reorder(layer.cot))
    tick = st.tick
    tick(
        sends=[to("c0x", "c0", side), to("c1", "c0", pair), to("c2i", "c0", middle)],
        work=[all_scales, weights_in],
    )
    tick(
        sends=[
            to("n0x", "n0", side),
            to("n1", "n0", pair),
            to("n2i", "n0", middle),
            y("joined"),
            y("out"),
        ]
    )
    tick(
        sends=[
            to("n1x", "n1", side),
            to("n3i", "n1", middle),
            to("n2o", "n2i", outward),
            y("gate"),
            near("joined"),
        ]
    )
    tick(
        [select("n2")],
        [
            to("n2x", "n2", side),
            to("n3o", "n3i", outward),
            to("c3i", "c1", middle),
            y("up"),
            far("joined"),
        ],
    )
    tick(
        [select("n3")],
        [
            to("n3x", "n3", side),
            to("c2o", "c2i", outward),
            y("down"),
            near("out"),
            far("out"),
        ],
        [whole("joined")],
    )
    tick(
        (),
        [to("c1x", "c1", side), to("c3o", "c3i", outward), near("gate"), far("gate"), near("up")],
        [gathered("n"), project],
    )
    tick(
        [select("c2")],
        [to("c2x", "c2", side), far("up"), near("down"), far("down")],
        [attend, whole("gate"), gate],
    )
    tick(
        [select("c3")],
        [to("c3x", "c3", side)],
        [whole("up"), up, whole("out"), whole("down"), output_part(3)],
    )
    tick(
        (),
        [to("o3x", "o3a", side)],
        [output_part(2), gathered("c"), attn_back, output_part(1)],
    )
    tick(
        [plus("o3", "o3k", "o3x")],
        [to("o2x", "o2a", side), to("o3i", "o3", inward)],
        [hidden_back, output_part(0)],
    )
    tick(
        [plus("o2", "o2k", "o2x"), plus("o3", "o3", "o3i")],
        [to("o1x", "o1a", side), to("o2i", "o2", inward), to("o3m", "o3", middle)],
        [attend_back],
    )
    tick(
        [plus("o2", "o2", "o2i")],
        [to("o0x", "o0a", side), to("o2m", "o2", middle)],
        [normed_part(3), normed_part(2), grad_a("down")],
    )
    tick(
        [plus("o1", "o1k", "o1x", "o3m")],
        [to("o1p", "o1", pair), to("d3x", "d3a", side), send_a("down")],
        [normed_part(1), grad_b("down"), grad_a("gate")],
    )
    tick(
        [plus("o", "o0k", "o0x", "o2m", "o1p"), plus("d3", "d3k", "d3x")],
        [to("d2x", "d2a", side), to("d3i", "d3", inward), send_b("down"), send_a("gate")],
        [normed_part(0), grad_b("gate"), grad_a("up")],
    )
    tick(
        [plus("d2", "d2k", "d2x"), plus("d3", "d3", "d3i")],
        [
            to("d1x", "d1a", side),
            to("d2i", "d2", inward),
            to("d3m", "d3", middle),
            send_b("gate"),
            send_a("up"),
        ],
        [grad_c("down"), grad_b("up"), grad_a("joined")],
    )
    tick(
        [plus("d2", "d2", "d2i")],
        [to("d0x", "d0a", side), to("d2m", "d2", middle), send_b("up"), send_a("joined")],
        [grad_c("gate"), grad_b("joined"), grad_a("out")],
    )
    tick(
        [plus("d1", "d1k", "d1x", "d3m")],
        [to("d1p", "d1", pair), send_b("joined"), send_a("out")],
        [grad_c("up"), grad_b("out")],
    )
    wide, narrow = ("gate", "up", "down"), ("joined", "out")
    tick(
        [plus("d", "d0k", "d0x", "d2m", "d1p")],
        [send_b("out")],
        [swap_rows(wide, specs[2:]), grad_c("joined"), norm_back],
    )
    tick((), (), [grad_c("out"), swap_rows(narrow, specs[:2])])
    grads = [st["g_" + name] for name in narrow + wide]
    return layer.finish_output(unorder(st["o"])), st["input_grad"], st["norm_sums"], grads


def on_device(
    n_ctx,
    n_dp,
    inputs,
    norm_gain,
    norm_bias,
    joined_weight,
    gate_weight,
    up_weight,
    out_weight,
    down_weight,
    cotangent,
    lengths,
):
    grid = (n_ctx, n_dp) == (8, 4)
    if grid:
        ctx = lax.axis_index("ctx")
        z, x = ctx // 2, ctx % 2
        high = z >= 2
        order = [z, z ^ 1, jnp.where(high, 1, 2), jnp.where(high, 0, 3)]
        natural = [2 * o + (x ^ r) for o in order for r in range(2)]
        slots = jnp.zeros((n_ctx,), jnp.int32)
        for slot, part in enumerate(natural):
            slots = jnp.where(jnp.arange(n_ctx) == part, slot, slots)
    else:
        slots = jnp.arange(n_ctx, dtype=jnp.int32)
    layer = Layer(n_ctx, slots, inputs, norm_gain, cotangent, lengths)
    units = gate_weight.shape[1] // n_ctx
    specs = [(3, layer.width), (1, layer.width)] + [(1, units)] * 3
    weights = (joined_weight, out_weight, gate_weight, up_weight, down_weight)
    scales = jnp.concatenate([norm_gain, norm_bias]).reshape(1, 2 * layer.own)
    run = on_grid if grid else on_any_mesh
    output, input_grad, norm_sums, grads = run(layer, specs, weights, scales)
    joined_grad, out_grad, gate_grad, up_grad, down_grad = grads
    return (
        output.reshape(inputs.shape),
        input_grad.reshape(inputs.shape),
        norm_sums[0, : layer.own],
        norm_sums[0, layer.own :],
        joined_grad,
        gate_grad,
        up_grad,
        out_grad,
        down_grad,
    )


def solution(mesh):
    rows = P(("dp", "ctx"), None)
    vector = P(("dp", "ctx"))
    tokens = P("dp", "ctx", None)
    return jax.shard_map(
        functools.partial(on_device, mesh.shape["ctx"], mesh.shape["dp"]),
        mesh=mesh,
        in_specs=(tokens, vector, vector, rows, rows, rows, rows, rows, tokens, P("dp")),
        out_specs=(tokens, tokens, vector, vector, rows, rows, rows, rows, rows),
        check_vma=False,
    )
```

```python
import functools

import jax
import jax.numpy as jnp
from jax import lax
from jax.experimental import pallas as pl
from jax.experimental.pallas import tpu as pltpu
from jax.sharding import PartitionSpec as P

HD = 64
ROT = 16
EPSILON = 1e-05
THETA = 10000.0
NEGATIVE = -1e30
BF = jnp.bfloat16
F32 = jnp.float32
LAST = (((1,), (1,)), ((), ()))
FIRST = (((0,), (0,)), ((), ()))


def dot(left, right):
    return jnp.dot(left, right, preferred_element_type=F32)


def dot_last(left, right):
    return lax.dot_general(left, right, LAST, preferred_element_type=F32)


def dot_first(left, right):
    return lax.dot_general(left, right, FIRST, preferred_element_type=F32)


def rotary_tables(length, width):
    half = ROT // 2
    lane = jnp.arange(width, dtype=jnp.int32) % HD
    frequency = THETA ** (-(2.0 * (lane % half).astype(F32)) / ROT)
    angles = jnp.arange(length, dtype=jnp.int32).astype(F32)[:, None] * frequency[None, :]
    cosine = jnp.where(lane[None, :] < ROT, jnp.cos(angles), 1.0)
    sine = jnp.sin(angles)
    sine = jnp.where(lane[None, :] < half, -sine, jnp.where(lane[None, :] < ROT, sine, 0.0))
    return cosine, sine


def partner(x):
    half = ROT // 2
    lane = lax.broadcasted_iota(jnp.int32, x.shape, 1) % HD
    down = jnp.concatenate([x[:, half:], x[:, :half]], axis=1)
    up = jnp.concatenate([x[:, -half:], x[:, :-half]], axis=1)
    return jnp.where(lane < half, down, up)


def attend_forward(
    length_ref, slot_ref, joined_ref, cos_ref, sin_ref, wide_ref, rot_ref, attn_ref, lse_ref, total
):
    parts, _, rows, triple = joined_ref.shape
    width = triple // 3
    length = parts * rows
    seq = pl.program_id(0)
    head = pl.program_id(1)
    alive_count = length_ref[seq]
    block = min(256, length)
    lane = lax.broadcasted_iota(jnp.int32, (1, width), 1)
    mine = (lane // HD) == head

    @pl.when(head == 0)
    def _():
        for part in range(parts):
            slot = slot_ref[part]
            here = slice(part * rows, (part + 1) * rows)

            def rotated(start):
                x = joined_ref[slot, 0, :, start : start + width]
                return (x * cos_ref[here, :] + partner(x) * sin_ref[here, :]).astype(BF)

            rot_ref[part, 0, :, :width] = rotated(0) * 0.125
            rot_ref[part, 0, :, width : 2 * width] = rotated(width)
            rot_ref[part, 0, :, 2 * width :] = joined_ref[slot, 0, :, 2 * width :].astype(BF)
        total[...] = jnp.zeros_like(total)
        lse_ref[...] = jnp.zeros_like(lse_ref)

    per = block // rows if block >= rows else 1
    block = per * rows
    for step in range(length // block):
        begin, end = step * per, (step + 1) * per
        stop = end * rows

        @pl.when(begin * rows < alive_count)
        def _(begin=begin, end=end, stop=stop):
            q = rot_ref[begin:end, 0, :, :width].reshape(block, width)
            q = jnp.where(mine, q, jnp.zeros_like(q))
            k = rot_ref[:end, 0, :, width : 2 * width].reshape(stop, width)
            v = rot_ref[:end, 0, :, 2 * width :].reshape(stop, width)
            scores = dot_last(q, k)
            q_pos = begin * rows + lax.broadcasted_iota(jnp.int32, (block, 1), 0)
            k_pos = lax.broadcasted_iota(jnp.int32, (block, stop), 1)
            scores = jnp.where(k_pos <= q_pos, scores, NEGATIVE)
            top = jnp.max(scores, axis=1, keepdims=True)
            expo = jnp.exp(scores - top)
            weight = jnp.sum(expo, axis=1, keepdims=True)
            out = dot(expo.astype(BF), v) / weight
            alive = q_pos < alive_count
            here = slice(begin * rows, stop)
            total[here, :] += jnp.where(mine & alive, out, 0.0)
            lse = jnp.where(alive, top + jnp.log(weight), 0.0)
            spot = lax.broadcasted_iota(jnp.int32, (1, lse_ref.shape[3]), 1) == head
            held = lse_ref[begin:end, 0].reshape(block, lse_ref.shape[3])
            lse_ref[begin:end, 0] = jnp.where(spot, lse, held).reshape(per, rows, -1)

    @pl.when(head == pl.num_programs(1) - 1)
    def _():
        for part in range(parts):
            attn_ref[slot_ref[part], 0] = total[part * rows : (part + 1) * rows, :].astype(BF)


def attend_backward(
    length_ref, slot_ref, rot_ref, attn_ref, grad_ref, lse_ref, cos_ref, sin_ref, out_ref, dq, dk, dv
):
    parts, _, rows, triple = rot_ref.shape
    width = triple // 3
    length = parts * rows
    seq = pl.program_id(0)
    head = pl.program_id(1)
    alive_count = length_ref[seq]
    per = max(1, min(256, length) // rows)
    block = per * rows
    lane = lax.broadcasted_iota(jnp.int32, (1, width), 1)
    mine = (lane // HD) == head

    @pl.when(head == 0)
    def _():
        dq[...] = jnp.zeros_like(dq)
        dk[...] = jnp.zeros_like(dk)
        dv[...] = jnp.zeros_like(dv)

    for step in range(length // block):
        begin, end = step * per, (step + 1) * per
        stop = end * rows

        @pl.when(begin * rows < alive_count)
        def _(begin=begin, end=end, stop=stop):
            q_pos = begin * rows + lax.broadcasted_iota(jnp.int32, (block, 1), 0)
            alive = q_pos < alive_count
            q = rot_ref[begin:end, 0, :, :width].reshape(block, width)
            q = jnp.where(mine, q, jnp.zeros_like(q))
            k = rot_ref[:end, 0, :, width : 2 * width].reshape(stop, width)
            v = rot_ref[:end, 0, :, 2 * width :].reshape(stop, width)
            slots = [slot_ref[part] for part in range(begin, end)]
            g = jnp.concatenate([grad_ref[slot, 0] for slot in slots], axis=0)
            g = jnp.where(mine & alive, g, jnp.zeros_like(g))
            o = jnp.concatenate([attn_ref[slot, 0] for slot in slots], axis=0)
            delta = jnp.sum(g.astype(F32) * o.astype(F32), axis=1, keepdims=True)
            held = lse_ref[begin:end, 0].reshape(block, lse_ref.shape[3])
            spot = lax.broadcasted_iota(jnp.int32, (1, lse_ref.shape[3]), 1) == head
            lse = jnp.sum(jnp.where(spot, held, 0.0), axis=1, keepdims=True)
            scores = dot_last(q, k)
            k_pos = lax.broadcasted_iota(jnp.int32, (block, stop), 1)
            probs = jnp.where((k_pos <= q_pos) & alive, jnp.exp(scores - lse), 0.0)
            d_probs = dot_last(g, v)
            d_scores = (probs * (d_probs - delta)).astype(BF)
            here = slice(begin * rows, stop)
            dq[here, :] += jnp.where(mine, dot(d_scores, k), 0.0)
            dk[:stop, :] += dot_first(d_scores, q)
            dv[:stop, :] += dot_first(probs.astype(BF), g)

    @pl.when(head == pl.num_programs(1) - 1)
    def _():
        for part in range(parts):
            slot = slot_ref[part]
            here = slice(part * rows, (part + 1) * rows)

            def unrotated(x):
                return (x * cos_ref[here, :] - partner(x) * sin_ref[here, :]).astype(BF)

            out_ref[slot, 0, :, :width] = unrotated(dq[here, :] * 0.125)
            out_ref[slot, 0, :, width : 2 * width] = unrotated(dk[here, :])
            out_ref[slot, 0, :, 2 * width :] = dv[here, :].astype(BF)


def attention_calls(parts, groups, rows, width, heads, lanes):
    length = parts * rows
    smem = pl.BlockSpec(memory_space=pltpu.SMEM)

    def spec(last):
        return pl.BlockSpec((parts, 1, rows, last), lambda s, h: (0, s, 0, 0))

    table = pl.BlockSpec((length, width), lambda s, h: (0, 0))

    def shape(last, dtype):
        return jax.ShapeDtypeStruct((parts, groups, rows, last), dtype)

    pairs = groups * heads * length * length // 2
    params = pltpu.CompilerParams(vmem_limit_bytes=48 * 1024 * 1024)
    forward = pl.pallas_call(
        attend_forward,
        grid=(groups, heads),
        in_specs=[smem, smem, spec(3 * width), table, table, pl.BlockSpec(memory_space=pl.ANY)],
        out_specs=[spec(3 * width), spec(width), spec(heads)],
        out_shape=[shape(3 * width, BF), shape(lanes, BF), shape(heads, F32)],
        scratch_shapes=[pltpu.VMEM((length, width), F32)],
        input_output_aliases={5: 1},
        compiler_params=params,
        cost_estimate=pl.CostEstimate(
            flops=pairs * 1024, bytes_accessed=16 * length * width, transcendentals=pairs
        ),
        name="attend_forward",
    )
    backward = pl.pallas_call(
        attend_backward,
        grid=(groups, heads),
        in_specs=[smem, smem, spec(3 * width), spec(width), spec(width), spec(heads), table, table],
        out_specs=spec(3 * width),
        out_shape=shape(3 * width, BF),
        scratch_shapes=[pltpu.VMEM((length, width), F32)] * 3,
        compiler_params=params,
        cost_estimate=pl.CostEstimate(
            flops=pairs * 2560, bytes_accessed=16 * length * width, transcendentals=pairs
        ),
        name="attend_backward",
    )
    return forward, backward


class Plan:
    def __init__(self, n, own, width, units):
        self.n, self.own, self.width, self.units = n, own, width, units
        self.body = units // 128 * 128
        self.tail = units - self.body
        self.joined = 3 * width
        self.first = self.joined + 2 * units
        self.used = width + units
        self.second = self.used + own
        spans = [(0, r * n * width, width, width) for r in range(3)]
        for start, span in ((0, self.body), (self.body, self.tail)):
            spans += [(w, start, units, span) for w in (2, 3)]
        self.spans = [*spans, (1, 0, width, width), (4, 0, units, units)]

    def segments(self):
        lane = 0
        for weight, start, stride, span in self.spans:
            yield weight, start, stride, lane, span
            lane += span


def pack_kernel(plan, *refs):
    scale_ref, sources, out_ref = refs[0], refs[1:-1], refs[-1]
    for dest in range(plan.n):
        for weight, start, stride, lane, span in plan.segments():
            begin = start + dest * stride
            out_ref[dest, :, lane : lane + span] = sources[weight][:, begin : begin + span]
        out_ref[dest, :, plan.first + plan.used :] = scale_ref[...]


def unpack_kernel(plan, outs_of, in_ref, *outs):
    own = plan.own
    for out, (source, sources, lane, lanes) in zip(outs, outs_of):
        for index in range(sources):
            block = in_ref[source + index, :, lane : lane + lanes]
            out[index * own : (index + 1) * own, :] = block
    for source in range(plan.n):
        outs[-1][source] = in_ref[source, :, plan.first + plan.used :]


def pack_rows_kernel(own, n_sources, me_ref, *refs):
    sources, outs = refs[:n_sources], refs[n_sources:]
    for step, out in enumerate(outs):
        row = pl.multiple_of((me_ref[0] ^ step) * own, own)
        lane = 0
        for source in sources:
            lanes = source.shape[1]
            out[:, lane : lane + lanes] = source[pl.ds(row, own), :]
            lane += lanes


def unpack_rows_kernel(n, own, layout, me_ref, *refs):
    pieces, outs, held = refs[:n], refs[n:-1], refs[-1]
    for step, piece in enumerate(pieces):
        held[me_ref[0] ^ step] = piece[...]
    for source in range(n):
        for out, start, stride, lane, span in layout:
            begin = start + source * stride
            block = held[source, :, lane : lane + span].astype(F32)
            outs[out][:, begin : begin + span] = block


def in_vmem(kernel, name, out_shape, scratch=(), scalars=0):
    def call(*operands):
        places = [pltpu.SMEM] * scalars + [pltpu.VMEM] * (len(operands) - scalars)
        outs = jax.tree.map(lambda _: pl.BlockSpec(memory_space=pltpu.VMEM), out_shape)
        moved = sum(o.size * o.dtype.itemsize for o in operands)
        return pl.pallas_call(
            kernel,
            in_specs=[pl.BlockSpec(memory_space=place) for place in places],
            out_specs=outs,
            out_shape=out_shape,
            scratch_shapes=list(scratch),
            compiler_params=pltpu.CompilerParams(vmem_limit_bytes=48 * 1024 * 1024),
            cost_estimate=pl.CostEstimate(flops=0, bytes_accessed=3 * moved, transcendentals=0),
            name=name,
        )(*operands)

    return call


def pack_columns(plan, weights, scales):
    shape = jax.ShapeDtypeStruct((plan.n, plan.own, plan.first + plan.second), BF)
    scales = jnp.pad(scales.reshape(2, plan.own), ((0, plan.own - 2), (0, 0)))
    return in_vmem(functools.partial(pack_kernel, plan), "pack_columns", shape)(scales, *weights)


def unpack_columns(plan, packed):
    n, own = plan.n, plan.own
    outs_of = [(half * n // 2, n // 2, 0, plan.first) for half in range(2)]
    outs_of.append((0, n, plan.first, plan.second))
    shapes = [jax.ShapeDtypeStruct((c * own, lanes), BF) for _, c, _, lanes in outs_of]
    shapes.append(jax.ShapeDtypeStruct((n, own, own), BF))
    kernel = functools.partial(unpack_kernel, plan, outs_of)
    *parts, scales = in_vmem(kernel, "unpack_columns", shapes)(packed)
    return parts, scales[:, :2]


def pack_rows(own, n, me, gradients):
    lanes = sum(g.shape[1] for g in gradients)
    shapes = [jax.ShapeDtypeStruct((own, lanes), BF)] * n
    kernel = functools.partial(pack_rows_kernel, own, len(gradients))
    return in_vmem(kernel, "pack_rows", shapes, scalars=1)(me.reshape(1), *gradients)


def unpack_rows(plan, me, pieces):
    layout = list(plan.segments())
    widths = [3 * plan.width, plan.width, plan.units, plan.units, plan.units]
    shapes = [jax.ShapeDtypeStruct((plan.own, plan.n * w), F32) for w in widths]
    kernel = functools.partial(unpack_rows_kernel, plan.n, plan.own, layout)
    held = pltpu.VMEM((plan.n, plan.own, pieces[0].shape[1]), BF)
    return in_vmem(kernel, "unpack_rows", shapes, scratch=[held], scalars=1)(
        me.reshape(1), *pieces
    )


def fetch_pieces(pieces, held, sems):
    rows = pieces[0].shape[0]
    return [
        pltpu.make_async_copy(piece, held.at[pl.ds(i * rows, rows), :], sems.at[i])
        for i, piece in enumerate(pieces)
    ]


def stream_kernel(n, n_pieces, n_extra, n_into, finish, *refs):
    blocks, refs = refs[:n], refs[n:]
    pieces, refs = refs[:n_pieces], refs[n_pieces + n_into :]
    extra, outs, (held, rows_ref, rows_sem, weight_sem) = refs[:n_extra], refs[n_extra:-4], refs[-4:]
    size = blocks[0].shape[0]
    step = pl.program_id(0)
    steps = n // 2
    weight = fetch_pieces(pieces, held, weight_sem)

    def copy(block, buffer, half):
        there = rows_ref.at[buffer, pl.ds(half * size, size), :]
        return pltpu.make_async_copy(block, there, rows_sem.at[buffer, half])

    def fetch(index):
        for place in range(steps):

            @pl.when(index == place)
            def _(place=place):
                for half in range(2):
                    copy(blocks[2 * place + half], place % 2, half).start()

    @pl.when(step == 0)
    def _():
        fetch(0)
        for piece in weight:
            piece.start()

    @pl.when(step + 1 < steps)
    def _():
        fetch(step + 1)

    buffer = lax.rem(step, 2)
    for half in range(2):
        copy(blocks[half], buffer, half).wait()

    @pl.when(step == 0)
    def _():
        for piece in weight:
            piece.wait()

    rows = rows_ref[buffer]
    outs[0][...] = rows
    finish(rows, held, extra, outs[1:])


def stream(name, blocks, pieces, extra, finish, outs, all_blocks, into=()):
    size, features = blocks[0].shape
    n = len(blocks)
    first = (all_blocks - n) // 2 if into else 0
    anywhere = pl.BlockSpec(memory_space=pl.ANY)

    def rows(width):
        return pl.BlockSpec((2 * size, width), lambda i: (first + i, 0))

    outs = [(features, BF), *outs]
    width = pieces[0].shape[1]
    begin = n + len(pieces)
    return pl.pallas_call(
        functools.partial(stream_kernel, n, len(pieces), len(extra), len(into), finish),
        grid=(n // 2,),
        in_specs=[anywhere] * (begin + len(into)) + [rows(e.shape[1]) for e in extra],
        out_specs=[rows(w) for w, _ in outs],
        out_shape=[jax.ShapeDtypeStruct((all_blocks * size, w), dtype) for w, dtype in outs],
        input_output_aliases={begin + i: i for i in range(len(into))},
        scratch_shapes=[
            pltpu.VMEM((features, width), BF),
            pltpu.VMEM((2, 2 * size, features), BF),
            pltpu.SemaphoreType.DMA((2, 2)),
            pltpu.SemaphoreType.DMA((len(pieces),)),
        ],
        compiler_params=pltpu.CompilerParams(vmem_limit_bytes=52 * 1024 * 1024),
        cost_estimate=pl.CostEstimate(
            flops=2 * n * size * features * width,
            bytes_accessed=2 * (n * size + width) * features * 2,
            transcendentals=0,
        ),
        name=name,
    )(*blocks, *pieces, *into, *extra)


def swiglu(plan, both):
    body, tail = plan.body, plan.tail
    hidden, factors = [], []
    for start, span in ((0, body), (2 * body, tail)):
        gate, up = both[:, start : start + span], both[:, start + span : start + 2 * span]
        sigmoid = jax.nn.sigmoid(gate)
        silu = gate * sigmoid
        hidden.append((silu * up).astype(BF))
        factors += [up * sigmoid * (1.0 + gate * (1.0 - sigmoid)), silu]
    return hidden, factors


def project_finish(plan, rows, held, extra, outs):
    joined, factor_ref, wide = outs
    joined[...] = dot(rows, held[:, : plan.joined])
    hidden, factors = swiglu(plan, dot(rows, held[:, plan.joined :]))
    lane = 0
    for factor in factors:
        factor_ref[:, lane : lane + factor.shape[1]] = factor
        lane += factor.shape[1]
    wide[:, : plan.width] = jnp.zeros((rows.shape[0], plan.width), BF)
    wide[:, plan.width : plan.width + plan.body] = hidden[0]
    pad = jnp.zeros((rows.shape[0], plan.second - plan.used), BF)
    wide[:, plan.width + plan.body :] = jnp.concatenate([hidden[1], pad], axis=1)


def return_finish(plan, rows, held, extra, outs):
    (factor_ref,), (d_attn, d_both) = extra, outs
    total = dot(rows, held[...])
    d_attn[...] = total[:, : plan.width].astype(BF)
    begin, body, tail = plan.width, plan.body, plan.tail
    for lane, start, span in (
        (0, begin, body),
        (body, begin, body),
        (2 * body, begin + body, tail),
        (2 * body + tail, begin + body, tail),
    ):
        here = slice(lane, lane + span)
        d_both[:, here] = (total[:, start : start + span] * factor_ref[:, here]).astype(BF)


def spread_kernel(count, n_pieces, places, *refs):
    lefts, refs = refs[: count * places], refs[count * places :]
    pieces, outs, (held, sems) = refs[:n_pieces], refs[n_pieces:-2], refs[-2:]
    weight = fetch_pieces(pieces, held, sems)
    for piece in weight:
        piece.start()
    size = outs[0].shape[0]
    each = n_pieces // 4
    rows = each * pieces[0].shape[0]
    for part in range(4):
        here = slice(part * rows, (part + 1) * rows)
        for piece in weight[part * each : (part + 1) * each]:
            piece.wait()
        for place in range(places):
            total, lane = 0.0, 0
            for left in lefts[place * count : (place + 1) * count]:
                lanes = left.shape[1]
                total += dot_last(left[...], held[here, lane : lane + lanes])
                lane += lanes
            outs[2 * place][:, here] = total[:size].astype(BF)
            outs[2 * place + 1][:, here] = total[size:].astype(BF)


def spread(name, lefts, pieces, places, size):
    anywhere = pl.BlockSpec(memory_space=pl.ANY)
    features = len(pieces) * pieces[0].shape[0]
    width = pieces[0].shape[1]
    tokens = 2 * size * len(places)

    def rows(left, place):
        return pl.BlockSpec((2 * size, left.shape[1]), lambda i: (place, 0))

    blocks = 2 * len(places)
    return pl.pallas_call(
        functools.partial(spread_kernel, len(lefts), len(pieces), len(places)),
        grid=(1,),
        in_specs=[rows(left, place) for place in places for left in lefts]
        + [anywhere] * len(pieces),
        out_specs=[pl.BlockSpec((size, features), lambda i: (0, 0))] * blocks,
        out_shape=[jax.ShapeDtypeStruct((size, features), BF)] * blocks,
        scratch_shapes=[
            pltpu.VMEM((features, width), BF),
            pltpu.SemaphoreType.DMA((len(pieces),)),
        ],
        compiler_params=pltpu.CompilerParams(vmem_limit_bytes=52 * 1024 * 1024),
        cost_estimate=pl.CostEstimate(
            flops=2 * tokens * features * width,
            bytes_accessed=2 * (tokens + features) * width + 2 * tokens * features,
            transcendentals=0,
        ),
        name=name,
    )(*[left for _ in places for left in lefts], *pieces)


class Layer:
    def __init__(self, n_ctx, slots, inputs, norm_gain, cotangent, lengths, units):
        self.groups, self.rows, self.features = inputs.shape
        self.tokens = self.groups * self.rows
        self.n_ctx, self.slots, self.lengths = n_ctx, slots, lengths
        self.own = norm_gain.shape[0]
        self.width = self.features // n_ctx
        self.plan = Plan(n_ctx, self.own, self.width, units)
        self.flat = inputs.reshape(self.tokens, self.features).astype(F32)
        self.cot = cotangent.reshape(self.tokens, self.features)
        self.tables = rotary_tables(n_ctx * self.rows, self.width)
        self.blocks = (n_ctx, self.groups, self.rows)

    def calls(self, lanes):
        heads = self.width // HD
        return attention_calls(self.n_ctx, self.groups, self.rows, self.width, heads, lanes)

    def standardize(self):
        center = self.flat - jnp.mean(self.flat, axis=-1, keepdims=True)
        variance = jnp.mean(center * center, axis=-1, keepdims=True)
        inverse = lax.rsqrt(variance + EPSILON)
        return center * inverse, inverse

    def norm(self, standard, scales):
        gain = scales[:, 0].astype(F32).reshape(1, self.features)
        bias = scales[:, 1].astype(F32).reshape(1, self.features)
        return (standard * gain + bias).astype(BF), gain

    def attend(self, joined, wide):
        lanes = wide.shape[1]
        shape = (*self.blocks, lanes)
        joined = joined.reshape(*self.blocks, 3 * self.width)
        rotated, wide, lse = self.calls(lanes)[0](
            self.lengths, self.slots, joined, *self.tables, wide.reshape(shape)
        )
        return rotated, wide.reshape(-1, lanes), lse

    def attend_back(self, rotated, wide, d_attn, lse):
        lanes = wide.shape[1]
        return self.calls(lanes)[1](
            self.lengths,
            self.slots,
            rotated,
            wide.reshape(*self.blocks, lanes),
            d_attn.reshape(*self.blocks, self.width),
            lse,
            *self.tables,
        ).reshape(-1, 3 * self.width)

    def finish_output(self, branches):
        return (self.flat + branches.astype(F32)).astype(BF)

    def norm_back(self, d_normed, standard, inverse, gain):
        d_normed = d_normed.astype(F32)
        grad = d_normed * gain
        centered = (
            grad
            - jnp.mean(grad, axis=-1, keepdims=True)
            - standard * jnp.mean(grad * standard, axis=-1, keepdims=True)
        )
        sums = [jnp.sum(d_normed * standard, axis=0), jnp.sum(d_normed, axis=0)]
        sums = jnp.concatenate([v.reshape(-1, self.own) for v in sums], axis=1)
        return (self.cot.astype(F32) + inverse * centered).astype(BF), sums


def on_any_mesh(layer, weights, scales):
    plan = layer.plan
    n, own, width = plan.n, plan.own, plan.width
    me = jnp.zeros((), jnp.int32)

    def swap(pieces):
        return lax.all_to_all(pieces, "ctx", split_axis=0, concat_axis=0, tiled=True)

    def gather(v, axis):
        return lax.all_gather(v, axis, axis=0, tiled=True)

    def scatter(v, axis):
        return lax.psum_scatter(v, axis, scatter_dimension=0, tiled=True)

    parts, scales = unpack_columns(plan, swap(pack_columns(plan, weights, scales)))
    w_first = gather(jnp.concatenate(parts[:2], axis=0), "dp")
    w_second = gather(parts[2], "dp")[:, : plan.used]
    standard, inverse = layer.standardize()
    normed, gain = layer.norm(standard, gather(scales, "dp"))
    normed, cot = gather(normed, "ctx"), gather(layer.cot, "ctx")
    total = dot(normed, w_first)
    hidden, factors = swiglu(plan, total[:, plan.joined :])
    empty = jnp.zeros((normed.shape[0], width), BF)
    rotated, attn, lse = layer.attend(total[:, : plan.joined], empty)
    wide = jnp.concatenate([attn, *hidden], axis=1)
    branches = scatter(dot_last(wide, w_second).astype(BF), "ctx")
    total = dot(cot, w_second)
    body = total[:, width : width + plan.body]
    tail = total[:, width + plan.body :]
    d_both = jnp.concatenate([body, body, tail, tail], axis=1) * jnp.concatenate(factors, axis=1)
    d_joined = layer.attend_back(rotated, attn, total[:, :width].astype(BF), lse)
    d_first = jnp.concatenate([d_joined, d_both.astype(BF)], axis=1)
    d_normed = scatter(dot_last(d_first, w_first).astype(BF), "ctx")
    sums = [scatter(dot_first(*v).astype(BF), "dp") for v in ((normed, d_first), (cot, wide))]
    pieces = list(swap(jnp.stack(pack_rows(own, n, me, sums))))
    grads = unpack_rows(plan, me, pieces)
    input_grad, norm_sums = layer.norm_back(d_normed, standard, inverse, gain)
    return layer.finish_output(branches), input_grad, scatter(norm_sums, ("dp", "ctx")), grads


def swaps(bit, n):
    return [(i, i ^ bit) for i in range(n)]


class State:
    def __init__(self, **arrays):
        self.held = arrays

    def __getitem__(self, name):
        return self.held[name]

    def drop(self, *names):
        for name in names:
            del self.held[name]

    def tick(self, before=(), sends=(), work=()):
        for action in before:
            self.held.update(action(self.held))
        view = dict(self.held)
        for name, source, axis, pairs in sends:
            view[name] = lax.ppermute(self.held[source], axis, pairs)
        for action in work:
            view.update(action(view))
        self.held = lax.optimization_barrier(view)


def on_grid(layer, weights, scales):
    plan = layer.plan
    n, own, features = plan.n, plan.own, layer.features
    ctx, dp = lax.axis_index("ctx"), lax.axis_index("dp")
    z = ctx // 2
    inner = (z == 1) | (z == 2)
    quarter = features // 4
    side, pair = ("ctx", swaps(1, n)), ("ctx", swaps(2, n))
    middle = ("ctx", [(2, 4), (3, 5), (4, 2), (5, 3)])
    outward = ("ctx", [(2, 0), (3, 1), (4, 6), (5, 7)])
    inward = ("ctx", [(b, a) for a, b in outward[1]])
    core, across = ("dp", swaps(1, 4)), ("dp", swaps(2, 4))

    def blocks_of(v, first, steps):
        blocks = [
            lax.dynamic_slice_in_dim(v, (first ^ step) * quarter, quarter, 1) for step in steps
        ]
        return jnp.concatenate(blocks, axis=1)

    def reorder(v):
        return blocks_of(v, dp, (0, 2, 1, 3))

    def unorder(v):
        return blocks_of(v, (dp % 2) * 2 + dp // 2, (0, 2, 1, 3))

    def weights_in(s):
        packed = pack_columns(plan, weights, scales)
        packed = lax.all_to_all(packed, "ctx", split_axis=0, concat_axis=0, tiled=True)
        parts, held = unpack_columns(plan, packed)
        return {"a0": parts[0], "b0": parts[1], "w0": parts[2], "scales": held}

    def standardize(s):
        standard, inverse = layer.standardize()
        return {"standard": standard, "inverse": inverse}

    def normalize(s):
        held = s["scales"]
        for bit in (1, 2):
            mine = dp // bit % 2
            got = lax.ppermute(held, "dp", swaps(bit, 4))
            first, second = jnp.where(mine == 0, held, got), jnp.where(mine == 0, got, held)
            held = jnp.concatenate([first, second], axis=0)
        normed, gain = layer.norm(s["standard"], held)
        return {"n0": reorder(normed), "gain": gain}

    def select(name):
        return lambda s: {name: jnp.where(inner, s[name + "i"], s[name + "o"])}

    def plus(name, *parts):
        return lambda s: {name: sum(s[part].astype(F32) for part in parts).astype(BF)}

    def pieces(s, *names):
        return [s[name + i] for i in "0213" for name in names]

    def slots(s, letter):
        return [s.get(letter + i) for i in ("0", "0x", "1", "1x", "2", "2x", "3", "3x")]

    def project(half):
        names = ("n", "joined", "factors", "wide")

        def work(s):
            outs = [(plan.joined, F32), (2 * plan.units, F32), (plan.second, BF)]
            finish = functools.partial(project_finish, plan)
            blocks = slots(s, "n")[half * n // 2 : (half + 1) * n // 2]
            into = [s[name] for name in names] if half else []
            made = stream("project", blocks, pieces(s, "a", "b"), [], finish, outs, n, into)
            return dict(zip(names, made))

        return work

    def attend(s):
        return dict(zip(("rotated", "wide", "lse"), layer.attend(s["joined"], s["wide"])))

    def bring_back(s):
        outs = [(plan.width, BF), (2 * plan.units, BF)]
        finish = functools.partial(return_finish, plan)
        made = stream(
            "bring_back", slots(s, "c"), pieces(s, "w"), [s["factors"]], finish, outs, n
        )
        return dict(zip(("c", "d_attn", "d_both"), made))

    def attend_back(s):
        d_joined = layer.attend_back(s["rotated"], s["wide"], s["d_attn"], s["lse"])
        return {"d_joined": d_joined}

    def scattered(name, letter, lefts, weight, places):
        def work(s):
            size = s["c0"].shape[0]
            made = spread(name, [s[v] for v in lefts], pieces(s, *weight), places, size)
            keys = [f"{letter}{place}{kind}" for place in places for kind in "ka"]
            return dict(zip(keys, made))

        return work

    def output_part(*places):
        return scattered("output_part", "o", ["wide"], "w", places)

    def normed_part(*places):
        return scattered("normed_part", "d", ["d_joined", "d_both"], "ab", places)

    factors = {"J": ("n", "d_joined"), "G": ("n", "d_both"), "W": ("c", "wide")}

    def product(s, name, begin, end):
        left, right = factors[name]
        return dot_first(s[left][:, begin * quarter : end * quarter], s[right])

    def grad_a(name):
        return lambda s: {name + "A": product(s, name, 2, 4).astype(BF)}

    def grad_b(name):
        def work(s):
            total = product(s, name, 1, 2) + s[name + "Ar"][quarter:].astype(F32)
            return {name + "B": total.astype(BF)}

        return work

    def grad_c(name):
        def work(s):
            total = product(s, name, 0, 1) + s[name + "Ar"][:quarter].astype(F32)
            return {name + "C": (total + s[name + "Br"].astype(F32)).astype(BF)}

        return work

    def to(name, source, way):
        return (name, source, *way)

    def send_a(name):
        return to(name + "Ar", name + "A", core)

    def send_b(name):
        return to(name + "Br", name + "B", across)

    def deal(s):
        dealt = pack_rows(own, n, ctx, [s[name + "C"] for name in "JGW"])
        return {f"q{step}": piece for step, piece in enumerate(dealt)}

    def swap(step):
        return to(f"q{step}r", f"q{step}", ("ctx", swaps(step, n)))

    def undeal(s):
        held = [s["q0"]] + [s[f"q{step}r"] for step in range(1, n)]
        grads = unpack_rows(plan, ctx, held)
        return {f"grad{weight}": grad for weight, grad in enumerate(grads)}

    def norm_back(s):
        input_grad, sums = layer.norm_back(unorder(s["d"]), s["standard"], s["inverse"], s["gain"])
        for axis, bit, size in [("dp", b, 4) for b in (2, 1)] + [("ctx", b, n) for b in (4, 2, 1)]:
            mine = lax.axis_index(axis) // bit % 2
            halves = sums.reshape(2, -1, sums.shape[1])
            first, second = halves[0], halves[1]
            give = jnp.where(mine == 0, second, first)
            keep = jnp.where(mine == 0, first, second)
            sums = keep + lax.ppermute(give, axis, swaps(bit, size))
        return {"input_grad": input_grad, "norm_sums": sums}

    def y(name):
        return to(name + "2", name + "0", across)

    def near(name):
        return to(name + "1", name + "0", core)

    def far(name):
        return to(name + "3", name + "2", core)

    st = State(c0=reorder(layer.cot))
    tick = st.tick
    tick((), [to("c0x", "c0", side), to("c1", "c0", pair)], [weights_in, standardize])
    tick(
        [normalize],
        [to("n0x", "n0", side), to("n1", "n0", pair), to("n2i", "n0", middle), y("a"), near("a")],
    )
    tick(
        (),
        [
            to("n1x", "n1", side),
            to("n3i", "n1", middle),
            to("n2o", "n2i", outward),
            y("b"),
            far("a"),
        ],
    )
    tick(
        [select("n2")],
        [
            to("n2x", "n2", side),
            to("n3o", "n3i", outward),
            to("c2i", "c0", middle),
            near("b"),
            far("b"),
        ],
    )
    tick(
        [select("n3")],
        [
            to("n3x", "n3", side),
            to("c3i", "c1", middle),
            to("c2o", "c2i", outward),
            y("w"),
            near("w"),
        ],
        [project(0)],
    )
    tick(
        [select("c2")],
        [to("c2x", "c2", side), to("c3o", "c3i", outward), far("w")],
        [project(1), attend],
    )
    tick(
        [select("c3")],
        [to("c3x", "c3", side), to("c1x", "c0x", pair)],
        [output_part(1, 3), output_part(0, 2)],
    )
    tick((), [to("o3x", "o3a", side), to("o1p", "o1a", pair)], [bring_back, grad_a("W")])
    tick(
        [plus("o3", "o3k", "o3x")],
        [to("o2x", "o2a", side), to("o3i", "o3", inward), send_a("W")],
        [attend_back],
    )
    tick(
        [plus("o2", "o2k", "o2x"), plus("o3", "o3", "o3i"), plus("o0a", "o0a", "o1p")],
        [to("o0x", "o0a", side), to("o2i", "o2", inward), to("o3m", "o3", middle)],
        [normed_part(1, 3), grad_b("W")],
    )
    tick(
        [plus("o2", "o2", "o2i"), plus("o1", "o1k", "o3m")],
        [to("d3x", "d3a", side), to("o2m", "o2", middle), to("o1r", "o1", pair), send_b("W")],
        [normed_part(0, 2), grad_a("G")],
    )
    tick(
        [plus("d3", "d3k", "d3x")],
        [to("d2x", "d2a", side), to("d3i", "d3", inward), send_a("G")],
        [grad_b("G"), grad_a("J"), plus("o", "o0k", "o0x", "o2m", "o1r")],
    )
    tick(
        [plus("d2", "d2k", "d2x"), plus("d3", "d3", "d3i")],
        [
            to("d1x", "d1a", side),
            to("d2i", "d2", inward),
            to("d3m", "d3", middle),
            send_b("G"),
            send_a("J"),
        ],
        [grad_c("W"), grad_b("J")],
    )
    tick(
        [plus("d2", "d2", "d2i")],
        [to("d0x", "d0a", side), to("d2m", "d2", middle), send_b("J")],
        [grad_c("G"), grad_c("J"), deal],
    )
    tick(
        [plus("d1", "d1k", "d1x", "d3m")],
        [to("d1r", "d1", pair), *map(swap, (4, 5, 6, 7))],
    )
    tick([plus("d", "d0k", "d0x", "d2m", "d1r")], map(swap, (1, 2, 3)), [norm_back])
    tick((), (), [undeal])
    grads = [st[f"grad{weight}"] for weight in range(5)]
    return layer.finish_output(unorder(st["o"])), st["input_grad"], st["norm_sums"], grads


def on_device(
    n_ctx,
    n_dp,
    inputs,
    norm_gain,
    norm_bias,
    joined_weight,
    gate_weight,
    up_weight,
    out_weight,
    down_weight,
    cotangent,
    lengths,
):
    grid = (n_ctx, n_dp) == (8, 4)
    if grid:
        ctx = lax.axis_index("ctx")
        z, x = ctx // 2, ctx % 2
        high = z >= 2
        order = [z, z ^ 1, jnp.where(high, 1, 2), jnp.where(high, 0, 3)]
        natural = [2 * o + (x ^ r) for o in order for r in range(2)]
        slots = jnp.zeros((n_ctx,), jnp.int32)
        for slot, part in enumerate(natural):
            slots = jnp.where(jnp.arange(n_ctx) == part, slot, slots)
    else:
        slots = jnp.arange(n_ctx, dtype=jnp.int32)
    units = gate_weight.shape[1] // n_ctx
    layer = Layer(n_ctx, slots, inputs, norm_gain, cotangent, lengths, units)
    weights = (joined_weight, out_weight, gate_weight, up_weight, down_weight)
    scales = jnp.concatenate([norm_gain, norm_bias])
    run = on_grid if grid else on_any_mesh
    output, input_grad, norm_sums, grads = run(layer, weights, scales)
    joined_grad, out_grad, gate_grad, up_grad, down_grad = grads
    return (
        output.reshape(inputs.shape),
        input_grad.reshape(inputs.shape),
        norm_sums[0, : layer.own],
        norm_sums[0, layer.own :],
        joined_grad,
        gate_grad,
        up_grad,
        out_grad,
        down_grad,
    )


def solution(mesh):
    rows = P(("dp", "ctx"), None)
    vector = P(("dp", "ctx"))
    tokens = P("dp", "ctx", None)
    return jax.shard_map(
        functools.partial(on_device, mesh.shape["ctx"], mesh.shape["dp"]),
        mesh=mesh,
        in_specs=(tokens, vector, vector, rows, rows, rows, rows, rows, tokens, P("dp")),
        out_specs=(tokens, tokens, vector, vector, rows, rows, rows, rows, rows),
        check_vma=False,
    )
```

```python
import functools

import jax
import jax.numpy as jnp
from jax import lax
from jax.experimental import pallas as pl
from jax.experimental.pallas import tpu as pltpu
from jax.sharding import PartitionSpec as P

HD = 64
ROT = 16
EPSILON = 1e-05
THETA = 10000.0
NEGATIVE = -1e30
BF = jnp.bfloat16
F32 = jnp.float32
LAST = (((1,), (1,)), ((), ()))
FIRST = (((0,), (0,)), ((), ()))


def dot(left, right):
    return jnp.dot(left, right, preferred_element_type=F32)


def dot_last(left, right):
    return lax.dot_general(left, right, LAST, preferred_element_type=F32)


def dot_first(left, right):
    return lax.dot_general(left, right, FIRST, preferred_element_type=F32)


def rotary_tables(length, width):
    half = ROT // 2
    lane = jnp.arange(width, dtype=jnp.int32) % HD
    frequency = THETA ** (-(2.0 * (lane % half).astype(F32)) / ROT)
    angles = jnp.arange(length, dtype=jnp.int32).astype(F32)[:, None] * frequency[None, :]
    cosine = jnp.where(lane[None, :] < ROT, jnp.cos(angles), 1.0)
    sine = jnp.sin(angles)
    sine = jnp.where(lane[None, :] < half, -sine, jnp.where(lane[None, :] < ROT, sine, 0.0))
    return cosine, sine


def partner(x):
    half = ROT // 2
    lane = lax.broadcasted_iota(jnp.int32, x.shape, 1) % HD
    down = jnp.concatenate([x[:, half:], x[:, :half]], axis=1)
    up = jnp.concatenate([x[:, -half:], x[:, :-half]], axis=1)
    return jnp.where(lane < half, down, up)


def attend_forward(
    length_ref, slot_ref, joined_ref, cos_ref, sin_ref, wide_ref, rot_ref, attn_ref, lse_ref, total
):
    parts, _, rows, triple = joined_ref.shape
    width = triple // 3
    length = parts * rows
    seq = pl.program_id(0)
    head = pl.program_id(1)
    alive_count = length_ref[seq]
    block = min(256, length)
    lane = lax.broadcasted_iota(jnp.int32, (1, width), 1)
    mine = (lane // HD) == head

    @pl.when(head == 0)
    def _():
        for part in range(parts):
            slot = slot_ref[part]
            here = slice(part * rows, (part + 1) * rows)

            def rotated(start):
                x = joined_ref[slot, 0, :, start : start + width]
                return (x * cos_ref[here, :] + partner(x) * sin_ref[here, :]).astype(BF)

            rot_ref[part, 0, :, :width] = rotated(0) * 0.125
            rot_ref[part, 0, :, width : 2 * width] = rotated(width)
            rot_ref[part, 0, :, 2 * width :] = joined_ref[slot, 0, :, 2 * width :].astype(BF)
        total[...] = jnp.zeros_like(total)
        lse_ref[...] = jnp.zeros_like(lse_ref)

    per = block // rows if block >= rows else 1
    block = per * rows
    for step in range(length // block):
        begin, end = step * per, (step + 1) * per
        stop = end * rows

        @pl.when(begin * rows < alive_count)
        def _(begin=begin, end=end, stop=stop):
            q = rot_ref[begin:end, 0, :, :width].reshape(block, width)
            q = jnp.where(mine, q, jnp.zeros_like(q))
            k = rot_ref[:end, 0, :, width : 2 * width].reshape(stop, width)
            v = rot_ref[:end, 0, :, 2 * width :].reshape(stop, width)
            scores = dot_last(q, k)
            q_pos = begin * rows + lax.broadcasted_iota(jnp.int32, (block, 1), 0)
            k_pos = lax.broadcasted_iota(jnp.int32, (block, stop), 1)
            scores = jnp.where(k_pos <= q_pos, scores, NEGATIVE)
            top = jnp.max(scores, axis=1, keepdims=True)
            expo = jnp.exp(scores - top)
            weight = jnp.sum(expo, axis=1, keepdims=True)
            out = dot(expo.astype(BF), v) / weight
            alive = q_pos < alive_count
            here = slice(begin * rows, stop)
            total[here, :] += jnp.where(mine & alive, out, 0.0)
            lse = jnp.where(alive, top + jnp.log(weight), 0.0)
            spot = lax.broadcasted_iota(jnp.int32, (1, lse_ref.shape[3]), 1) == head
            held = lse_ref[begin:end, 0].reshape(block, lse_ref.shape[3])
            lse_ref[begin:end, 0] = jnp.where(spot, lse, held).reshape(per, rows, -1)

    @pl.when(head == pl.num_programs(1) - 1)
    def _():
        for part in range(parts):
            attn_ref[slot_ref[part], 0] = total[part * rows : (part + 1) * rows, :].astype(BF)


def attend_backward(
    length_ref, slot_ref, rot_ref, attn_ref, grad_ref, lse_ref, cos_ref, sin_ref, out_ref, dq, dk, dv
):
    parts, _, rows, triple = rot_ref.shape
    width = triple // 3
    length = parts * rows
    seq = pl.program_id(0)
    head = pl.program_id(1)
    alive_count = length_ref[seq]
    per = max(1, min(256, length) // rows)
    block = per * rows
    lane = lax.broadcasted_iota(jnp.int32, (1, width), 1)
    mine = (lane // HD) == head

    @pl.when(head == 0)
    def _():
        dq[...] = jnp.zeros_like(dq)
        dk[...] = jnp.zeros_like(dk)
        dv[...] = jnp.zeros_like(dv)

    for step in range(length // block):
        begin, end = step * per, (step + 1) * per
        stop = end * rows

        @pl.when(begin * rows < alive_count)
        def _(begin=begin, end=end, stop=stop):
            q_pos = begin * rows + lax.broadcasted_iota(jnp.int32, (block, 1), 0)
            alive = q_pos < alive_count
            q = rot_ref[begin:end, 0, :, :width].reshape(block, width)
            q = jnp.where(mine, q, jnp.zeros_like(q))
            k = rot_ref[:end, 0, :, width : 2 * width].reshape(stop, width)
            v = rot_ref[:end, 0, :, 2 * width :].reshape(stop, width)
            slots = [slot_ref[part] for part in range(begin, end)]
            g = jnp.concatenate([grad_ref[slot, 0] for slot in slots], axis=0)
            g = jnp.where(mine & alive, g, jnp.zeros_like(g))
            o = jnp.concatenate([attn_ref[slot, 0] for slot in slots], axis=0)
            delta = jnp.sum(g.astype(F32) * o.astype(F32), axis=1, keepdims=True)
            held = lse_ref[begin:end, 0].reshape(block, lse_ref.shape[3])
            spot = lax.broadcasted_iota(jnp.int32, (1, lse_ref.shape[3]), 1) == head
            lse = jnp.sum(jnp.where(spot, held, 0.0), axis=1, keepdims=True)
            scores = dot_last(q, k)
            k_pos = lax.broadcasted_iota(jnp.int32, (block, stop), 1)
            probs = jnp.where((k_pos <= q_pos) & alive, jnp.exp(scores - lse), 0.0)
            d_probs = dot_last(g, v)
            d_scores = (probs * (d_probs - delta)).astype(BF)
            here = slice(begin * rows, stop)
            dq[here, :] += jnp.where(mine, dot(d_scores, k), 0.0)
            dk[:stop, :] += dot_first(d_scores, q)
            dv[:stop, :] += dot_first(probs.astype(BF), g)

    @pl.when(head == pl.num_programs(1) - 1)
    def _():
        for part in range(parts):
            slot = slot_ref[part]
            here = slice(part * rows, (part + 1) * rows)

            def unrotated(x):
                return (x * cos_ref[here, :] - partner(x) * sin_ref[here, :]).astype(BF)

            out_ref[slot, 0, :, :width] = unrotated(dq[here, :] * 0.125)
            out_ref[slot, 0, :, width : 2 * width] = unrotated(dk[here, :])
            out_ref[slot, 0, :, 2 * width :] = dv[here, :].astype(BF)


def attention_calls(parts, groups, rows, width, heads, lanes):
    length = parts * rows
    smem = pl.BlockSpec(memory_space=pltpu.SMEM)

    def spec(last):
        return pl.BlockSpec((parts, 1, rows, last), lambda s, h: (0, s, 0, 0))

    table = pl.BlockSpec((length, width), lambda s, h: (0, 0))

    def shape(last, dtype):
        return jax.ShapeDtypeStruct((parts, groups, rows, last), dtype)

    pairs = groups * heads * length * length // 2
    params = pltpu.CompilerParams(vmem_limit_bytes=48 * 1024 * 1024)
    forward = pl.pallas_call(
        attend_forward,
        grid=(groups, heads),
        in_specs=[smem, smem, spec(3 * width), table, table, pl.BlockSpec(memory_space=pl.ANY)],
        out_specs=[spec(3 * width), spec(width), spec(heads)],
        out_shape=[shape(3 * width, BF), shape(lanes, BF), shape(heads, F32)],
        scratch_shapes=[pltpu.VMEM((length, width), F32)],
        input_output_aliases={5: 1},
        compiler_params=params,
        cost_estimate=pl.CostEstimate(
            flops=pairs * 1024, bytes_accessed=16 * length * width, transcendentals=pairs
        ),
        name="attend_forward",
    )
    backward = pl.pallas_call(
        attend_backward,
        grid=(groups, heads),
        in_specs=[smem, smem, spec(3 * width), spec(width), spec(width), spec(heads), table, table],
        out_specs=spec(3 * width),
        out_shape=shape(3 * width, BF),
        scratch_shapes=[pltpu.VMEM((length, width), F32)] * 3,
        compiler_params=params,
        cost_estimate=pl.CostEstimate(
            flops=pairs * 2560, bytes_accessed=16 * length * width, transcendentals=pairs
        ),
        name="attend_backward",
    )
    return forward, backward


class Plan:
    def __init__(self, n, own, width, units):
        self.n, self.own, self.width, self.units = n, own, width, units
        self.body = units // 128 * 128
        self.tail = units - self.body
        self.joined = 3 * width
        self.first = self.joined + 2 * units
        self.used = width + units
        self.second = self.used + own
        spans = [(0, r * n * width, width, width) for r in range(3)]
        for start, span in ((0, self.body), (self.body, self.tail)):
            spans += [(w, start, units, span) for w in (2, 3)]
        self.spans = [*spans, (1, 0, width, width), (4, 0, units, units)]

    def segments(self):
        lane = 0
        for weight, start, stride, span in self.spans:
            yield weight, start, stride, lane, span
            lane += span


def pack_kernel(plan, *refs):
    scale_ref, sources, out_ref = refs[0], refs[1:-1], refs[-1]
    for dest in range(plan.n):
        for weight, start, stride, lane, span in plan.segments():
            begin = start + dest * stride
            out_ref[dest, :, lane : lane + span] = sources[weight][:, begin : begin + span]
        out_ref[dest, :, plan.first + plan.used :] = scale_ref[...]


def unpack_kernel(plan, outs_of, in_ref, *outs):
    own = plan.own
    for out, (source, sources, lane, lanes) in zip(outs, outs_of):
        for index in range(sources):
            block = in_ref[source + index, :, lane : lane + lanes]
            out[index * own : (index + 1) * own, :] = block
    for source in range(plan.n):
        outs[-1][source] = in_ref[source, :, plan.first + plan.used :]


def pack_rows_kernel(own, *refs):
    sources, out = refs[:-1], refs[-1]
    for dest in range(out.shape[0]):
        lane = 0
        for source in sources:
            lanes = source.shape[1]
            out[dest, :, lane : lane + lanes] = source[dest * own : (dest + 1) * own, :]
            lane += lanes


def unpack_rows_kernel(n, layout, held, *outs):
    for source in range(n):
        for out, start, stride, lane, span in layout:
            begin = start + source * stride
            block = held[source, :, lane : lane + span].astype(F32)
            outs[out][:, begin : begin + span] = block


def in_vmem(kernel, name, out_shape):
    def call(*operands):
        place = pl.BlockSpec(memory_space=pltpu.VMEM)
        moved = sum(o.size * o.dtype.itemsize for o in operands)
        return pl.pallas_call(
            kernel,
            in_specs=[place] * len(operands),
            out_specs=jax.tree.map(lambda _: place, out_shape),
            out_shape=out_shape,
            compiler_params=pltpu.CompilerParams(vmem_limit_bytes=48 * 1024 * 1024),
            cost_estimate=pl.CostEstimate(flops=0, bytes_accessed=3 * moved, transcendentals=0),
            name=name,
        )(*operands)

    return call


def pack_columns(plan, weights, scales):
    shape = jax.ShapeDtypeStruct((plan.n, plan.own, plan.first + plan.second), BF)
    scales = jnp.pad(scales.reshape(2, plan.own), ((0, plan.own - 2), (0, 0)))
    return in_vmem(functools.partial(pack_kernel, plan), "pack_columns", shape)(scales, *weights)


def unpack_columns(plan, packed):
    n, own = plan.n, plan.own
    outs_of = [(half * n // 2, n // 2, 0, plan.first) for half in range(2)]
    outs_of += [(0, n, 0, plan.first), (0, n, plan.first, plan.second)]
    shapes = [jax.ShapeDtypeStruct((c * own, lanes), BF) for _, c, _, lanes in outs_of]
    shapes.append(jax.ShapeDtypeStruct((n, own, own), BF))
    kernel = functools.partial(unpack_kernel, plan, outs_of)
    *parts, scales = in_vmem(kernel, "unpack_columns", shapes)(packed)
    return parts, scales[:, :2]


def pack_rows(own, n, gradients):
    lanes = sum(g.shape[1] for g in gradients)
    shape = jax.ShapeDtypeStruct((n, own, lanes), BF)
    return in_vmem(functools.partial(pack_rows_kernel, own), "pack_rows", shape)(*gradients)


def unpack_rows(plan, packed):
    widths = [3 * plan.width, plan.width, plan.units, plan.units, plan.units]
    shapes = [jax.ShapeDtypeStruct((plan.own, plan.n * w), F32) for w in widths]
    kernel = functools.partial(unpack_rows_kernel, plan.n, list(plan.segments()))
    return in_vmem(kernel, "unpack_rows", shapes)(packed)


def fetch_pieces(pieces, held, sems):
    copies, row = [], 0
    for i, piece in enumerate(pieces):
        there = held.at[pl.ds(row, piece.shape[0]), :]
        copies.append(pltpu.make_async_copy(piece, there, sems.at[i]))
        row += piece.shape[0]
    return copies


def stream_kernel(n, n_pieces, n_extra, finish, *refs):
    blocks, refs = refs[:n], refs[n:]
    pieces, refs = refs[:n_pieces], refs[n_pieces:]
    extra, outs, (held, rows_ref, rows_sem, weight_sem) = refs[:n_extra], refs[n_extra:-4], refs[-4:]
    size = blocks[0].shape[0]
    step = pl.program_id(0)
    steps = n // 2
    weight = fetch_pieces(pieces, held, weight_sem)

    def copy(block, buffer, half):
        there = rows_ref.at[buffer, pl.ds(half * size, size), :]
        return pltpu.make_async_copy(block, there, rows_sem.at[buffer, half])

    def fetch(index):
        for place in range(steps):

            @pl.when(index == place)
            def _(place=place):
                for half in range(2):
                    copy(blocks[2 * place + half], place % 2, half).start()

    @pl.when(step == 0)
    def _():
        fetch(0)
        for piece in weight:
            piece.start()

    @pl.when(step + 1 < steps)
    def _():
        fetch(step + 1)

    buffer = lax.rem(step, 2)
    for half in range(2):
        copy(blocks[half], buffer, half).wait()

    @pl.when(step == 0)
    def _():
        for piece in weight:
            piece.wait()

    finish(rows_ref[buffer], held, extra, outs)


def stream(name, blocks, pieces, extra, finish, outs):
    size, features = blocks[0].shape
    n = len(blocks)
    anywhere = pl.BlockSpec(memory_space=pl.ANY)

    def rows(width):
        return pl.BlockSpec((2 * size, width), lambda i: (i, 0))

    def beside(array):
        if array.shape[0] == n * size:
            return rows(array.shape[1])
        return pl.BlockSpec(array.shape, lambda i: (0, 0))

    outs = [(features, BF), *outs]
    width = pieces[0].shape[1]
    return pl.pallas_call(
        functools.partial(stream_kernel, n, len(pieces), len(extra), finish),
        grid=(n // 2,),
        in_specs=[anywhere] * (n + len(pieces)) + [beside(e) for e in extra],
        out_specs=[rows(w) for w, _ in outs],
        out_shape=[jax.ShapeDtypeStruct((n * size, w), dtype) for w, dtype in outs],
        scratch_shapes=[
            pltpu.VMEM((features, width), BF),
            pltpu.VMEM((2, 2 * size, features), BF),
            pltpu.SemaphoreType.DMA((2, 2)),
            pltpu.SemaphoreType.DMA((len(pieces),)),
        ],
        compiler_params=pltpu.CompilerParams(vmem_limit_bytes=52 * 1024 * 1024),
        cost_estimate=pl.CostEstimate(
            flops=2 * n * size * features * width,
            bytes_accessed=2 * (n * size + width) * features * 2,
            transcendentals=0,
        ),
        name=name,
    )(*blocks, *pieces, *extra)


def swiglu(plan, both):
    body, tail = plan.body, plan.tail
    hidden, factors = [], []
    for start, span in ((0, body), (2 * body, tail)):
        gate, up = both[:, start : start + span], both[:, start + span : start + 2 * span]
        sigmoid = jax.nn.sigmoid(gate)
        silu = gate * sigmoid
        hidden.append((silu * up).astype(BF))
        factors += [up * sigmoid * (1.0 + gate * (1.0 - sigmoid)), silu]
    return hidden, factors


def project_finish(plan, rows, held, extra, outs):
    (scales,), (normed, joined, factor_ref, wide) = extra, outs
    rows = (rows.astype(F32) * scales[0:1, :] + scales[1:2, :]).astype(BF)
    normed[...] = rows
    joined[...] = dot(rows, held[:, : plan.joined])
    hidden, factors = swiglu(plan, dot(rows, held[:, plan.joined :]))
    lane = 0
    for factor in factors:
        factor_ref[:, lane : lane + factor.shape[1]] = factor.astype(factor_ref.dtype)
        lane += factor.shape[1]
    wide[:, : plan.width] = jnp.zeros((rows.shape[0], plan.width), BF)
    wide[:, plan.width : plan.width + plan.body] = hidden[0]
    pad = jnp.zeros((rows.shape[0], plan.second - plan.used), BF)
    wide[:, plan.width + plan.body :] = jnp.concatenate([hidden[1], pad], axis=1)


def return_finish(plan, rows, held, extra, outs):
    (factor_ref,), (cot, d_attn, d_both) = extra, outs
    cot[...] = rows
    total = dot(rows, held[...])
    d_attn[...] = total[:, : plan.width].astype(BF)
    begin, body, tail = plan.width, plan.body, plan.tail
    for lane, start, span in (
        (0, begin, body),
        (body, begin, body),
        (2 * body, begin + body, tail),
        (2 * body + tail, begin + body, tail),
    ):
        here = slice(lane, lane + span)
        d_both[:, here] = (total[:, start : start + span] * factor_ref[:, here]).astype(BF)


def spread_kernel(count, n_pieces, places, *refs):
    lefts, refs = refs[: count * places], refs[count * places :]
    pieces, outs, (held, sems) = refs[:n_pieces], refs[n_pieces:-2], refs[-2:]
    weight = fetch_pieces(pieces, held, sems)
    for piece in weight:
        piece.start()
    size = outs[0].shape[0]
    rows = held.shape[0] // 4
    begins = [sum(p.shape[0] for p in pieces[:i]) for i in range(n_pieces)]
    for part in range(4):
        here = slice(part * rows, (part + 1) * rows)
        for begin, piece in zip(begins, weight):
            if begin // rows == part:
                piece.wait()
        for place in range(places):
            total, lane = 0.0, 0
            for left in lefts[place * count : (place + 1) * count]:
                lanes = left.shape[1]
                total += dot_last(left[...], held[here, lane : lane + lanes])
                lane += lanes
            outs[2 * place][:, here] = total[:size].astype(BF)
            outs[2 * place + 1][:, here] = total[size:].astype(BF)


def spread(name, lefts, pieces, places, size):
    anywhere = pl.BlockSpec(memory_space=pl.ANY)
    features = sum(piece.shape[0] for piece in pieces)
    width = pieces[0].shape[1]
    tokens = 2 * size * len(places)

    def rows(left, place):
        return pl.BlockSpec((2 * size, left.shape[1]), lambda i: (place, 0))

    blocks = 2 * len(places)
    return pl.pallas_call(
        functools.partial(spread_kernel, len(lefts), len(pieces), len(places)),
        grid=(1,),
        in_specs=[rows(left, place) for place in places for left in lefts]
        + [anywhere] * len(pieces),
        out_specs=[pl.BlockSpec((size, features), lambda i: (0, 0))] * blocks,
        out_shape=[jax.ShapeDtypeStruct((size, features), BF)] * blocks,
        scratch_shapes=[
            pltpu.VMEM((features, width), BF),
            pltpu.SemaphoreType.DMA((len(pieces),)),
        ],
        compiler_params=pltpu.CompilerParams(vmem_limit_bytes=52 * 1024 * 1024),
        cost_estimate=pl.CostEstimate(
            flops=2 * tokens * features * width,
            bytes_accessed=2 * (tokens + features) * width + 2 * tokens * features,
            transcendentals=0,
        ),
        name=name,
    )(*[left for _ in places for left in lefts], *pieces)


class Layer:
    def __init__(self, n_ctx, slots, inputs, norm_gain, cotangent, lengths, units):
        self.groups, self.rows, self.features = inputs.shape
        self.tokens = self.groups * self.rows
        self.n_ctx, self.slots, self.lengths = n_ctx, slots, lengths
        self.own = norm_gain.shape[0]
        self.width = self.features // n_ctx
        self.plan = Plan(n_ctx, self.own, self.width, units)
        self.flat = inputs.reshape(self.tokens, self.features).astype(F32)
        self.cot = cotangent.reshape(self.tokens, self.features)
        self.tables = rotary_tables(n_ctx * self.rows, self.width)
        self.blocks = (n_ctx, self.groups, self.rows)

    def calls(self, lanes):
        heads = self.width // HD
        return attention_calls(self.n_ctx, self.groups, self.rows, self.width, heads, lanes)

    def standardize(self):
        center = self.flat - jnp.mean(self.flat, axis=-1, keepdims=True)
        variance = jnp.mean(center * center, axis=-1, keepdims=True)
        inverse = lax.rsqrt(variance + EPSILON)
        return center * inverse, inverse

    def norm(self, standard, scales):
        gain, bias = self.scales(scales)
        return (standard * gain + bias).astype(BF), gain

    def scales(self, scales):
        return [scales[:, i].astype(F32).reshape(1, self.features) for i in range(2)]

    def attend(self, joined, wide, tables):
        lanes = wide.shape[1]
        shape = (*self.blocks, lanes)
        joined = joined.reshape(*self.blocks, 3 * self.width)
        rotated, wide, lse = self.calls(lanes)[0](
            self.lengths, self.slots, joined, *tables, wide.reshape(shape)
        )
        return rotated, wide.reshape(-1, lanes), lse

    def attend_back(self, rotated, wide, d_attn, lse, tables):
        lanes = wide.shape[1]
        return self.calls(lanes)[1](
            self.lengths,
            self.slots,
            rotated,
            wide.reshape(*self.blocks, lanes),
            d_attn.reshape(*self.blocks, self.width),
            lse,
            *tables,
        ).reshape(-1, 3 * self.width)

    def finish_output(self, branches):
        return (self.flat + branches.astype(F32)).astype(BF)

    def norm_back(self, d_normed, standard, inverse, gain):
        d_normed = d_normed.astype(F32)
        grad = d_normed * gain
        centered = (
            grad
            - jnp.mean(grad, axis=-1, keepdims=True)
            - standard * jnp.mean(grad * standard, axis=-1, keepdims=True)
        )
        sums = [jnp.sum(d_normed * standard, axis=0), jnp.sum(d_normed, axis=0)]
        sums = jnp.concatenate([v.reshape(-1, self.own) for v in sums], axis=1)
        return (self.cot.astype(F32) + inverse * centered).astype(BF), sums


def on_any_mesh(layer, weights, scales):
    plan = layer.plan
    n, own, width = plan.n, plan.own, plan.width

    def swap(pieces):
        return lax.all_to_all(pieces, "ctx", split_axis=0, concat_axis=0, tiled=True)

    def gather(v, axis):
        return lax.all_gather(v, axis, axis=0, tiled=True)

    def scatter(v, axis):
        return lax.psum_scatter(v, axis, scatter_dimension=0, tiled=True)

    parts, scales = unpack_columns(plan, swap(pack_columns(plan, weights, scales)))
    w_first, w_second = gather(parts[2], "dp"), gather(parts[3], "dp")[:, : plan.used]
    standard, inverse = layer.standardize()
    normed, gain = layer.norm(standard, gather(scales, "dp"))
    normed, cot = gather(normed, "ctx"), gather(layer.cot, "ctx")
    total = dot(normed, w_first)
    hidden, factors = swiglu(plan, total[:, plan.joined :])
    empty = jnp.zeros((normed.shape[0], width), BF)
    rotated, attn, lse = layer.attend(total[:, : plan.joined], empty, layer.tables)
    wide = jnp.concatenate([attn, *hidden], axis=1)
    branches = scatter(dot_last(wide, w_second).astype(BF), "ctx")
    total = dot(cot, w_second)
    body = total[:, width : width + plan.body]
    tail = total[:, width + plan.body :]
    d_both = jnp.concatenate([body, body, tail, tail], axis=1) * jnp.concatenate(factors, axis=1)
    d_attn = total[:, :width].astype(BF)
    d_joined = layer.attend_back(rotated, attn, d_attn, lse, layer.tables)
    d_first = jnp.concatenate([d_joined, d_both.astype(BF)], axis=1)
    d_normed = scatter(dot_last(d_first, w_first).astype(BF), "ctx")
    sums = [scatter(dot_first(*v).astype(BF), "dp") for v in ((normed, d_first), (cot, wide))]
    grads = unpack_rows(plan, swap(pack_rows(own, n, sums)))
    input_grad, norm_sums = layer.norm_back(d_normed, standard, inverse, gain)
    return layer.finish_output(branches), input_grad, scatter(norm_sums, ("dp", "ctx")), grads


def swaps(bit, n):
    return [(i, i ^ bit) for i in range(n)]


class State:
    def __init__(self, **arrays):
        self.held = arrays

    def __getitem__(self, name):
        return self.held[name]

    def drop(self, *names):
        for name in names:
            del self.held[name]

    def tick(self, before=(), sends=(), work=()):
        for action in before:
            self.held.update(action(self.held))
        view = dict(self.held)
        for name, source, axis, pairs in sends:
            view[name] = lax.ppermute(self.held[source], axis, pairs)
        for action in work:
            view.update(action(view))
        self.held = lax.optimization_barrier(view)


def on_grid(layer, weights, scales):
    plan = layer.plan
    n, own, features = plan.n, plan.own, layer.features
    ctx, dp = lax.axis_index("ctx"), lax.axis_index("dp")
    z = ctx // 2
    inner = (z == 1) | (z == 2)
    quarter = features // 4
    side, pair = ("ctx", swaps(1, n)), ("ctx", swaps(2, n))
    middle = ("ctx", [(2, 4), (3, 5), (4, 2), (5, 3)])
    outward = ("ctx", [(2, 0), (3, 1), (4, 6), (5, 7)])
    inward = ("ctx", [(b, a) for a, b in outward[1]])
    core, across = ("dp", swaps(1, 4)), ("dp", swaps(2, 4))

    def blocks_of(v, first, steps):
        blocks = [
            lax.dynamic_slice_in_dim(v, (first ^ step) * quarter, quarter, 1) for step in steps
        ]
        return jnp.concatenate(blocks, axis=1)

    def reorder(v):
        return blocks_of(v, dp, (0, 2, 1, 3))

    def unorder(v):
        return blocks_of(v, (dp % 2) * 2 + dp // 2, (0, 2, 1, 3))

    def weights_in(s):
        packed = pack_columns(plan, weights, scales)
        packed = lax.all_to_all(packed, "ctx", split_axis=0, concat_axis=0, tiled=True)
        parts, held = unpack_columns(plan, packed)
        return {"scales": held, **dict(zip(("a0", "b0", "ab0", "w0"), parts))}

    def all_scales(s):
        held = s["scales"]
        for bit in (1, 2):
            mine = dp // bit % 2
            got = lax.ppermute(held, "dp", swaps(bit, 4))
            first, second = jnp.where(mine == 0, held, got), jnp.where(mine == 0, got, held)
            held = jnp.concatenate([first, second], axis=0)
        gain, bias = layer.scales(held)
        return {"gain": gain, "both": reorder(jnp.concatenate([gain, bias], axis=0))}

    def select(name):
        return lambda s: {name: jnp.where(inner, s[name + "i"], s[name + "o"])}

    def plus(name, *parts):
        return lambda s: {name: sum(s[part].astype(F32) for part in parts).astype(BF)}

    def pieces(s, name):
        names = "a0 b0 a2 b2 ab1 a3 b3" if name == "ab" else "w0 w2 w1 w3"
        return [s[key] for key in names.split()]

    def slots(s, letter):
        return [s[letter + i] for i in ("0", "0x", "1", "1x", "2", "2x", "3", "3x")]

    def project(s):
        outs = [(plan.joined, F32), (2 * plan.units, BF), (plan.second, BF)]
        finish = functools.partial(project_finish, plan)
        held = pieces(s, "ab")
        made = stream("project", slots(s, "n"), held, [s["both"]], finish, outs)
        return dict(zip(("n", "joined", "factors", "wide"), made))

    def tables(s):
        return {"tables": layer.tables}

    def attend(s):
        made = layer.attend(s["joined"], s["wide"], s["tables"])
        return dict(zip(("rotated", "wide", "lse"), made))

    def bring_back(s):
        outs = [(plan.width, BF), (2 * plan.units, BF)]
        finish = functools.partial(return_finish, plan)
        made = stream(
            "bring_back", slots(s, "c"), pieces(s, "w"), [s["factors"]], finish, outs
        )
        return dict(zip(("c", "d_attn", "d_both"), made))

    def attend_back(s):
        d_joined = layer.attend_back(
            s["rotated"], s["wide"], s["d_attn"], s["lse"], s["tables"]
        )
        return {"d_joined": d_joined}

    def scattered(name, letter, lefts, weight, places):
        def work(s):
            size = s["c0"].shape[0]
            made = spread(name, [s[v] for v in lefts], pieces(s, weight), places, size)
            keys = [f"{letter}{place}{kind}" for place in places for kind in "ka"]
            return dict(zip(keys, made))

        return work

    def output_part(*places):
        return scattered("output_part", "o", ["wide"], "w", places)

    def normed_part(*places):
        return scattered("normed_part", "d", ["d_joined", "d_both"], "ab", places)

    factors = {"J": ("n", "d_joined"), "G": ("n", "d_both"), "W": ("c", "wide")}

    def product(s, name, begin, end):
        left, right = factors[name]
        return dot_first(s[left][:, begin * quarter : end * quarter], s[right])

    def grad_a(name):
        return lambda s: {name + "A": product(s, name, 2, 4).astype(BF)}

    def grad_b(name):
        def work(s):
            total = product(s, name, 1, 2) + s[name + "Ar"][quarter:].astype(F32)
            return {name + "B": total.astype(BF)}

        return work

    def grad_c(name):
        def work(s):
            total = product(s, name, 0, 1) + s[name + "Ar"][:quarter].astype(F32)
            return {name + "C": (total + s[name + "Br"].astype(F32)).astype(BF)}

        return work

    def to(name, source, way):
        return (name, source, *way)

    def send_a(name):
        return to(name + "Ar", name + "A", core)

    def send_b(name):
        return to(name + "Br", name + "B", across)

    def swap_rows(s):
        held = pack_rows(own, n, [s[name + "C"] for name in "JGW"])
        held = lax.all_to_all(held, "ctx", split_axis=0, concat_axis=0, tiled=True)
        return {f"grad{weight}": grad for weight, grad in enumerate(unpack_rows(plan, held))}

    def norm_back(s):
        input_grad, sums = layer.norm_back(unorder(s["d"]), standard, inverse, s["gain"])
        for axis, bit, size in [("dp", b, 4) for b in (2, 1)] + [("ctx", b, n) for b in (4, 2, 1)]:
            mine = lax.axis_index(axis) // bit % 2
            halves = sums.reshape(2, -1, sums.shape[1])
            first, second = halves[0], halves[1]
            give = jnp.where(mine == 0, second, first)
            keep = jnp.where(mine == 0, first, second)
            sums = keep + lax.ppermute(give, axis, swaps(bit, size))
        return {"input_grad": input_grad, "norm_sums": sums}

    def y(name):
        return to(name + "2", name + "0", across)

    def near(name):
        return to(name + "1", name + "0", core)

    def far(name):
        return to(name + "3", name + "2", core)

    standard, inverse = layer.standardize()
    st = State(c0=reorder(layer.cot), n0=reorder(standard.astype(BF)))
    tick = st.tick
    tick(
        (),
        [
            to("n0x", "n0", side),
            to("n1", "n0", pair),
            to("n2i", "n0", middle),
            to("c0x", "c0", side),
            to("c1", "c0", pair),
        ],
        [weights_in],
    )
    tick(
        (),
        [to("n1x", "n1", side), to("n3i", "n1", middle), to("n2o", "n2i", outward), y("a")],
        [all_scales, tables],
    )
    tick(
        [select("n2")],
        [
            to("n2x", "n2", side),
            to("n3o", "n3i", outward),
            to("c2i", "c0", middle),
            y("b"),
            far("a"),
        ],
    )
    tick(
        [select("n3")],
        [
            to("n3x", "n3", side),
            to("c2o", "c2i", outward),
            to("c3i", "c1", middle),
            far("b"),
            near("ab"),
        ],
    )
    tick(
        [select("c2")],
        [to("c2x", "c2", side), to("c3o", "c3i", outward), y("w"), near("w")],
        [project],
    )
    tick(
        [select("c3")],
        [to("c3x", "c3", side), to("c1x", "c0x", pair), far("w")],
        [attend, output_part(1, 3)],
    )
    tick(
        (),
        [to("o3x", "o3a", side), to("o1p", "o1a", pair)],
        [output_part(0, 2), bring_back, grad_a("G")],
    )
    tick(
        [plus("o3", "o3k", "o3x")],
        [to("o2x", "o2a", side), to("o3i", "o3", inward), send_a("G")],
        [attend_back],
    )
    tick(
        [plus("o2", "o2k", "o2x"), plus("o3", "o3", "o3i"), plus("o0a", "o0a", "o1p")],
        [to("o0x", "o0a", side), to("o2i", "o2", inward), to("o3m", "o3", middle)],
        [normed_part(1, 3), grad_b("G")],
    )
    tick(
        [plus("o2", "o2", "o2i"), plus("o1", "o1k", "o3m")],
        [to("d3x", "d3a", side), to("o2m", "o2", middle), to("o1r", "o1", pair), send_b("G")],
        [normed_part(0, 2), grad_a("W")],
    )
    tick(
        [plus("d3", "d3k", "d3x")],
        [to("d2x", "d2a", side), to("d3i", "d3", inward), send_a("W")],
        [grad_b("W"), grad_a("J"), plus("o", "o0k", "o0x", "o2m", "o1r")],
    )
    tick(
        [plus("d2", "d2k", "d2x"), plus("d3", "d3", "d3i")],
        [
            to("d1x", "d1a", side),
            to("d2i", "d2", inward),
            to("d3m", "d3", middle),
            send_b("W"),
            send_a("J"),
        ],
        [grad_c("G"), grad_b("J")],
    )
    tick(
        [plus("d2", "d2", "d2i"), plus("d1", "d1k", "d1x", "d3m")],
        [to("d0x", "d0a", side), to("d2m", "d2", middle), to("d1r", "d1", pair), send_b("J")],
        [grad_c("W"), grad_c("J")],
    )
    tick([plus("d", "d0k", "d0x", "d2m", "d1r")], (), [swap_rows, norm_back])
    grads = [st[f"grad{weight}"] for weight in range(5)]
    return layer.finish_output(unorder(st["o"])), st["input_grad"], st["norm_sums"], grads


def on_device(
    n_ctx,
    n_dp,
    inputs,
    norm_gain,
    norm_bias,
    joined_weight,
    gate_weight,
    up_weight,
    out_weight,
    down_weight,
    cotangent,
    lengths,
):
    grid = (n_ctx, n_dp) == (8, 4)
    if grid:
        ctx = lax.axis_index("ctx")
        z, x = ctx // 2, ctx % 2
        high = z >= 2
        order = [z, z ^ 1, jnp.where(high, 1, 2), jnp.where(high, 0, 3)]
        natural = [2 * o + (x ^ r) for o in order for r in range(2)]
        slots = jnp.zeros((n_ctx,), jnp.int32)
        for slot, part in enumerate(natural):
            slots = jnp.where(jnp.arange(n_ctx) == part, slot, slots)
    else:
        slots = jnp.arange(n_ctx, dtype=jnp.int32)
    units = gate_weight.shape[1] // n_ctx
    layer = Layer(n_ctx, slots, inputs, norm_gain, cotangent, lengths, units)
    weights = (joined_weight, out_weight, gate_weight, up_weight, down_weight)
    scales = jnp.concatenate([norm_gain, norm_bias])
    run = on_grid if grid else on_any_mesh
    output, input_grad, norm_sums, grads = run(layer, weights, scales)
    joined_grad, out_grad, gate_grad, up_grad, down_grad = grads
    return (
        output.reshape(inputs.shape),
        input_grad.reshape(inputs.shape),
        norm_sums[0, : layer.own],
        norm_sums[0, layer.own :],
        joined_grad,
        gate_grad,
        up_grad,
        out_grad,
        down_grad,
    )


def solution(mesh):
    rows = P(("dp", "ctx"), None)
    vector = P(("dp", "ctx"))
    tokens = P("dp", "ctx", None)
    return jax.shard_map(
        functools.partial(on_device, mesh.shape["ctx"], mesh.shape["dp"]),
        mesh=mesh,
        in_specs=(tokens, vector, vector, rows, rows, rows, rows, rows, tokens, P("dp")),
        out_specs=(tokens, tokens, vector, vector, rows, rows, rows, rows, rows),
        check_vma=False,
    )
```

```python
import functools

import jax
import jax.numpy as jnp
from jax import lax
from jax.experimental import pallas as pl
from jax.experimental.pallas import tpu as pltpu
from jax.sharding import PartitionSpec as P

HD = 64
ROT = 16
EPSILON = 1e-05
THETA = 10000.0
NEGATIVE = -1e30
BF = jnp.bfloat16
F32 = jnp.float32
LAST = (((1,), (1,)), ((), ()))
FIRST = (((0,), (0,)), ((), ()))


def dot(left, right):
    return jnp.dot(left, right, preferred_element_type=F32)


def dot_last(left, right):
    return lax.dot_general(left, right, LAST, preferred_element_type=F32)


def dot_first(left, right):
    return lax.dot_general(left, right, FIRST, preferred_element_type=F32)


def rotary_tables(length, width):
    half = ROT // 2
    lane = jnp.arange(width, dtype=jnp.int32) % HD
    frequency = THETA ** (-(2.0 * (lane % half).astype(F32)) / ROT)
    angles = jnp.arange(length, dtype=jnp.int32).astype(F32)[:, None] * frequency[None, :]
    cosine = jnp.where(lane[None, :] < ROT, jnp.cos(angles), 1.0)
    sine = jnp.sin(angles)
    sine = jnp.where(lane[None, :] < half, -sine, jnp.where(lane[None, :] < ROT, sine, 0.0))
    return cosine, sine


def partner(x):
    half = ROT // 2
    lane = lax.broadcasted_iota(jnp.int32, x.shape, 1) % HD
    down = jnp.concatenate([x[:, half:], x[:, :half]], axis=1)
    up = jnp.concatenate([x[:, -half:], x[:, :-half]], axis=1)
    return jnp.where(lane < half, down, up)


def attend_forward(
    length_ref, slot_ref, joined_ref, cos_ref, sin_ref, wide_ref, rot_ref, attn_ref, lse_ref, total
):
    parts, _, rows, triple = joined_ref.shape
    width = triple // 3
    length = parts * rows
    seq = pl.program_id(0)
    head = pl.program_id(1)
    alive_count = length_ref[seq]
    block = min(256, length)
    lane = lax.broadcasted_iota(jnp.int32, (1, width), 1)
    mine = (lane // HD) == head

    @pl.when(head == 0)
    def _():
        for part in range(parts):
            slot = slot_ref[part]
            here = slice(part * rows, (part + 1) * rows)

            def rotated(start):
                x = joined_ref[slot, 0, :, start : start + width]
                return (x * cos_ref[here, :] + partner(x) * sin_ref[here, :]).astype(BF)

            rot_ref[part, 0, :, :width] = rotated(0) * 0.125
            rot_ref[part, 0, :, width : 2 * width] = rotated(width)
            rot_ref[part, 0, :, 2 * width :] = joined_ref[slot, 0, :, 2 * width :].astype(BF)
        total[...] = jnp.zeros_like(total)
        lse_ref[...] = jnp.zeros_like(lse_ref)

    per = block // rows if block >= rows else 1
    block = per * rows
    for step in range(length // block):
        begin, end = step * per, (step + 1) * per
        stop = end * rows

        @pl.when(begin * rows < alive_count)
        def _(begin=begin, end=end, stop=stop):
            q = rot_ref[begin:end, 0, :, :width].reshape(block, width)
            q = jnp.where(mine, q, jnp.zeros_like(q))
            k = rot_ref[:end, 0, :, width : 2 * width].reshape(stop, width)
            v = rot_ref[:end, 0, :, 2 * width :].reshape(stop, width)
            scores = dot_last(q, k)
            q_pos = begin * rows + lax.broadcasted_iota(jnp.int32, (block, 1), 0)
            k_pos = lax.broadcasted_iota(jnp.int32, (block, stop), 1)
            scores = jnp.where(k_pos <= q_pos, scores, NEGATIVE)
            top = jnp.max(scores, axis=1, keepdims=True)
            expo = jnp.exp(scores - top)
            weight = jnp.sum(expo, axis=1, keepdims=True)
            out = dot(expo.astype(BF), v) / weight
            alive = q_pos < alive_count
            here = slice(begin * rows, stop)
            total[here, :] += jnp.where(mine & alive, out, 0.0)
            lse = jnp.where(alive, top + jnp.log(weight), 0.0)
            spot = lax.broadcasted_iota(jnp.int32, (1, lse_ref.shape[3]), 1) == head
            held = lse_ref[begin:end, 0].reshape(block, lse_ref.shape[3])
            lse_ref[begin:end, 0] = jnp.where(spot, lse, held).reshape(per, rows, -1)

    @pl.when(head == pl.num_programs(1) - 1)
    def _():
        for part in range(parts):
            attn_ref[slot_ref[part], 0] = total[part * rows : (part + 1) * rows, :].astype(BF)


def attend_backward(
    length_ref, slot_ref, rot_ref, attn_ref, grad_ref, lse_ref, cos_ref, sin_ref, out_ref, dq, dk, dv
):
    parts, _, rows, triple = rot_ref.shape
    width = triple // 3
    length = parts * rows
    seq = pl.program_id(0)
    head = pl.program_id(1)
    alive_count = length_ref[seq]
    per = max(1, min(256, length) // rows)
    block = per * rows
    lane = lax.broadcasted_iota(jnp.int32, (1, width), 1)
    mine = (lane // HD) == head

    @pl.when(head == 0)
    def _():
        dq[...] = jnp.zeros_like(dq)
        dk[...] = jnp.zeros_like(dk)
        dv[...] = jnp.zeros_like(dv)

    for step in range(length // block):
        begin, end = step * per, (step + 1) * per
        stop = end * rows

        @pl.when(begin * rows < alive_count)
        def _(begin=begin, end=end, stop=stop):
            q_pos = begin * rows + lax.broadcasted_iota(jnp.int32, (block, 1), 0)
            alive = q_pos < alive_count
            q = rot_ref[begin:end, 0, :, :width].reshape(block, width)
            q = jnp.where(mine, q, jnp.zeros_like(q))
            k = rot_ref[:end, 0, :, width : 2 * width].reshape(stop, width)
            v = rot_ref[:end, 0, :, 2 * width :].reshape(stop, width)
            slots = [slot_ref[part] for part in range(begin, end)]
            g = jnp.concatenate([grad_ref[slot, 0] for slot in slots], axis=0)
            g = jnp.where(mine & alive, g, jnp.zeros_like(g))
            o = jnp.concatenate([attn_ref[slot, 0] for slot in slots], axis=0)
            delta = jnp.sum(g.astype(F32) * o.astype(F32), axis=1, keepdims=True)
            held = lse_ref[begin:end, 0].reshape(block, lse_ref.shape[3])
            spot = lax.broadcasted_iota(jnp.int32, (1, lse_ref.shape[3]), 1) == head
            lse = jnp.sum(jnp.where(spot, held, 0.0), axis=1, keepdims=True)
            scores = dot_last(q, k)
            k_pos = lax.broadcasted_iota(jnp.int32, (block, stop), 1)
            probs = jnp.where((k_pos <= q_pos) & alive, jnp.exp(scores - lse), 0.0)
            d_probs = dot_last(g, v)
            d_scores = (probs * (d_probs - delta)).astype(BF)
            here = slice(begin * rows, stop)
            dq[here, :] += jnp.where(mine, dot(d_scores, k), 0.0)
            dk[:stop, :] += dot_first(d_scores, q)
            dv[:stop, :] += dot_first(probs.astype(BF), g)

    @pl.when(head == pl.num_programs(1) - 1)
    def _():
        for part in range(parts):
            slot = slot_ref[part]
            here = slice(part * rows, (part + 1) * rows)

            def unrotated(x):
                return (x * cos_ref[here, :] - partner(x) * sin_ref[here, :]).astype(BF)

            out_ref[slot, 0, :, :width] = unrotated(dq[here, :] * 0.125)
            out_ref[slot, 0, :, width : 2 * width] = unrotated(dk[here, :])
            out_ref[slot, 0, :, 2 * width :] = dv[here, :].astype(BF)


def attention_calls(parts, groups, rows, width, heads, lanes):
    length = parts * rows
    smem = pl.BlockSpec(memory_space=pltpu.SMEM)

    def spec(last):
        return pl.BlockSpec((parts, 1, rows, last), lambda s, h: (0, s, 0, 0))

    table = pl.BlockSpec((length, width), lambda s, h: (0, 0))

    def shape(last, dtype):
        return jax.ShapeDtypeStruct((parts, groups, rows, last), dtype)

    pairs = groups * heads * length * length // 2
    params = pltpu.CompilerParams(vmem_limit_bytes=48 * 1024 * 1024)
    forward = pl.pallas_call(
        attend_forward,
        grid=(groups, heads),
        in_specs=[smem, smem, spec(3 * width), table, table, pl.BlockSpec(memory_space=pl.ANY)],
        out_specs=[spec(3 * width), spec(width), spec(heads)],
        out_shape=[shape(3 * width, BF), shape(lanes, BF), shape(heads, F32)],
        scratch_shapes=[pltpu.VMEM((length, width), F32)],
        input_output_aliases={5: 1},
        compiler_params=params,
        cost_estimate=pl.CostEstimate(
            flops=pairs * 1024, bytes_accessed=16 * length * width, transcendentals=pairs
        ),
        name="attend_forward",
    )
    backward = pl.pallas_call(
        attend_backward,
        grid=(groups, heads),
        in_specs=[smem, smem, spec(3 * width), spec(width), spec(width), spec(heads), table, table],
        out_specs=spec(3 * width),
        out_shape=shape(3 * width, BF),
        scratch_shapes=[pltpu.VMEM((length, width), F32)] * 3,
        compiler_params=params,
        cost_estimate=pl.CostEstimate(
            flops=pairs * 2560, bytes_accessed=16 * length * width, transcendentals=pairs
        ),
        name="attend_backward",
    )
    return forward, backward


class Plan:
    def __init__(self, n, own, width, units):
        self.n, self.own, self.width, self.units = n, own, width, units
        self.body = units // 128 * 128
        self.tail = units - self.body
        self.joined = 3 * width
        self.first = self.joined + 2 * units
        self.used = width + units
        self.second = self.used + own
        spans = [(0, r * n * width, width, width) for r in range(3)]
        for start, span in ((0, self.body), (self.body, self.tail)):
            spans += [(w, start, units, span) for w in (2, 3)]
        self.spans = [*spans, (1, 0, width, width), (4, 0, units, units)]

    def segments(self):
        lane = 0
        for weight, start, stride, span in self.spans:
            yield weight, start, stride, lane, span
            lane += span


def pack_kernel(plan, chosen, *refs):
    scale_ref, sources, out_ref = refs[0], dict(zip(chosen, refs[1:-1])), refs[-1]
    lane = 0
    for weight, start, stride, _, span in plan.segments():
        if weight in chosen:
            for dest in range(plan.n):
                begin = start + dest * stride
                out_ref[dest, :, lane : lane + span] = sources[weight][:, begin : begin + span]
            lane += span
    if lane < out_ref.shape[2]:
        for dest in range(plan.n):
            out_ref[dest, :, lane:] = scale_ref[...]


def unpack_kernel(own, outs_of, in_ref, *outs):
    for out, (source, sources, lane, lanes) in zip(outs, outs_of):
        for index in range(sources):
            block = in_ref[source + index, :, lane : lane + lanes]
            out[index * own : (index + 1) * own, :] = block


def pack_rows_kernel(own, *refs):
    sources, out = refs[:-1], refs[-1]
    for dest in range(out.shape[0]):
        lane = 0
        for source in sources:
            lanes = source.shape[1]
            out[dest, :, lane : lane + lanes] = source[dest * own : (dest + 1) * own, :]
            lane += lanes


def unpack_rows_kernel(n, layout, held, *outs):
    for source in range(n):
        for out, start, stride, lane, span in layout:
            begin = start + source * stride
            block = held[source, :, lane : lane + span].astype(F32)
            outs[out][:, begin : begin + span] = block


def in_vmem(kernel, name, out_shape):
    def call(*operands):
        place = pl.BlockSpec(memory_space=pltpu.VMEM)
        moved = sum(o.size * o.dtype.itemsize for o in operands)
        return pl.pallas_call(
            kernel,
            in_specs=[place] * len(operands),
            out_specs=jax.tree.map(lambda _: place, out_shape),
            out_shape=out_shape,
            compiler_params=pltpu.CompilerParams(vmem_limit_bytes=48 * 1024 * 1024),
            cost_estimate=pl.CostEstimate(flops=0, bytes_accessed=3 * moved, transcendentals=0),
            name=name,
        )(*operands)

    return call


def pack_columns(plan, weights, scales):
    scales = jnp.pad(scales.reshape(2, plan.own), ((0, plan.own - 2), (0, 0)))
    packed = []
    for chosen, lanes in (((0, 2, 3), plan.first), ((1, 4), plan.second)):
        shape = jax.ShapeDtypeStruct((plan.n, plan.own, lanes), BF)
        kernel = functools.partial(pack_kernel, plan, chosen)
        packed.append(in_vmem(kernel, "pack_columns", shape)(scales, *[weights[w] for w in chosen]))
    return packed


def unpack_columns(plan, packed, parts):
    n, own, lanes = packed.shape
    outs_of = [(half * n // 2, n // 2, 0, lanes) for half in range(2)] if parts else []
    outs_of.append((0, n, 0, lanes))
    shapes = [jax.ShapeDtypeStruct((c * own, lanes), BF) for _, c, _, lanes in outs_of]
    kernel = functools.partial(unpack_kernel, own, outs_of)
    return in_vmem(kernel, "unpack_columns", shapes)(packed)


def pack_rows(own, n, gradients):
    lanes = sum(g.shape[1] for g in gradients)
    shape = jax.ShapeDtypeStruct((n, own, lanes), BF)
    return in_vmem(functools.partial(pack_rows_kernel, own), "pack_rows", shape)(*gradients)


def unpack_rows(plan, packed, chosen, begins):
    layout = []
    for weight, start, stride, lane, span in plan.segments():
        if weight in chosen:
            group = 0 if weight == 0 else 1 if weight in (2, 3) else 2
            lane += begins[group] - (0, plan.joined, plan.first)[group]
            layout.append((chosen.index(weight), start, stride, lane, span))
    widths = [3 * plan.width, plan.width, plan.units, plan.units, plan.units]
    shapes = [jax.ShapeDtypeStruct((plan.own, plan.n * widths[w]), F32) for w in chosen]
    kernel = functools.partial(unpack_rows_kernel, plan.n, layout)
    return in_vmem(kernel, "unpack_rows", shapes)(packed)


def fetch_pieces(pieces, held, sems):
    copies, row = [], 0
    for i, piece in enumerate(pieces):
        there = held.at[pl.ds(row, piece.shape[0]), :]
        copies.append(pltpu.make_async_copy(piece, there, sems.at[i]))
        row += piece.shape[0]
    return copies


def stream_kernel(n, n_pieces, n_extra, n_into, finish, *refs):
    blocks, refs = refs[:n], refs[n:]
    pieces, refs = refs[:n_pieces], refs[n_pieces + n_into :]
    extra, outs, (held, rows_ref, rows_sem, weight_sem) = refs[:n_extra], refs[n_extra:-4], refs[-4:]
    size = blocks[0].shape[0]
    step = pl.program_id(0)
    steps = n // 2
    weight = fetch_pieces(pieces, held, weight_sem)

    def copy(block, buffer, half):
        there = rows_ref.at[buffer, pl.ds(half * size, size), :]
        return pltpu.make_async_copy(block, there, rows_sem.at[buffer, half])

    def fetch(index):
        for place in range(steps):

            @pl.when(index == place)
            def _(place=place):
                for half in range(2):
                    copy(blocks[2 * place + half], place % 2, half).start()

    @pl.when(step == 0)
    def _():
        fetch(0)
        for piece in weight:
            piece.start()

    @pl.when(step + 1 < steps)
    def _():
        fetch(step + 1)

    buffer = lax.rem(step, 2)
    for half in range(2):
        copy(blocks[half], buffer, half).wait()

    @pl.when(step == 0)
    def _():
        for piece in weight:
            piece.wait()

    finish(rows_ref[buffer], held, extra, outs)


def stream(name, slots, places, pieces, extra, finish, outs, into):
    size, features = slots[0].shape
    blocks = [slots[2 * place + half] for place in places for half in range(2)]
    n = len(blocks)
    first, stride = places[0], places[1] - places[0]
    anywhere = pl.BlockSpec(memory_space=pl.ANY)

    def rows(width):
        return pl.BlockSpec((2 * size, width), lambda i: (first + stride * i, 0))

    outs = [(features, BF), *outs]
    width = pieces[0].shape[1]
    begin = n + len(pieces)
    return pl.pallas_call(
        functools.partial(stream_kernel, n, len(pieces), len(extra), len(into), finish),
        grid=(n // 2,),
        in_specs=[anywhere] * (begin + len(into)) + [rows(e.shape[1]) for e in extra],
        out_specs=[rows(w) for w, _ in outs],
        out_shape=[jax.ShapeDtypeStruct((len(slots) * size, w), dtype) for w, dtype in outs],
        input_output_aliases={begin + i: i for i in range(len(into))},
        scratch_shapes=[
            pltpu.VMEM((features, width), BF),
            pltpu.VMEM((2, 2 * size, features), BF),
            pltpu.SemaphoreType.DMA((2, 2)),
            pltpu.SemaphoreType.DMA((len(pieces),)),
        ],
        compiler_params=pltpu.CompilerParams(vmem_limit_bytes=52 * 1024 * 1024),
        cost_estimate=pl.CostEstimate(
            flops=2 * n * size * features * width,
            bytes_accessed=2 * (n * size + width) * features * 2,
            transcendentals=0,
        ),
        name=name,
    )(*blocks, *pieces, *into, *extra)


def swiglu(plan, both):
    body, tail = plan.body, plan.tail
    hidden, factors = [], []
    for start, span in ((0, body), (2 * body, tail)):
        gate, up = both[:, start : start + span], both[:, start + span : start + 2 * span]
        sigmoid = jax.nn.sigmoid(gate)
        silu = gate * sigmoid
        hidden.append((silu * up).astype(BF))
        factors += [up * sigmoid * (1.0 + gate * (1.0 - sigmoid)), silu]
    return hidden, factors


def project_finish(plan, rows, held, extra, outs):
    normed, joined, factor_ref, wide = outs
    normed[...] = rows
    joined[...] = dot(rows, held[:, : plan.joined])
    hidden, factors = swiglu(plan, dot(rows, held[:, plan.joined :]))
    lane = 0
    for factor in factors:
        factor_ref[:, lane : lane + factor.shape[1]] = factor.astype(factor_ref.dtype)
        lane += factor.shape[1]
    wide[:, : plan.width] = jnp.zeros((rows.shape[0], plan.width), BF)
    wide[:, plan.width : plan.width + plan.body] = hidden[0]
    pad = jnp.zeros((rows.shape[0], plan.second - plan.used), BF)
    wide[:, plan.width + plan.body :] = jnp.concatenate([hidden[1], pad], axis=1)


def return_finish(plan, rows, held, extra, outs):
    (factor_ref,), (cot, d_attn, d_both) = extra, outs
    cot[...] = rows
    total = dot(rows, held[...])
    d_attn[...] = total[:, : plan.width].astype(BF)
    begin, body, tail = plan.width, plan.body, plan.tail
    for lane, start, span in (
        (0, begin, body),
        (body, begin, body),
        (2 * body, begin + body, tail),
        (2 * body + tail, begin + body, tail),
    ):
        here = slice(lane, lane + span)
        d_both[:, here] = (total[:, start : start + span] * factor_ref[:, here]).astype(BF)


def spread_kernel(count, n_pieces, places, *refs):
    lefts, refs = refs[: count * places], refs[count * places :]
    pieces, outs, (held, sems) = refs[:n_pieces], refs[n_pieces:-2], refs[-2:]
    weight = fetch_pieces(pieces, held, sems)
    for piece in weight:
        piece.start()
    size = outs[0].shape[0]
    rows = held.shape[0] // 4
    begins = [sum(p.shape[0] for p in pieces[:i]) for i in range(n_pieces)]
    for part in range(4):
        here = slice(part * rows, (part + 1) * rows)
        for begin, piece in zip(begins, weight):
            if begin // rows == part:
                piece.wait()
        for place in range(places):
            total, lane = 0.0, 0
            for left in lefts[place * count : (place + 1) * count]:
                lanes = left.shape[1]
                total += dot_last(left[...], held[here, lane : lane + lanes])
                lane += lanes
            outs[2 * place][:, here] = total[:size].astype(BF)
            outs[2 * place + 1][:, here] = total[size:].astype(BF)


def spread(name, lefts, pieces, places, size):
    anywhere = pl.BlockSpec(memory_space=pl.ANY)
    features = sum(piece.shape[0] for piece in pieces)
    width = pieces[0].shape[1]
    tokens = 2 * size * len(places)

    def rows(left, place):
        return pl.BlockSpec((2 * size, left.shape[1]), lambda i: (place, 0))

    blocks = 2 * len(places)
    return pl.pallas_call(
        functools.partial(spread_kernel, len(lefts), len(pieces), len(places)),
        grid=(1,),
        in_specs=[rows(left, place) for place in places for left in lefts]
        + [anywhere] * len(pieces),
        out_specs=[pl.BlockSpec((size, features), lambda i: (0, 0))] * blocks,
        out_shape=[jax.ShapeDtypeStruct((size, features), BF)] * blocks,
        scratch_shapes=[
            pltpu.VMEM((features, width), BF),
            pltpu.SemaphoreType.DMA((len(pieces),)),
        ],
        compiler_params=pltpu.CompilerParams(vmem_limit_bytes=52 * 1024 * 1024),
        cost_estimate=pl.CostEstimate(
            flops=2 * tokens * features * width,
            bytes_accessed=2 * (tokens + features) * width + 2 * tokens * features,
            transcendentals=0,
        ),
        name=name,
    )(*[left for _ in places for left in lefts], *pieces)


class Layer:
    def __init__(self, n_ctx, slots, inputs, norm_gain, cotangent, lengths, units):
        self.groups, self.rows, self.features = inputs.shape
        self.tokens = self.groups * self.rows
        self.n_ctx, self.slots, self.lengths = n_ctx, slots, lengths
        self.own = norm_gain.shape[0]
        self.width = self.features // n_ctx
        self.plan = Plan(n_ctx, self.own, self.width, units)
        self.flat = inputs.reshape(self.tokens, self.features).astype(F32)
        self.cot = cotangent.reshape(self.tokens, self.features)
        self.tables = rotary_tables(n_ctx * self.rows, self.width)
        self.blocks = (n_ctx, self.groups, self.rows)

    def calls(self, lanes):
        heads = self.width // HD
        return attention_calls(self.n_ctx, self.groups, self.rows, self.width, heads, lanes)

    def standardize(self):
        center = self.flat - jnp.mean(self.flat, axis=-1, keepdims=True)
        variance = jnp.mean(center * center, axis=-1, keepdims=True)
        inverse = lax.rsqrt(variance + EPSILON)
        return center * inverse, inverse

    def norm(self, standard, scales):
        gain, bias = self.scales(scales)
        return (standard * gain + bias).astype(BF), gain

    def scales(self, scales):
        return [scales[:, i].astype(F32).reshape(1, self.features) for i in range(2)]

    def attend(self, joined, wide, tables):
        lanes = wide.shape[1]
        shape = (*self.blocks, lanes)
        joined = joined.reshape(*self.blocks, 3 * self.width)
        rotated, wide, lse = self.calls(lanes)[0](
            self.lengths, self.slots, joined, *tables, wide.reshape(shape)
        )
        return rotated, wide.reshape(-1, lanes), lse

    def attend_back(self, rotated, wide, d_attn, lse, tables):
        lanes = wide.shape[1]
        return self.calls(lanes)[1](
            self.lengths,
            self.slots,
            rotated,
            wide.reshape(*self.blocks, lanes),
            d_attn.reshape(*self.blocks, self.width),
            lse,
            *tables,
        ).reshape(-1, 3 * self.width)

    def finish_output(self, branches):
        return (self.flat + branches.astype(F32)).astype(BF)

    def norm_back(self, d_normed, standard, inverse, gain):
        d_normed = d_normed.astype(F32)
        grad = d_normed * gain
        centered = (
            grad
            - jnp.mean(grad, axis=-1, keepdims=True)
            - standard * jnp.mean(grad * standard, axis=-1, keepdims=True)
        )
        sums = [jnp.sum(d_normed * standard, axis=0), jnp.sum(d_normed, axis=0)]
        sums = jnp.concatenate([v.reshape(-1, self.own) for v in sums], axis=1)
        return (self.cot.astype(F32) + inverse * centered).astype(BF), sums


def on_any_mesh(layer, weights, scales):
    plan = layer.plan
    n, own, width = plan.n, plan.own, plan.width

    def swap(pieces):
        return lax.all_to_all(pieces, "ctx", split_axis=0, concat_axis=0, tiled=True)

    def gather(v, axis):
        return lax.all_gather(v, axis, axis=0, tiled=True)

    def scatter(v, axis):
        return lax.psum_scatter(v, axis, scatter_dimension=0, tiled=True)

    first, second = (swap(packed) for packed in pack_columns(plan, weights, scales))
    w_first = gather(unpack_columns(plan, first, False)[0], "dp")
    w_second = gather(unpack_columns(plan, second, False)[0], "dp")[:, : plan.used]
    scales = second[:, :2, plan.used :]
    standard, inverse = layer.standardize()
    normed, gain = layer.norm(standard, gather(scales, "dp"))
    normed, cot = gather(normed, "ctx"), gather(layer.cot, "ctx")
    total = dot(normed, w_first)
    hidden, factors = swiglu(plan, total[:, plan.joined :])
    empty = jnp.zeros((normed.shape[0], width), BF)
    rotated, attn, lse = layer.attend(total[:, : plan.joined], empty, layer.tables)
    wide = jnp.concatenate([attn, *hidden], axis=1)
    branches = scatter(dot_last(wide, w_second).astype(BF), "ctx")
    total = dot(cot, w_second)
    body = total[:, width : width + plan.body]
    tail = total[:, width + plan.body :]
    d_both = jnp.concatenate([body, body, tail, tail], axis=1) * jnp.concatenate(factors, axis=1)
    d_attn = total[:, :width].astype(BF)
    d_joined = layer.attend_back(rotated, attn, d_attn, lse, layer.tables)
    d_first = jnp.concatenate([d_joined, d_both.astype(BF)], axis=1)
    d_normed = scatter(dot_last(d_first, w_first).astype(BF), "ctx")
    sums = [scatter(dot_first(*v).astype(BF), "dp") for v in ((normed, d_first), (cot, wide))]
    begins = (0, plan.joined, plan.first)
    grads = unpack_rows(plan, swap(pack_rows(own, n, sums)), [0, 1, 2, 3, 4], begins)
    input_grad, norm_sums = layer.norm_back(d_normed, standard, inverse, gain)
    return layer.finish_output(branches), input_grad, scatter(norm_sums, ("dp", "ctx")), grads


def swaps(bit, n):
    return [(i, i ^ bit) for i in range(n)]


class State:
    def __init__(self, **arrays):
        self.held = arrays

    def __getitem__(self, name):
        return self.held[name]

    def drop(self, *names):
        for name in names:
            del self.held[name]

    def tick(self, before=(), sends=(), work=()):
        for action in before:
            self.held.update(action(self.held))
        view = dict(self.held)
        for name, source, axis, pairs in sends:
            view[name] = lax.ppermute(self.held[source], axis, pairs)
        for action in work:
            view.update(action(view))
        names = list(view)
        held = lax.optimization_barrier([view[name] for name in names])
        self.held = dict(zip(names, held))


def on_grid(layer, weights, scales):
    plan = layer.plan
    n, own, features = plan.n, plan.own, layer.features
    ctx, dp = lax.axis_index("ctx"), lax.axis_index("dp")
    z = ctx // 2
    inner = (z == 1) | (z == 2)
    quarter = features // 4
    side, pair = ("ctx", swaps(1, n)), ("ctx", swaps(2, n))
    middle = ("ctx", [(2, 4), (3, 5), (4, 2), (5, 3)])
    outward = ("ctx", [(2, 0), (3, 1), (4, 6), (5, 7)])
    inward = ("ctx", [(b, a) for a, b in outward[1]])
    core, across = ("dp", swaps(1, 4)), ("dp", swaps(2, 4))

    def blocks_of(v, first, steps):
        blocks = [
            lax.dynamic_slice_in_dim(v, (first ^ step) * quarter, quarter, 1) for step in steps
        ]
        return jnp.concatenate(blocks, axis=1)

    def reorder(v):
        return blocks_of(v, dp, (0, 2, 1, 3))

    def unorder(v):
        return blocks_of(v, (dp % 2) * 2 + dp // 2, (0, 2, 1, 3))

    opened = {}

    def doubled(held, axis, bit, size):
        mine = lax.axis_index(axis) // bit % 2
        got = lax.ppermute(held, axis, swaps(bit, size))
        first, second = jnp.where(mine == 0, held, got), jnp.where(mine == 0, got, held)
        return jnp.concatenate([first, second], axis=0)

    def begin(s):
        held = scales.reshape(1, 2, own)
        for bit in (1, 2, 4):
            held = doubled(held, "ctx", bit, n)
        packed, second = pack_columns(plan, weights, scales)
        packed, held, c0 = lax.optimization_barrier((packed, held, s["c0"]))
        packed = lax.all_to_all(packed, "ctx", split_axis=0, concat_axis=0, tiled=True)
        made = {"c0x": lax.ppermute(c0, *side), "c1": lax.ppermute(c0, *pair)}
        for bit in (1, 2):
            held = doubled(held, "dp", bit, 4)
        normed, gain = layer.norm(standard, held)
        n0 = reorder(normed)
        made |= {"n0": n0, "gain": gain, "n0x": lax.ppermute(n0, *side)}
        made |= {"n1": lax.ppermute(n0, *pair), "n2i": lax.ppermute(n0, *middle)}
        parts = unpack_columns(plan, packed, True)
        return made | {"second": second} | dict(zip(("a0", "b0", "ab0"), parts))

    def second_in(s):
        opened["second"] = lax.all_to_all(
            s["second"], "ctx", split_axis=0, concat_axis=0, tiled=True
        )
        return {}

    def select(name):
        return lambda s: {name: jnp.where(inner, s[name + "i"], s[name + "o"])}

    def plus(name, *parts):
        return lambda s: {name: sum(s[part].astype(F32) for part in parts).astype(BF)}

    def pieces(s, name):
        names = "a0 b0 a2 b2 ab1 a3 b3" if name == "ab" else "w0 w2 w1 w3"
        return [s[key] for key in names.split()]

    def slots(s, letter):
        return [s.get(letter + i) for i in ("0", "0x", "1", "1x", "2", "2x", "3", "3x")]

    def streamed(name, letter, weight, names, finish, widths, extra, places):
        def work(s):
            done = [s[key] for key in names] if places[0] else []
            held = (slots(s, letter), places, pieces(s, weight), [s[key] for key in extra])
            made = stream(name, *held, functools.partial(finish, plan), widths, done)
            return dict(zip(names, made))

        return work

    def project(*places):
        names = ("n", "joined", "factors", "wide")
        widths = [(plan.joined, F32), (2 * plan.units, BF), (plan.second, BF)]
        return streamed("project", "n", "ab", names, project_finish, widths, [], places)

    def bring_back(*places):
        names = ("c", "d_attn", "d_both")
        widths = [(plan.width, BF), (2 * plan.units, BF)]
        held = ("factors",)
        return streamed("bring_back", "c", "w", names, return_finish, widths, held, places)

    def tables(s):
        return {"tables": layer.tables}

    def attend(s):
        made = layer.attend(s["joined"], s["wide"], s["tables"])
        return dict(zip(("rotated", "wide", "lse"), made))

    def attend_back(s):
        d_joined = layer.attend_back(
            s["rotated"], s["wide"], s["d_attn"], s["lse"], s["tables"]
        )
        return {"d_joined": d_joined}

    def scattered(name, letter, lefts, weight, places):
        def work(s):
            size = s["c0"].shape[0]
            made = spread(name, [s[v] for v in lefts], pieces(s, weight), places, size)
            keys = [f"{letter}{place}{kind}" for place in places for kind in "ka"]
            return dict(zip(keys, made))

        return work

    def output_part(*places):
        return scattered("output_part", "o", ["wide"], "w", places)

    def normed_part(*places):
        return scattered("normed_part", "d", ["d_joined", "d_both"], "ab", places)

    factors = {"J": ("n", "d_joined"), "G": ("n", "d_both"), "W": ("c", "wide")}

    def product(s, name, begin, end):
        left, right = factors[name]
        return dot_first(s[left][:, begin * quarter : end * quarter], s[right])

    def grad_a(name):
        return lambda s: {name + "A": product(s, name, 2, 4).astype(BF)}

    def grad_b(name):
        def work(s):
            total = product(s, name, 1, 2) + s[name + "Ar"][quarter:].astype(F32)
            return {name + "B": total.astype(BF)}

        return work

    def grad_c(name):
        def work(s):
            total = product(s, name, 0, 1) + s[name + "Ar"][:quarter].astype(F32)
            return {name + "C": (total + s[name + "Br"].astype(F32)).astype(BF)}

        return work

    def to(name, source, way):
        return (name, source, *way)

    def cross(name):
        return lambda s: {name + "Ar": lax.ppermute(s[name + "A"], *core)}

    def send_a(name):
        return to(name + "Ar", name + "A", core)

    def send_b(name):
        return to(name + "Br", name + "B", across)

    def packed_rows(*names):
        return lambda s: {names: pack_rows(own, n, [s[name + "C"] for name in names])}

    def swap_packed(*names):
        def work(s):
            opened[names] = lax.all_to_all(
                s[names], "ctx", split_axis=0, concat_axis=0, tiled=True
            )
            return {}

        return work

    def norm_back(s):
        input_grad, sums = layer.norm_back(unorder(s["d"]), standard, inverse, s["gain"])

        def halved(sums, dim, axis, bit, size):
            mine = lax.axis_index(axis) // bit % 2
            first, second = jnp.split(sums, 2, axis=dim)
            give = jnp.where(mine == 0, second, first)
            return jnp.where(mine == 0, first, second) + lax.ppermute(give, axis, swaps(bit, size))

        sums = sums.reshape(4, n, 2 * own)
        for bit in (4, 2, 1):
            sums = halved(sums, 1, "ctx", bit, n)
        names = ("J", "W")
        packed, sums = lax.optimization_barrier((s[names], sums))
        opened[names] = lax.all_to_all(packed, "ctx", split_axis=0, concat_axis=0, tiled=True)
        for bit in (2, 1):
            sums = halved(sums, 0, "dp", bit, 4)
        return {"input_grad": input_grad, "norm_sums": sums[0]}

    def y(name):
        return to(name + "2", name + "0", across)

    def near(name):
        return to(name + "1", name + "0", core)

    def far(name):
        return to(name + "3", name + "2", core)

    standard, inverse = layer.standardize()
    st = State(c0=reorder(layer.cot))
    tick = st.tick
    tick((), (), [begin])
    tick(
        (),
        [
            to("n1x", "n1", side),
            to("n3i", "n1", middle),
            to("n2o", "n2i", outward),
            y("a"),
            near("ab"),
        ],
        [second_in, tables],
    )
    tick(
        [select("n2")],
        [
            to("n2x", "n2", side),
            to("n3o", "n3i", outward),
            to("c2i", "c0", middle),
            y("b"),
            far("a"),
        ],
    )
    tick(
        [select("n3")],
        [
            to("n3x", "n3", side),
            to("c2o", "c2i", outward),
            to("c3i", "c1", middle),
            far("b"),
        ],
        [project(0, 1)],
    )
    tick(
        [select("c2"), lambda s: {"w0": unpack_columns(plan, opened["second"], False)[0]}],
        [to("c2x", "c2", side), to("c3o", "c3i", outward), y("w"), near("w")],
        [project(2, 3)],
    )
    tick(
        [select("c3")],
        [to("c3x", "c3", side), to("c1x", "c0x", pair), far("w")],
        [attend, output_part(0, 1, 2, 3)],
    )
    tick(
        (),
        [to("o3x", "o3a", side), to("o1p", "o1a", pair)],
        [bring_back(0, 1, 2, 3), grad_a("G")],
    )
    tick(
        [plus("o3", "o3k", "o3x")],
        [to("o2x", "o2a", side), to("o3i", "o3", inward), send_a("G")],
        [attend_back, grad_b("G")],
    )
    tick(
        [plus("o2", "o2k", "o2x"), plus("o3", "o3", "o3i"), plus("o0a", "o0a", "o1p")],
        [to("o0x", "o0a", side), to("o2i", "o2", inward), to("o3m", "o3", middle), send_b("G")],
        [normed_part(1, 3)],
    )
    tick(
        [plus("o2", "o2", "o2i"), plus("o1", "o1k", "o3m")],
        [to("d3x", "d3a", side), to("o2m", "o2", middle), to("o1r", "o1", pair)],
        [normed_part(0, 2), grad_c("G"), packed_rows("G")],
    )
    tick(
        [plus("d3", "d3k", "d3x")],
        [to("d2x", "d2a", side), to("d3i", "d3", inward)],
        [
            swap_packed("G"),
            grad_a("J"),
            cross("J"),
            grad_b("J"),
            grad_a("W"),
            plus("o", "o0k", "o0x", "o2m", "o1r"),
        ],
    )
    tick(
        [plus("d2", "d2k", "d2x"), plus("d3", "d3", "d3i")],
        [
            to("d1x", "d1a", side),
            to("d2i", "d2", inward),
            to("d3m", "d3", middle),
            send_b("J"),
            send_a("W"),
        ],
        [grad_b("W"), grad_c("J")],
    )
    tick(
        [plus("d2", "d2", "d2i"), plus("d1", "d1k", "d1x", "d3m")],
        [to("d0x", "d0a", side), to("d2m", "d2", middle), to("d1r", "d1", pair), send_b("W")],
        [grad_c("W"), packed_rows("J", "W")],
    )
    tick([plus("d", "d0k", "d0x", "d2m", "d1r")], (), [norm_back])
    gate_grad, up_grad = unpack_rows(plan, opened["G",], [2, 3], (0, 0, 0))
    begins = (0, 0, plan.joined)
    joined_grad, out_grad, down_grad = unpack_rows(plan, opened["J", "W"], [0, 1, 4], begins)
    grads = [joined_grad, out_grad, gate_grad, up_grad, down_grad]
    return layer.finish_output(unorder(st["o"])), st["input_grad"], st["norm_sums"], grads


def on_device(
    n_ctx,
    n_dp,
    inputs,
    norm_gain,
    norm_bias,
    joined_weight,
    gate_weight,
    up_weight,
    out_weight,
    down_weight,
    cotangent,
    lengths,
):
    grid = (n_ctx, n_dp) == (8, 4)
    if grid:
        ctx = lax.axis_index("ctx")
        z, x = ctx // 2, ctx % 2
        high = z >= 2
        order = [z, z ^ 1, jnp.where(high, 1, 2), jnp.where(high, 0, 3)]
        natural = [2 * o + (x ^ r) for o in order for r in range(2)]
        slots = jnp.zeros((n_ctx,), jnp.int32)
        for slot, part in enumerate(natural):
            slots = jnp.where(jnp.arange(n_ctx) == part, slot, slots)
    else:
        slots = jnp.arange(n_ctx, dtype=jnp.int32)
    units = gate_weight.shape[1] // n_ctx
    layer = Layer(n_ctx, slots, inputs, norm_gain, cotangent, lengths, units)
    weights = (joined_weight, out_weight, gate_weight, up_weight, down_weight)
    scales = jnp.concatenate([norm_gain, norm_bias])
    run = on_grid if grid else on_any_mesh
    output, input_grad, norm_sums, grads = run(layer, weights, scales)
    joined_grad, out_grad, gate_grad, up_grad, down_grad = grads
    return (
        output.reshape(inputs.shape),
        input_grad.reshape(inputs.shape),
        norm_sums[0, : layer.own],
        norm_sums[0, layer.own :],
        joined_grad,
        gate_grad,
        up_grad,
        out_grad,
        down_grad,
    )


def solution(mesh):
    rows = P(("dp", "ctx"), None)
    vector = P(("dp", "ctx"))
    tokens = P("dp", "ctx", None)
    return jax.shard_map(
        functools.partial(on_device, mesh.shape["ctx"], mesh.shape["dp"]),
        mesh=mesh,
        in_specs=(tokens, vector, vector, rows, rows, rows, rows, rows, tokens, P("dp")),
        out_specs=(tokens, tokens, vector, vector, rows, rows, rows, rows, rows),
        check_vma=False,
    )
```

```python
import functools

import jax
import jax.numpy as jnp
from jax import lax
from jax.experimental import pallas as pl
from jax.experimental.pallas import tpu as pltpu
from jax.sharding import PartitionSpec as P

HD = 64
ROT = 16
ATTEND_ROWS = 512
EPSILON = 1e-05
THETA = 10000.0
NEGATIVE = -1e30
BF = jnp.bfloat16
F32 = jnp.float32
LAST = (((1,), (1,)), ((), ()))
FIRST = (((0,), (0,)), ((), ()))


def dot(left, right):
    return jnp.dot(left, right, preferred_element_type=F32)


def dot_last(left, right):
    return lax.dot_general(left, right, LAST, preferred_element_type=F32)


def dot_first(left, right):
    return lax.dot_general(left, right, FIRST, preferred_element_type=F32)


def rotary_tables(length, width):
    half = ROT // 2
    lane = jnp.arange(width, dtype=jnp.int32) % HD
    frequency = THETA ** (-(2.0 * (lane % half).astype(F32)) / ROT)
    angles = jnp.arange(length, dtype=jnp.int32).astype(F32)[:, None] * frequency[None, :]
    cosine = jnp.where(lane[None, :] < ROT, jnp.cos(angles), 1.0)
    sine = jnp.sin(angles)
    sine = jnp.where(lane[None, :] < half, -sine, jnp.where(lane[None, :] < ROT, sine, 0.0))
    return cosine, sine


def partner(x):
    half = ROT // 2
    lane = lax.broadcasted_iota(jnp.int32, x.shape, 1) % HD
    down = jnp.concatenate([x[:, half:], x[:, :half]], axis=1)
    up = jnp.concatenate([x[:, -half:], x[:, :-half]], axis=1)
    return jnp.where(lane < half, down, up)


def attend_forward(
    length_ref, slot_ref, joined_ref, cos_ref, sin_ref, wide_ref, rot_ref, attn_ref, lse_ref
):
    parts, _, rows, triple = joined_ref.shape
    width = triple // 3
    length = parts * rows
    alive_count = length_ref[pl.program_id(0)]
    per = max(1, min(ATTEND_ROWS, length) // rows)
    block = per * rows
    for part in range(parts):
        slot = slot_ref[part]
        here = slice(part * rows, (part + 1) * rows)

        def rotated(start):
            x = joined_ref[slot, 0, :, start : start + width]
            return (x * cos_ref[here, :] + partner(x) * sin_ref[here, :]).astype(BF)

        rot_ref[part, 0, :, :width] = rotated(0) * 0.125
        rot_ref[part, 0, :, width : 2 * width] = rotated(width)
        rot_ref[part, 0, :, 2 * width :] = joined_ref[slot, 0, :, 2 * width :].astype(BF)
    lse_ref[...] = jnp.zeros_like(lse_ref)
    heads = width // HD
    for step in range(length // block):
        begin, end = step * per, (step + 1) * per
        stop = end * rows
        slots = [slot_ref[part] for part in range(begin, end)]

        @pl.when(begin * rows >= alive_count)
        def _(slots=slots):
            for slot in slots:
                attn_ref[slot, 0] = jnp.zeros((rows, width), BF)

        @pl.when(begin * rows < alive_count)
        def _(begin=begin, end=end, stop=stop, slots=slots):
            q_pos = begin * rows + lax.broadcasted_iota(jnp.int32, (block, 1), 0)
            k_pos = lax.broadcasted_iota(jnp.int32, (block, stop), 1)
            allowed = k_pos <= q_pos
            alive = q_pos < alive_count
            for head in range(heads):
                lane = head * HD
                q = rot_ref[begin:end, 0, :, lane : lane + HD].reshape(block, HD)
                lane += width
                k = rot_ref[:end, 0, :, lane : lane + HD].reshape(stop, HD)
                lane += width
                v = rot_ref[:end, 0, :, lane : lane + HD].reshape(stop, HD)
                scores = jnp.where(allowed, dot_last(q, k), NEGATIVE)
                top = jnp.max(scores, axis=1, keepdims=True)
                expo = jnp.exp(scores - top)
                weight = jnp.sum(expo, axis=1, keepdims=True)
                out = jnp.where(alive, dot(expo.astype(BF), v) / weight, 0.0).astype(BF)
                for index, slot in enumerate(slots):
                    there = slice(index * rows, (index + 1) * rows)
                    attn_ref[slot, 0, :, head * HD : (head + 1) * HD] = out[there, :]
                lse = jnp.where(alive, top + jnp.log(weight), 0.0)
                lse_ref[begin:end, 0, :, head : head + 1] = lse.reshape(per, rows, 1)


def attend_backward(
    length_ref, slot_ref, rot_ref, attn_ref, grad_ref, lse_ref, cos_ref, sin_ref, out_ref, dq, dk, dv
):
    parts, _, rows, triple = rot_ref.shape
    width = triple // 3
    length = parts * rows
    seq = pl.program_id(0)
    head = pl.program_id(1)
    alive_count = length_ref[seq]
    per = max(1, min(ATTEND_ROWS, length) // rows)
    block = per * rows
    lane = lax.broadcasted_iota(jnp.int32, (1, width), 1)
    mine = (lane // HD) == head

    @pl.when(head == 0)
    def _():
        dq[...] = jnp.zeros_like(dq)
        dk[...] = jnp.zeros_like(dk)
        dv[...] = jnp.zeros_like(dv)

    for step in range(length // block):
        begin, end = step * per, (step + 1) * per
        stop = end * rows

        @pl.when(begin * rows < alive_count)
        def _(begin=begin, end=end, stop=stop):
            q_pos = begin * rows + lax.broadcasted_iota(jnp.int32, (block, 1), 0)
            alive = q_pos < alive_count
            q = rot_ref[begin:end, 0, :, :width].reshape(block, width)
            q = jnp.where(mine, q, jnp.zeros_like(q))
            k = rot_ref[:end, 0, :, width : 2 * width].reshape(stop, width)
            v = rot_ref[:end, 0, :, 2 * width :].reshape(stop, width)
            slots = [slot_ref[part] for part in range(begin, end)]
            g = jnp.concatenate([grad_ref[slot, 0] for slot in slots], axis=0)
            g = jnp.where(mine & alive, g, jnp.zeros_like(g))
            o = jnp.concatenate([attn_ref[slot, 0] for slot in slots], axis=0)
            delta = jnp.sum(g.astype(F32) * o.astype(F32), axis=1, keepdims=True)
            held = lse_ref[begin:end, 0].reshape(block, lse_ref.shape[3])
            spot = lax.broadcasted_iota(jnp.int32, (1, lse_ref.shape[3]), 1) == head
            lse = jnp.sum(jnp.where(spot, held, 0.0), axis=1, keepdims=True)
            scores = dot_last(q, k)
            k_pos = lax.broadcasted_iota(jnp.int32, (block, stop), 1)
            probs = jnp.where((k_pos <= q_pos) & alive, jnp.exp(scores - lse), 0.0)
            d_probs = dot_last(g, v)
            d_scores = (probs * (d_probs - delta)).astype(BF)
            here = slice(begin * rows, stop)
            dq[here, :] += jnp.where(mine, dot(d_scores, k), 0.0)
            dk[:stop, :] += dot_first(d_scores, q)
            dv[:stop, :] += dot_first(probs.astype(BF), g)

    @pl.when(head == pl.num_programs(1) - 1)
    def _():
        for part in range(parts):
            slot = slot_ref[part]
            here = slice(part * rows, (part + 1) * rows)

            def unrotated(x):
                return (x * cos_ref[here, :] - partner(x) * sin_ref[here, :]).astype(BF)

            out_ref[slot, 0, :, :width] = unrotated(dq[here, :] * 0.125)
            out_ref[slot, 0, :, width : 2 * width] = unrotated(dk[here, :])
            out_ref[slot, 0, :, 2 * width :] = dv[here, :].astype(BF)


def attention_calls(parts, groups, rows, width, heads, lanes):
    length = parts * rows
    smem = pl.BlockSpec(memory_space=pltpu.SMEM)

    def spec(last):
        return pl.BlockSpec((parts, 1, rows, last), lambda s, *_: (0, s, 0, 0))

    table = pl.BlockSpec((length, width), lambda *_: (0, 0))

    def shape(last, dtype):
        return jax.ShapeDtypeStruct((parts, groups, rows, last), dtype)

    pairs = groups * heads * length * length // 2
    params = pltpu.CompilerParams(vmem_limit_bytes=48 * 1024 * 1024)
    forward = pl.pallas_call(
        attend_forward,
        grid=(groups,),
        in_specs=[smem, smem, spec(3 * width), table, table, pl.BlockSpec(memory_space=pl.ANY)],
        out_specs=[spec(3 * width), spec(width), spec(heads)],
        out_shape=[shape(3 * width, BF), shape(lanes, BF), shape(heads, F32)],
        input_output_aliases={5: 1},
        compiler_params=params,
        cost_estimate=pl.CostEstimate(
            flops=pairs * 1024, bytes_accessed=16 * length * width, transcendentals=pairs
        ),
        name="attend_forward",
    )
    backward = pl.pallas_call(
        attend_backward,
        grid=(groups, heads),
        in_specs=[smem, smem, spec(3 * width), spec(width), spec(width), spec(heads), table, table],
        out_specs=spec(3 * width),
        out_shape=shape(3 * width, BF),
        scratch_shapes=[pltpu.VMEM((length, width), F32)] * 3,
        compiler_params=params,
        cost_estimate=pl.CostEstimate(
            flops=pairs * 2560, bytes_accessed=16 * length * width, transcendentals=pairs
        ),
        name="attend_backward",
    )
    return forward, backward


class Plan:
    def __init__(self, n, own, width, units):
        self.n, self.own, self.width, self.units = n, own, width, units
        self.body = units // 128 * 128
        self.tail = units - self.body
        self.joined = 3 * width
        self.first = self.joined + 2 * units
        self.used = width + units
        self.second = self.used + own
        spans = [(0, r * n * width, width, width) for r in range(3)]
        for start, span in ((0, self.body), (self.body, self.tail)):
            spans += [(w, start, units, span) for w in (2, 3)]
        self.spans = [*spans, (1, 0, width, width), (4, 0, units, units)]

    def segments(self):
        lane = 0
        for weight, start, stride, span in self.spans:
            yield weight, start, stride, lane, span
            lane += span


def pack_kernel(plan, chosen, *refs):
    scale_ref, sources, out_ref = refs[0], dict(zip(chosen, refs[1:-1])), refs[-1]
    lane = 0
    for weight, start, stride, _, span in plan.segments():
        if weight in chosen:
            for dest in range(plan.n):
                begin = start + dest * stride
                out_ref[dest, :, lane : lane + span] = sources[weight][:, begin : begin + span]
            lane += span
    if lane < out_ref.shape[2]:
        for dest in range(plan.n):
            out_ref[dest, :, lane:] = scale_ref[...]


def unpack_kernel(own, outs_of, in_ref, *outs):
    for out, (source, sources, lane, lanes) in zip(outs, outs_of):
        for index in range(sources):
            block = in_ref[source + index, :, lane : lane + lanes]
            out[index * own : (index + 1) * own, :] = block


def pack_rows_kernel(own, *refs):
    sources, out = refs[:-1], refs[-1]
    for dest in range(out.shape[0]):
        lane = 0
        for source in sources:
            lanes = source.shape[1]
            out[dest, :, lane : lane + lanes] = source[dest * own : (dest + 1) * own, :]
            lane += lanes


def unpack_rows_kernel(n, layout, held, *outs):
    for source in range(n):
        for out, start, stride, lane, span in layout:
            begin = start + source * stride
            block = held[source, :, lane : lane + span].astype(F32)
            outs[out][:, begin : begin + span] = block


def in_vmem(kernel, name, out_shape):
    def call(*operands):
        place = pl.BlockSpec(memory_space=pltpu.VMEM)
        moved = sum(o.size * o.dtype.itemsize for o in operands)
        return pl.pallas_call(
            kernel,
            in_specs=[place] * len(operands),
            out_specs=jax.tree.map(lambda _: place, out_shape),
            out_shape=out_shape,
            compiler_params=pltpu.CompilerParams(vmem_limit_bytes=48 * 1024 * 1024),
            cost_estimate=pl.CostEstimate(flops=0, bytes_accessed=3 * moved, transcendentals=0),
            name=name,
        )(*operands)

    return call


def pack_columns(plan, weights, scales):
    scales = jnp.pad(scales.reshape(2, plan.own), ((0, plan.own - 2), (0, 0)))
    packed = []
    for chosen, lanes in (((0, 2, 3), plan.first), ((1, 4), plan.second)):
        shape = jax.ShapeDtypeStruct((plan.n, plan.own, lanes), BF)
        kernel = functools.partial(pack_kernel, plan, chosen)
        packed.append(in_vmem(kernel, "pack_columns", shape)(scales, *[weights[w] for w in chosen]))
    return packed


def unpack_columns(plan, packed, parts):
    n, own, lanes = packed.shape
    outs_of = [(half * n // 2, n // 2, 0, lanes) for half in range(2)] if parts else []
    outs_of.append((0, n, 0, lanes))
    shapes = [jax.ShapeDtypeStruct((c * own, lanes), BF) for _, c, _, lanes in outs_of]
    kernel = functools.partial(unpack_kernel, own, outs_of)
    return in_vmem(kernel, "unpack_columns", shapes)(packed)


def pack_rows(own, n, gradients):
    lanes = sum(g.shape[1] for g in gradients)
    shape = jax.ShapeDtypeStruct((n, own, lanes), BF)
    return in_vmem(functools.partial(pack_rows_kernel, own), "pack_rows", shape)(*gradients)


def unpack_rows(plan, packed, chosen, begins):
    layout = []
    for weight, start, stride, lane, span in plan.segments():
        if weight in chosen:
            group = 0 if weight == 0 else 1 if weight in (2, 3) else 2
            lane += begins[group] - (0, plan.joined, plan.first)[group]
            layout.append((chosen.index(weight), start, stride, lane, span))
    widths = [3 * plan.width, plan.width, plan.units, plan.units, plan.units]
    shapes = [jax.ShapeDtypeStruct((plan.own, plan.n * widths[w]), F32) for w in chosen]
    kernel = functools.partial(unpack_rows_kernel, plan.n, layout)
    return in_vmem(kernel, "unpack_rows", shapes)(packed)


def fetch_pieces(pieces, held, sems):
    copies, row = [], 0
    for i, piece in enumerate(pieces):
        there = held.at[pl.ds(row, piece.shape[0]), :]
        copies.append(pltpu.make_async_copy(piece, there, sems.at[i]))
        row += piece.shape[0]
    return copies


def stream_kernel(n, n_pieces, n_extra, n_into, finish, *refs):
    blocks, refs = refs[:n], refs[n:]
    pieces, refs = refs[:n_pieces], refs[n_pieces + n_into :]
    extra, outs, (held, rows_ref, rows_sem, weight_sem) = refs[:n_extra], refs[n_extra:-4], refs[-4:]
    size = blocks[0].shape[0]
    step = pl.program_id(0)
    steps = n // 2
    weight = fetch_pieces(pieces, held, weight_sem)

    def copy(block, buffer, half):
        there = rows_ref.at[buffer, pl.ds(half * size, size), :]
        return pltpu.make_async_copy(block, there, rows_sem.at[buffer, half])

    def fetch(index):
        for place in range(steps):

            @pl.when(index == place)
            def _(place=place):
                for half in range(2):
                    copy(blocks[2 * place + half], place % 2, half).start()

    @pl.when(step == 0)
    def _():
        fetch(0)
        for piece in weight:
            piece.start()

    @pl.when(step + 1 < steps)
    def _():
        fetch(step + 1)

    buffer = lax.rem(step, 2)
    for half in range(2):
        copy(blocks[half], buffer, half).wait()

    @pl.when(step == 0)
    def _():
        for piece in weight:
            piece.wait()

    finish(rows_ref[buffer], held, extra, outs)


def stream(name, slots, places, pieces, extra, finish, outs, into):
    size, features = slots[0].shape
    blocks = [slots[2 * place + half] for place in places for half in range(2)]
    n = len(blocks)
    first, stride = places[0], places[1] - places[0]
    anywhere = pl.BlockSpec(memory_space=pl.ANY)

    def rows(width):
        return pl.BlockSpec((2 * size, width), lambda i: (first + stride * i, 0))

    outs = [(features, BF), *outs]
    width = pieces[0].shape[1]
    begin = n + len(pieces)
    return pl.pallas_call(
        functools.partial(stream_kernel, n, len(pieces), len(extra), len(into), finish),
        grid=(n // 2,),
        in_specs=[anywhere] * (begin + len(into)) + [rows(e.shape[1]) for e in extra],
        out_specs=[rows(w) for w, _ in outs],
        out_shape=[jax.ShapeDtypeStruct((len(slots) * size, w), dtype) for w, dtype in outs],
        input_output_aliases={begin + i: i for i in range(len(into))},
        scratch_shapes=[
            pltpu.VMEM((features, width), BF),
            pltpu.VMEM((2, 2 * size, features), BF),
            pltpu.SemaphoreType.DMA((2, 2)),
            pltpu.SemaphoreType.DMA((len(pieces),)),
        ],
        compiler_params=pltpu.CompilerParams(vmem_limit_bytes=52 * 1024 * 1024),
        cost_estimate=pl.CostEstimate(
            flops=2 * n * size * features * width,
            bytes_accessed=2 * (n * size + width) * features * 2,
            transcendentals=0,
        ),
        name=name,
    )(*blocks, *pieces, *into, *extra)


def swiglu(plan, both):
    body, tail = plan.body, plan.tail
    hidden, factors = [], []
    for start, span in ((0, body), (2 * body, tail)):
        gate, up = both[:, start : start + span], both[:, start + span : start + 2 * span]
        sigmoid = jax.nn.sigmoid(gate)
        silu = gate * sigmoid
        hidden.append((silu * up).astype(BF))
        factors += [up * sigmoid * (1.0 + gate * (1.0 - sigmoid)), silu]
    return hidden, factors


def project_finish(plan, rows, held, extra, outs):
    normed, joined, factor_ref, wide = outs
    normed[...] = rows
    joined[...] = dot(rows, held[:, : plan.joined])
    hidden, factors = swiglu(plan, dot(rows, held[:, plan.joined :]))
    lane = 0
    for factor in factors:
        factor_ref[:, lane : lane + factor.shape[1]] = factor.astype(factor_ref.dtype)
        lane += factor.shape[1]
    wide[:, : plan.width] = jnp.zeros((rows.shape[0], plan.width), BF)
    wide[:, plan.width : plan.width + plan.body] = hidden[0]
    pad = jnp.zeros((rows.shape[0], plan.second - plan.used), BF)
    wide[:, plan.width + plan.body :] = jnp.concatenate([hidden[1], pad], axis=1)


def return_finish(plan, rows, held, extra, outs):
    (factor_ref,), (cot, d_attn, d_both) = extra, outs
    cot[...] = rows
    total = dot(rows, held[...])
    d_attn[...] = total[:, : plan.width].astype(BF)
    begin, body, tail = plan.width, plan.body, plan.tail
    for lane, start, span in (
        (0, begin, body),
        (body, begin, body),
        (2 * body, begin + body, tail),
        (2 * body + tail, begin + body, tail),
    ):
        here = slice(lane, lane + span)
        d_both[:, here] = (total[:, start : start + span] * factor_ref[:, here]).astype(BF)


def spread_kernel(count, n_pieces, places, *refs):
    lefts, refs = refs[: count * places], refs[count * places :]
    pieces, outs, (held, sems) = refs[:n_pieces], refs[n_pieces:-2], refs[-2:]
    weight = fetch_pieces(pieces, held, sems)
    for piece in weight:
        piece.start()
    size = outs[0].shape[0]
    rows = held.shape[0] // 4
    begins = [sum(p.shape[0] for p in pieces[:i]) for i in range(n_pieces)]
    for part in range(4):
        here = slice(part * rows, (part + 1) * rows)
        for begin, piece in zip(begins, weight):
            if begin // rows == part:
                piece.wait()
        for place in range(places):
            total, lane = 0.0, 0
            for left in lefts[place * count : (place + 1) * count]:
                lanes = left.shape[1]
                total += dot_last(left[...], held[here, lane : lane + lanes])
                lane += lanes
            outs[2 * place][:, here] = total[:size].astype(BF)
            outs[2 * place + 1][:, here] = total[size:].astype(BF)


def spread(name, lefts, pieces, places, size):
    anywhere = pl.BlockSpec(memory_space=pl.ANY)
    features = sum(piece.shape[0] for piece in pieces)
    width = pieces[0].shape[1]
    tokens = 2 * size * len(places)

    def rows(left, place):
        return pl.BlockSpec((2 * size, left.shape[1]), lambda i: (place, 0))

    blocks = 2 * len(places)
    return pl.pallas_call(
        functools.partial(spread_kernel, len(lefts), len(pieces), len(places)),
        grid=(1,),
        in_specs=[rows(left, place) for place in places for left in lefts]
        + [anywhere] * len(pieces),
        out_specs=[pl.BlockSpec((size, features), lambda i: (0, 0))] * blocks,
        out_shape=[jax.ShapeDtypeStruct((size, features), BF)] * blocks,
        scratch_shapes=[
            pltpu.VMEM((features, width), BF),
            pltpu.SemaphoreType.DMA((len(pieces),)),
        ],
        compiler_params=pltpu.CompilerParams(vmem_limit_bytes=52 * 1024 * 1024),
        cost_estimate=pl.CostEstimate(
            flops=2 * tokens * features * width,
            bytes_accessed=2 * (tokens + features) * width + 2 * tokens * features,
            transcendentals=0,
        ),
        name=name,
    )(*[left for _ in places for left in lefts], *pieces)


class Layer:
    def __init__(self, n_ctx, slots, inputs, norm_gain, cotangent, lengths, units):
        self.groups, self.rows, self.features = inputs.shape
        self.tokens = self.groups * self.rows
        self.n_ctx, self.slots, self.lengths = n_ctx, slots, lengths
        self.own = norm_gain.shape[0]
        self.width = self.features // n_ctx
        self.plan = Plan(n_ctx, self.own, self.width, units)
        self.flat = inputs.reshape(self.tokens, self.features).astype(F32)
        self.cot = cotangent.reshape(self.tokens, self.features)
        self.tables = rotary_tables(n_ctx * self.rows, self.width)
        self.blocks = (n_ctx, self.groups, self.rows)

    def calls(self, lanes):
        heads = self.width // HD
        return attention_calls(self.n_ctx, self.groups, self.rows, self.width, heads, lanes)

    def standardize(self):
        center = self.flat - jnp.mean(self.flat, axis=-1, keepdims=True)
        variance = jnp.mean(center * center, axis=-1, keepdims=True)
        inverse = lax.rsqrt(variance + EPSILON)
        return center * inverse, inverse

    def norm(self, standard, scales):
        gain, bias = self.scales(scales)
        return (standard * gain + bias).astype(BF), gain

    def scales(self, scales):
        return [scales[:, i].astype(F32).reshape(1, self.features) for i in range(2)]

    def attend(self, joined, wide, tables):
        lanes = wide.shape[1]
        shape = (*self.blocks, lanes)
        joined = joined.reshape(*self.blocks, 3 * self.width)
        rotated, wide, lse = self.calls(lanes)[0](
            self.lengths, self.slots, joined, *tables, wide.reshape(shape)
        )
        return rotated, wide.reshape(-1, lanes), lse

    def attend_back(self, rotated, wide, d_attn, lse, tables):
        lanes = wide.shape[1]
        return self.calls(lanes)[1](
            self.lengths,
            self.slots,
            rotated,
            wide.reshape(*self.blocks, lanes),
            d_attn.reshape(*self.blocks, self.width),
            lse,
            *tables,
        ).reshape(-1, 3 * self.width)

    def finish_output(self, branches):
        return (self.flat + branches.astype(F32)).astype(BF)

    def norm_back(self, d_normed, standard, inverse, gain):
        d_normed = d_normed.astype(F32)
        grad = d_normed * gain
        centered = (
            grad
            - jnp.mean(grad, axis=-1, keepdims=True)
            - standard * jnp.mean(grad * standard, axis=-1, keepdims=True)
        )
        sums = [jnp.sum(d_normed * standard, axis=0), jnp.sum(d_normed, axis=0)]
        sums = jnp.concatenate([v.reshape(-1, self.own) for v in sums], axis=1)
        return (self.cot.astype(F32) + inverse * centered).astype(BF), sums


def on_any_mesh(layer, weights, scales):
    plan = layer.plan
    n, own, width = plan.n, plan.own, plan.width

    def swap(pieces):
        return lax.all_to_all(pieces, "ctx", split_axis=0, concat_axis=0, tiled=True)

    def gather(v, axis):
        return lax.all_gather(v, axis, axis=0, tiled=True)

    def scatter(v, axis):
        return lax.psum_scatter(v, axis, scatter_dimension=0, tiled=True)

    first, second = (swap(packed) for packed in pack_columns(plan, weights, scales))
    w_first = gather(unpack_columns(plan, first, False)[0], "dp")
    w_second = gather(unpack_columns(plan, second, False)[0], "dp")[:, : plan.used]
    scales = second[:, :2, plan.used :]
    standard, inverse = layer.standardize()
    normed, gain = layer.norm(standard, gather(scales, "dp"))
    normed, cot = gather(normed, "ctx"), gather(layer.cot, "ctx")
    total = dot(normed, w_first)
    hidden, factors = swiglu(plan, total[:, plan.joined :])
    empty = jnp.zeros((normed.shape[0], width), BF)
    rotated, attn, lse = layer.attend(total[:, : plan.joined], empty, layer.tables)
    wide = jnp.concatenate([attn, *hidden], axis=1)
    branches = scatter(dot_last(wide, w_second).astype(BF), "ctx")
    total = dot(cot, w_second)
    body = total[:, width : width + plan.body]
    tail = total[:, width + plan.body :]
    d_both = jnp.concatenate([body, body, tail, tail], axis=1) * jnp.concatenate(factors, axis=1)
    d_attn = total[:, :width].astype(BF)
    d_joined = layer.attend_back(rotated, attn, d_attn, lse, layer.tables)
    d_first = jnp.concatenate([d_joined, d_both.astype(BF)], axis=1)
    d_normed = scatter(dot_last(d_first, w_first).astype(BF), "ctx")
    sums = [scatter(dot_first(*v).astype(BF), "dp") for v in ((normed, d_first), (cot, wide))]
    begins = (0, plan.joined, plan.first)
    grads = unpack_rows(plan, swap(pack_rows(own, n, sums)), [0, 1, 2, 3, 4], begins)
    input_grad, norm_sums = layer.norm_back(d_normed, standard, inverse, gain)
    return layer.finish_output(branches), input_grad, scatter(norm_sums, ("dp", "ctx")), grads


def swaps(bit, n):
    return [(i, i ^ bit) for i in range(n)]


class State:
    def __init__(self, **arrays):
        self.held = arrays

    def __getitem__(self, name):
        return self.held[name]

    def drop(self, *names):
        for name in names:
            del self.held[name]

    def tick(self, before=(), sends=(), work=()):
        for action in before:
            self.held.update(action(self.held))
        view = dict(self.held)
        for name, source, axis, pairs in sends:
            view[name] = lax.ppermute(self.held[source], axis, pairs)
        for action in work:
            view.update(action(view))
        names = list(view)
        held = lax.optimization_barrier([view[name] for name in names])
        self.held = dict(zip(names, held))


def on_grid(layer, weights, scales):
    plan = layer.plan
    n, own, features = plan.n, plan.own, layer.features
    ctx, dp = lax.axis_index("ctx"), lax.axis_index("dp")
    z = ctx // 2
    inner = (z == 1) | (z == 2)
    quarter = features // 4
    side, pair = ("ctx", swaps(1, n)), ("ctx", swaps(2, n))
    middle = ("ctx", [(2, 4), (3, 5), (4, 2), (5, 3)])
    outward = ("ctx", [(2, 0), (3, 1), (4, 6), (5, 7)])
    inward = ("ctx", [(b, a) for a, b in outward[1]])
    core, across = ("dp", swaps(1, 4)), ("dp", swaps(2, 4))

    def blocks_of(v, first, steps):
        blocks = [
            lax.dynamic_slice_in_dim(v, (first ^ step) * quarter, quarter, 1) for step in steps
        ]
        return jnp.concatenate(blocks, axis=1)

    def reorder(v):
        return blocks_of(v, dp, (0, 2, 1, 3))

    def unorder(v):
        return blocks_of(v, (dp % 2) * 2 + dp // 2, (0, 2, 1, 3))

    opened = {}

    def doubled(held, axis, bit, size):
        mine = lax.axis_index(axis) // bit % 2
        got = lax.ppermute(held, axis, swaps(bit, size))
        first, second = jnp.where(mine == 0, held, got), jnp.where(mine == 0, got, held)
        return jnp.concatenate([first, second], axis=0)

    def begin(s):
        held = scales.reshape(1, 2, own)
        for bit in (1, 2, 4):
            held = doubled(held, "ctx", bit, n)
        packed, second = pack_columns(plan, weights, scales)
        packed, held, c0 = lax.optimization_barrier((packed, held, s["c0"]))
        packed = lax.all_to_all(packed, "ctx", split_axis=0, concat_axis=0, tiled=True)
        made = {"c0x": lax.ppermute(c0, *side), "c1": lax.ppermute(c0, *pair)}
        for bit in (1, 2):
            held = doubled(held, "dp", bit, 4)
        normed, gain = layer.norm(standard, held)
        n0 = reorder(normed)
        made |= {"n0": n0, "gain": gain, "n0x": lax.ppermute(n0, *side)}
        made |= {"n1": lax.ppermute(n0, *pair), "n2i": lax.ppermute(n0, *middle)}
        parts = unpack_columns(plan, packed, True)
        return made | {"second": second} | dict(zip(("a0", "b0", "ab0"), parts))

    def second_in(s):
        opened["second"] = lax.all_to_all(
            s["second"], "ctx", split_axis=0, concat_axis=0, tiled=True
        )
        return {}

    def select(name):
        return lambda s: {name: jnp.where(inner, s[name + "i"], s[name + "o"])}

    def plus(name, *parts):
        return lambda s: {name: sum(s[part].astype(F32) for part in parts).astype(BF)}

    def pieces(s, name):
        names = "a0 b0 a2 b2 ab1 a3 b3" if name == "ab" else "w0 w2 w1 w3"
        return [s[key] for key in names.split()]

    def slots(s, letter):
        return [s.get(letter + i) for i in ("0", "0x", "1", "1x", "2", "2x", "3", "3x")]

    def streamed(name, letter, weight, names, finish, widths, extra, places):
        def work(s):
            done = [s[key] for key in names] if places[0] else []
            held = (slots(s, letter), places, pieces(s, weight), [s[key] for key in extra])
            made = stream(name, *held, functools.partial(finish, plan), widths, done)
            return dict(zip(names, made))

        return work

    def project(*places):
        names = ("n", "joined", "factors", "wide")
        widths = [(plan.joined, F32), (2 * plan.units, BF), (plan.second, BF)]
        return streamed("project", "n", "ab", names, project_finish, widths, [], places)

    def bring_back(*places):
        names = ("c", "d_attn", "d_both")
        widths = [(plan.width, BF), (2 * plan.units, BF)]
        held = ("factors",)
        return streamed("bring_back", "c", "w", names, return_finish, widths, held, places)

    def tables(s):
        return {"tables": layer.tables}

    def attend(s):
        made = layer.attend(s["joined"], s["wide"], s["tables"])
        return dict(zip(("rotated", "wide", "lse"), made))

    def attend_back(s):
        d_joined = layer.attend_back(
            s["rotated"], s["wide"], s["d_attn"], s["lse"], s["tables"]
        )
        return {"d_joined": d_joined}

    def scattered(name, letter, lefts, weight, places):
        def work(s):
            size = s["c0"].shape[0]
            made = spread(name, [s[v] for v in lefts], pieces(s, weight), places, size)
            keys = [f"{letter}{place}{kind}" for place in places for kind in "ka"]
            return dict(zip(keys, made))

        return work

    def output_part(*places):
        return scattered("output_part", "o", ["wide"], "w", places)

    def normed_part(*places):
        return scattered("normed_part", "d", ["d_joined", "d_both"], "ab", places)

    factors = {"J": ("n", "d_joined"), "G": ("n", "d_both"), "W": ("c", "wide")}

    def product(s, name, begin, end):
        left, right = factors[name]
        return dot_first(s[left][:, begin * quarter : end * quarter], s[right])

    def grad_a(name):
        return lambda s: {name + "A": product(s, name, 2, 4).astype(BF)}

    def grad_b(name):
        def work(s):
            total = product(s, name, 1, 2) + s[name + "Ar"][quarter:].astype(F32)
            return {name + "B": total.astype(BF)}

        return work

    def grad_c(name):
        def work(s):
            total = product(s, name, 0, 1) + s[name + "Ar"][:quarter].astype(F32)
            return {name + "C": (total + s[name + "Br"].astype(F32)).astype(BF)}

        return work

    def to(name, source, way):
        return (name, source, *way)

    def cross(name):
        return lambda s: {name + "Ar": lax.ppermute(s[name + "A"], *core)}

    def send_a(name):
        return to(name + "Ar", name + "A", core)

    def send_b(name):
        return to(name + "Br", name + "B", across)

    def packed_rows(*names):
        return lambda s: {names: pack_rows(own, n, [s[name + "C"] for name in names])}

    def swap_packed(*names):
        def work(s):
            opened[names] = lax.all_to_all(
                s[names], "ctx", split_axis=0, concat_axis=0, tiled=True
            )
            return {}

        return work

    def norm_back(s):
        input_grad, sums = layer.norm_back(unorder(s["d"]), standard, inverse, s["gain"])

        def halved(sums, dim, axis, bit, size):
            mine = lax.axis_index(axis) // bit % 2
            first, second = jnp.split(sums, 2, axis=dim)
            give = jnp.where(mine == 0, second, first)
            return jnp.where(mine == 0, first, second) + lax.ppermute(give, axis, swaps(bit, size))

        sums = sums.reshape(4, n, 2 * own)
        for bit in (4, 2, 1):
            sums = halved(sums, 1, "ctx", bit, n)
        names = ("J", "W")
        packed, sums = lax.optimization_barrier((s[names], sums))
        opened[names] = lax.all_to_all(packed, "ctx", split_axis=0, concat_axis=0, tiled=True)
        for bit in (2, 1):
            sums = halved(sums, 0, "dp", bit, 4)
        return {"input_grad": input_grad, "norm_sums": sums[0]}

    def y(name):
        return to(name + "2", name + "0", across)

    def near(name):
        return to(name + "1", name + "0", core)

    def far(name):
        return to(name + "3", name + "2", core)

    standard, inverse = layer.standardize()
    st = State(c0=reorder(layer.cot))
    tick = st.tick
    tick((), (), [begin])
    tick(
        (),
        [
            to("n1x", "n1", side),
            to("n3i", "n1", middle),
            to("n2o", "n2i", outward),
            y("a"),
            near("ab"),
        ],
        [second_in, tables],
    )
    tick(
        [select("n2")],
        [
            to("n2x", "n2", side),
            to("n3o", "n3i", outward),
            to("c2i", "c0", middle),
            y("b"),
            far("a"),
        ],
    )
    tick(
        [select("n3")],
        [
            to("n3x", "n3", side),
            to("c2o", "c2i", outward),
            to("c3i", "c1", middle),
            far("b"),
        ],
        [project(0, 1)],
    )
    tick(
        [select("c2"), lambda s: {"w0": unpack_columns(plan, opened["second"], False)[0]}],
        [to("c2x", "c2", side), to("c3o", "c3i", outward), y("w"), near("w")],
        [project(2, 3)],
    )
    tick(
        [select("c3")],
        [to("c3x", "c3", side), to("c1x", "c0x", pair), far("w")],
        [attend, output_part(0, 1, 2, 3)],
    )
    tick(
        (),
        [to("o3x", "o3a", side), to("o1p", "o1a", pair)],
        [bring_back(0, 1, 2, 3), grad_a("G")],
    )
    tick(
        [plus("o3", "o3k", "o3x")],
        [to("o2x", "o2a", side), to("o3i", "o3", inward), send_a("G")],
        [attend_back, grad_b("G")],
    )
    tick(
        [plus("o2", "o2k", "o2x"), plus("o3", "o3", "o3i"), plus("o0a", "o0a", "o1p")],
        [to("o0x", "o0a", side), to("o2i", "o2", inward), to("o3m", "o3", middle), send_b("G")],
        [normed_part(1, 3)],
    )
    tick(
        [plus("o2", "o2", "o2i"), plus("o1", "o1k", "o3m")],
        [to("d3x", "d3a", side), to("o2m", "o2", middle), to("o1r", "o1", pair)],
        [normed_part(0, 2), grad_c("G"), packed_rows("G")],
    )
    tick(
        [plus("d3", "d3k", "d3x")],
        [to("d2x", "d2a", side), to("d3i", "d3", inward)],
        [
            swap_packed("G"),
            grad_a("J"),
            cross("J"),
            grad_b("J"),
            grad_a("W"),
            plus("o", "o0k", "o0x", "o2m", "o1r"),
        ],
    )
    tick(
        [plus("d2", "d2k", "d2x"), plus("d3", "d3", "d3i")],
        [
            to("d1x", "d1a", side),
            to("d2i", "d2", inward),
            to("d3m", "d3", middle),
            send_b("J"),
            send_a("W"),
        ],
        [grad_b("W"), grad_c("J")],
    )
    tick(
        [plus("d2", "d2", "d2i"), plus("d1", "d1k", "d1x", "d3m")],
        [to("d0x", "d0a", side), to("d2m", "d2", middle), to("d1r", "d1", pair), send_b("W")],
        [grad_c("W"), packed_rows("J", "W")],
    )
    tick([plus("d", "d0k", "d0x", "d2m", "d1r")], (), [norm_back])
    gate_grad, up_grad = unpack_rows(plan, opened["G",], [2, 3], (0, 0, 0))
    begins = (0, 0, plan.joined)
    joined_grad, out_grad, down_grad = unpack_rows(plan, opened["J", "W"], [0, 1, 4], begins)
    grads = [joined_grad, out_grad, gate_grad, up_grad, down_grad]
    return layer.finish_output(unorder(st["o"])), st["input_grad"], st["norm_sums"], grads


def on_device(
    n_ctx,
    n_dp,
    inputs,
    norm_gain,
    norm_bias,
    joined_weight,
    gate_weight,
    up_weight,
    out_weight,
    down_weight,
    cotangent,
    lengths,
):
    grid = (n_ctx, n_dp) == (8, 4)
    if grid:
        ctx = lax.axis_index("ctx")
        z, x = ctx // 2, ctx % 2
        high = z >= 2
        order = [z, z ^ 1, jnp.where(high, 1, 2), jnp.where(high, 0, 3)]
        natural = [2 * o + (x ^ r) for o in order for r in range(2)]
        slots = jnp.zeros((n_ctx,), jnp.int32)
        for slot, part in enumerate(natural):
            slots = jnp.where(jnp.arange(n_ctx) == part, slot, slots)
    else:
        slots = jnp.arange(n_ctx, dtype=jnp.int32)
    units = gate_weight.shape[1] // n_ctx
    layer = Layer(n_ctx, slots, inputs, norm_gain, cotangent, lengths, units)
    weights = (joined_weight, out_weight, gate_weight, up_weight, down_weight)
    scales = jnp.concatenate([norm_gain, norm_bias])
    run = on_grid if grid else on_any_mesh
    output, input_grad, norm_sums, grads = run(layer, weights, scales)
    joined_grad, out_grad, gate_grad, up_grad, down_grad = grads
    return (
        output.reshape(inputs.shape),
        input_grad.reshape(inputs.shape),
        norm_sums[0, : layer.own],
        norm_sums[0, layer.own :],
        joined_grad,
        gate_grad,
        up_grad,
        out_grad,
        down_grad,
    )


def solution(mesh):
    rows = P(("dp", "ctx"), None)
    vector = P(("dp", "ctx"))
    tokens = P("dp", "ctx", None)
    return jax.shard_map(
        functools.partial(on_device, mesh.shape["ctx"], mesh.shape["dp"]),
        mesh=mesh,
        in_specs=(tokens, vector, vector, rows, rows, rows, rows, rows, tokens, P("dp")),
        out_specs=(tokens, tokens, vector, vector, rows, rows, rows, rows, rows),
        check_vma=False,
    )
```

```python
import functools

import jax
import jax.numpy as jnp
from jax import lax
from jax.experimental import pallas as pl
from jax.experimental.pallas import tpu as pltpu
from jax.sharding import PartitionSpec as P

HD = 64
ROT = 16
ATTEND_ROWS = 512
EPSILON = 1e-05
THETA = 10000.0
NEGATIVE = -1e30
BF = jnp.bfloat16
F32 = jnp.float32
LAST = (((1,), (1,)), ((), ()))
FIRST = (((0,), (0,)), ((), ()))


def dot(left, right):
    return jnp.dot(left, right, preferred_element_type=F32)


def dot_last(left, right):
    return lax.dot_general(left, right, LAST, preferred_element_type=F32)


def dot_first(left, right):
    return lax.dot_general(left, right, FIRST, preferred_element_type=F32)


def rotary_tables(length, width):
    half = ROT // 2
    lane = jnp.arange(width, dtype=jnp.int32) % HD
    frequency = THETA ** (-(2.0 * (lane % half).astype(F32)) / ROT)
    angles = jnp.arange(length, dtype=jnp.int32).astype(F32)[:, None] * frequency[None, :]
    cosine = jnp.where(lane[None, :] < ROT, jnp.cos(angles), 1.0)
    sine = jnp.sin(angles)
    sine = jnp.where(lane[None, :] < half, -sine, jnp.where(lane[None, :] < ROT, sine, 0.0))
    return cosine, sine


def partner(x):
    half = ROT // 2
    lane = lax.broadcasted_iota(jnp.int32, x.shape, 1) % HD
    down = jnp.concatenate([x[:, half:], x[:, :half]], axis=1)
    up = jnp.concatenate([x[:, -half:], x[:, :-half]], axis=1)
    return jnp.where(lane < half, down, up)


def attend_forward(
    length_ref, slot_ref, joined_ref, cos_ref, sin_ref, wide_ref, rot_ref, attn_ref, lse_ref
):
    parts, _, rows, triple = joined_ref.shape
    width = triple // 3
    length = parts * rows
    alive_count = length_ref[pl.program_id(0)]
    per = max(1, min(ATTEND_ROWS, length) // rows)
    block = per * rows
    for part in range(parts):
        slot = slot_ref[part]
        here = slice(part * rows, (part + 1) * rows)

        def rotated(start):
            x = joined_ref[slot, 0, :, start : start + width]
            return (x * cos_ref[here, :] + partner(x) * sin_ref[here, :]).astype(BF)

        rot_ref[part, 0, :, :width] = rotated(0) * 0.125
        rot_ref[part, 0, :, width : 2 * width] = rotated(width)
        rot_ref[part, 0, :, 2 * width :] = joined_ref[slot, 0, :, 2 * width :].astype(BF)
    lse_ref[...] = jnp.zeros_like(lse_ref)
    heads = width // HD
    for step in range(length // block):
        begin, end = step * per, (step + 1) * per
        stop = end * rows
        slots = [slot_ref[part] for part in range(begin, end)]

        @pl.when(begin * rows >= alive_count)
        def _(slots=slots):
            for slot in slots:
                attn_ref[slot, 0] = jnp.zeros((rows, width), BF)

        @pl.when(begin * rows < alive_count)
        def _(begin=begin, end=end, stop=stop, slots=slots):
            q_pos = begin * rows + lax.broadcasted_iota(jnp.int32, (block, 1), 0)
            k_pos = lax.broadcasted_iota(jnp.int32, (block, stop), 1)
            allowed = k_pos <= q_pos
            alive = q_pos < alive_count
            for head in range(heads):
                lane = head * HD
                q = rot_ref[begin:end, 0, :, lane : lane + HD].reshape(block, HD)
                lane += width
                k = rot_ref[:end, 0, :, lane : lane + HD].reshape(stop, HD)
                lane += width
                v = rot_ref[:end, 0, :, lane : lane + HD].reshape(stop, HD)
                scores = jnp.where(allowed, dot_last(q, k), NEGATIVE)
                top = jnp.max(scores, axis=1, keepdims=True)
                expo = jnp.exp(scores - top)
                weight = jnp.sum(expo, axis=1, keepdims=True)
                out = jnp.where(alive, dot(expo.astype(BF), v) / weight, 0.0).astype(BF)
                for index, slot in enumerate(slots):
                    there = slice(index * rows, (index + 1) * rows)
                    attn_ref[slot, 0, :, head * HD : (head + 1) * HD] = out[there, :]
                lse = jnp.where(alive, top + jnp.log(weight), 0.0)
                lse_ref[begin:end, 0, :, head : head + 1] = lse.reshape(per, rows, 1)


def attend_backward(
    length_ref, slot_ref, rot_ref, attn_ref, grad_ref, lse_ref, cos_ref, sin_ref, out_ref, dq, dk, dv
):
    parts, _, rows, triple = rot_ref.shape
    width = triple // 3
    length = parts * rows
    seq = pl.program_id(0)
    head = pl.program_id(1)
    alive_count = length_ref[seq]
    per = max(1, min(ATTEND_ROWS, length) // rows)
    block = per * rows
    lane = lax.broadcasted_iota(jnp.int32, (1, width), 1)
    mine = (lane // HD) == head

    @pl.when(head == 0)
    def _():
        dq[...] = jnp.zeros_like(dq)
        dk[...] = jnp.zeros_like(dk)
        dv[...] = jnp.zeros_like(dv)

    for step in range(length // block):
        begin, end = step * per, (step + 1) * per
        stop = end * rows

        @pl.when(begin * rows < alive_count)
        def _(begin=begin, end=end, stop=stop):
            q_pos = begin * rows + lax.broadcasted_iota(jnp.int32, (block, 1), 0)
            alive = q_pos < alive_count
            q = rot_ref[begin:end, 0, :, :width].reshape(block, width)
            q = jnp.where(mine, q, jnp.zeros_like(q))
            k = rot_ref[:end, 0, :, width : 2 * width].reshape(stop, width)
            v = rot_ref[:end, 0, :, 2 * width :].reshape(stop, width)
            slots = [slot_ref[part] for part in range(begin, end)]
            g = jnp.concatenate([grad_ref[slot, 0] for slot in slots], axis=0)
            g = jnp.where(mine & alive, g, jnp.zeros_like(g))
            o = jnp.concatenate([attn_ref[slot, 0] for slot in slots], axis=0)
            delta = jnp.sum(g.astype(F32) * o.astype(F32), axis=1, keepdims=True)
            held = lse_ref[begin:end, 0].reshape(block, lse_ref.shape[3])
            spot = lax.broadcasted_iota(jnp.int32, (1, lse_ref.shape[3]), 1) == head
            lse = jnp.sum(jnp.where(spot, held, 0.0), axis=1, keepdims=True)
            scores = dot_last(q, k)
            k_pos = lax.broadcasted_iota(jnp.int32, (block, stop), 1)
            probs = jnp.where((k_pos <= q_pos) & alive, jnp.exp(scores - lse), 0.0)
            d_probs = dot_last(g, v)
            d_scores = (probs * (d_probs - delta)).astype(BF)
            here = slice(begin * rows, stop)
            dq[here, :] += jnp.where(mine, dot(d_scores, k), 0.0)
            dk[:stop, :] += dot_first(d_scores, q)
            dv[:stop, :] += dot_first(probs.astype(BF), g)

    @pl.when(head == pl.num_programs(1) - 1)
    def _():
        for part in range(parts):
            slot = slot_ref[part]
            here = slice(part * rows, (part + 1) * rows)

            def unrotated(x):
                return (x * cos_ref[here, :] - partner(x) * sin_ref[here, :]).astype(BF)

            out_ref[slot, 0, :, :width] = unrotated(dq[here, :] * 0.125)
            out_ref[slot, 0, :, width : 2 * width] = unrotated(dk[here, :])
            out_ref[slot, 0, :, 2 * width :] = dv[here, :].astype(BF)


def attention_calls(parts, groups, rows, width, heads, lanes):
    length = parts * rows
    smem = pl.BlockSpec(memory_space=pltpu.SMEM)

    def spec(last):
        return pl.BlockSpec((parts, 1, rows, last), lambda s, *_: (0, s, 0, 0))

    table = pl.BlockSpec((length, width), lambda *_: (0, 0))

    def shape(last, dtype):
        return jax.ShapeDtypeStruct((parts, groups, rows, last), dtype)

    pairs = groups * heads * length * length // 2
    params = pltpu.CompilerParams(vmem_limit_bytes=48 * 1024 * 1024)
    forward = pl.pallas_call(
        attend_forward,
        grid=(groups,),
        in_specs=[smem, smem, spec(3 * width), table, table, pl.BlockSpec(memory_space=pl.ANY)],
        out_specs=[spec(3 * width), spec(width), spec(heads)],
        out_shape=[shape(3 * width, BF), shape(lanes, BF), shape(heads, F32)],
        input_output_aliases={5: 1},
        compiler_params=params,
        cost_estimate=pl.CostEstimate(
            flops=pairs * 1024, bytes_accessed=16 * length * width, transcendentals=pairs
        ),
        name="attend_forward",
    )
    backward = pl.pallas_call(
        attend_backward,
        grid=(groups, heads),
        in_specs=[smem, smem, spec(3 * width), spec(width), spec(width), spec(heads), table, table],
        out_specs=spec(3 * width),
        out_shape=shape(3 * width, BF),
        scratch_shapes=[pltpu.VMEM((length, width), F32)] * 3,
        compiler_params=params,
        cost_estimate=pl.CostEstimate(
            flops=pairs * 2560, bytes_accessed=16 * length * width, transcendentals=pairs
        ),
        name="attend_backward",
    )
    return forward, backward


class Plan:
    def __init__(self, n, own, width, units):
        self.n, self.own, self.width, self.units = n, own, width, units
        self.body = units // 128 * 128
        self.tail = units - self.body
        self.joined = 3 * width
        self.first = self.joined + 2 * units
        self.used = width + units
        self.second = self.used + own
        spans = [(0, r * n * width, width, width) for r in range(3)]
        for start, span in ((0, self.body), (self.body, self.tail)):
            spans += [(w, start, units, span) for w in (2, 3)]
        self.spans = [*spans, (1, 0, width, width), (4, 0, units, units)]

    def segments(self):
        lane = 0
        for weight, start, stride, span in self.spans:
            yield weight, start, stride, lane, span
            lane += span


def pack_kernel(plan, chosen, *refs):
    scale_ref, sources, out_ref = refs[0], dict(zip(chosen, refs[1:-1])), refs[-1]
    lane = 0
    for weight, start, stride, _, span in plan.segments():
        if weight in chosen:
            for dest in range(plan.n):
                begin = start + dest * stride
                out_ref[dest, :, lane : lane + span] = sources[weight][:, begin : begin + span]
            lane += span
    if lane < out_ref.shape[2]:
        for dest in range(plan.n):
            out_ref[dest, :, lane:] = scale_ref[...]


def unpack_kernel(own, outs_of, in_ref, *outs):
    for out, (source, sources, lane, lanes) in zip(outs, outs_of):
        for index in range(sources):
            block = in_ref[source + index, :, lane : lane + lanes]
            out[index * own : (index + 1) * own, :] = block


def pack_rows_kernel(own, *refs):
    sources, out = refs[:-1], refs[-1]
    for dest in range(out.shape[0]):
        lane = 0
        for source in sources:
            lanes = source.shape[1]
            out[dest, :, lane : lane + lanes] = source[dest * own : (dest + 1) * own, :]
            lane += lanes


def unpack_rows_kernel(n, layout, held, *outs):
    for source in range(n):
        for out, start, stride, lane, span in layout:
            begin = start + source * stride
            block = held[source, :, lane : lane + span].astype(F32)
            outs[out][:, begin : begin + span] = block


def in_vmem(kernel, name, out_shape):
    def call(*operands):
        place = pl.BlockSpec(memory_space=pltpu.VMEM)
        moved = sum(o.size * o.dtype.itemsize for o in operands)
        return pl.pallas_call(
            kernel,
            in_specs=[place] * len(operands),
            out_specs=jax.tree.map(lambda _: place, out_shape),
            out_shape=out_shape,
            compiler_params=pltpu.CompilerParams(vmem_limit_bytes=48 * 1024 * 1024),
            cost_estimate=pl.CostEstimate(flops=0, bytes_accessed=3 * moved, transcendentals=0),
            name=name,
        )(*operands)

    return call


def pack_columns(plan, weights, scales):
    scales = jnp.pad(scales.reshape(2, plan.own), ((0, plan.own - 2), (0, 0)))
    packed = []
    for chosen, lanes in (((0, 2, 3), plan.first), ((1, 4), plan.second)):
        shape = jax.ShapeDtypeStruct((plan.n, plan.own, lanes), BF)
        kernel = functools.partial(pack_kernel, plan, chosen)
        packed.append(in_vmem(kernel, "pack_columns", shape)(scales, *[weights[w] for w in chosen]))
    return packed


def unpack_columns(plan, packed, parts):
    n, own, lanes = packed.shape
    outs_of = [(half * n // 2, n // 2, 0, lanes) for half in range(2)] if parts else []
    outs_of.append((0, n, 0, lanes))
    shapes = [jax.ShapeDtypeStruct((c * own, lanes), BF) for _, c, _, lanes in outs_of]
    kernel = functools.partial(unpack_kernel, own, outs_of)
    return in_vmem(kernel, "unpack_columns", shapes)(packed)


def pack_rows(own, n, gradients):
    lanes = sum(g.shape[1] for g in gradients)
    shape = jax.ShapeDtypeStruct((n, own, lanes), BF)
    return in_vmem(functools.partial(pack_rows_kernel, own), "pack_rows", shape)(*gradients)


def unpack_rows(plan, packed, chosen, begins):
    layout = []
    for weight, start, stride, lane, span in plan.segments():
        if weight in chosen:
            group = 0 if weight == 0 else 1 if weight in (2, 3) else 2
            lane += begins[group] - (0, plan.joined, plan.first)[group]
            layout.append((chosen.index(weight), start, stride, lane, span))
    widths = [3 * plan.width, plan.width, plan.units, plan.units, plan.units]
    shapes = [jax.ShapeDtypeStruct((plan.own, plan.n * widths[w]), F32) for w in chosen]
    kernel = functools.partial(unpack_rows_kernel, plan.n, layout)
    return in_vmem(kernel, "unpack_rows", shapes)(packed)


def fetch_pieces(pieces, held, sems):
    copies, row = [], 0
    for i, piece in enumerate(pieces):
        there = held.at[pl.ds(row, piece.shape[0]), :]
        copies.append(pltpu.make_async_copy(piece, there, sems.at[i]))
        row += piece.shape[0]
    return copies


def stream_kernel(n, n_pieces, n_extra, n_into, finish, *refs):
    blocks, refs = refs[:n], refs[n:]
    pieces, refs = refs[:n_pieces], refs[n_pieces + n_into :]
    extra, outs, (held, rows_ref, rows_sem, weight_sem) = refs[:n_extra], refs[n_extra:-4], refs[-4:]
    size = blocks[0].shape[0]
    step = pl.program_id(0)
    steps = n // 2
    weight = fetch_pieces(pieces, held, weight_sem)

    def copy(block, buffer, half):
        there = rows_ref.at[buffer, pl.ds(half * size, size), :]
        return pltpu.make_async_copy(block, there, rows_sem.at[buffer, half])

    def fetch(index):
        for place in range(steps):

            @pl.when(index == place)
            def _(place=place):
                for half in range(2):
                    copy(blocks[2 * place + half], place % 2, half).start()

    @pl.when(step == 0)
    def _():
        fetch(0)
        for piece in weight:
            piece.start()

    @pl.when(step + 1 < steps)
    def _():
        fetch(step + 1)

    buffer = lax.rem(step, 2)
    for half in range(2):
        copy(blocks[half], buffer, half).wait()

    @pl.when(step == 0)
    def _():
        for piece in weight:
            piece.wait()

    finish(rows_ref[buffer], held, extra, outs)


def stream(name, slots, places, pieces, extra, finish, outs, into):
    size, features = slots[0].shape
    blocks = [slots[2 * place + half] for place in places for half in range(2)]
    n = len(blocks)
    first, stride = places[0], places[1] - places[0]
    anywhere = pl.BlockSpec(memory_space=pl.ANY)

    def rows(width):
        return pl.BlockSpec((2 * size, width), lambda i: (first + stride * i, 0))

    outs = [(features, BF), *outs]
    width = pieces[0].shape[1]
    begin = n + len(pieces)
    return pl.pallas_call(
        functools.partial(stream_kernel, n, len(pieces), len(extra), len(into), finish),
        grid=(n // 2,),
        in_specs=[anywhere] * (begin + len(into)) + [rows(e.shape[1]) for e in extra],
        out_specs=[rows(w) for w, _ in outs],
        out_shape=[jax.ShapeDtypeStruct((len(slots) * size, w), dtype) for w, dtype in outs],
        input_output_aliases={begin + i: i for i in range(len(into))},
        scratch_shapes=[
            pltpu.VMEM((features, width), BF),
            pltpu.VMEM((2, 2 * size, features), BF),
            pltpu.SemaphoreType.DMA((2, 2)),
            pltpu.SemaphoreType.DMA((len(pieces),)),
        ],
        compiler_params=pltpu.CompilerParams(vmem_limit_bytes=52 * 1024 * 1024),
        cost_estimate=pl.CostEstimate(
            flops=2 * n * size * features * width,
            bytes_accessed=2 * (n * size + width) * features * 2,
            transcendentals=0,
        ),
        name=name,
    )(*blocks, *pieces, *into, *extra)


def swiglu(plan, both):
    body, tail = plan.body, plan.tail
    hidden, factors = [], []
    for start, span in ((0, body), (2 * body, tail)):
        gate, up = both[:, start : start + span], both[:, start + span : start + 2 * span]
        sigmoid = jax.nn.sigmoid(gate)
        silu = gate * sigmoid
        hidden.append((silu * up).astype(BF))
        factors += [up * sigmoid * (1.0 + gate * (1.0 - sigmoid)), silu]
    return hidden, factors


def project_finish(plan, rows, held, extra, outs):
    normed, joined, factor_ref, wide = outs
    normed[...] = rows
    joined[...] = dot(rows, held[:, : plan.joined])
    hidden, factors = swiglu(plan, dot(rows, held[:, plan.joined :]))
    lane = 0
    for factor in factors:
        factor_ref[:, lane : lane + factor.shape[1]] = factor.astype(factor_ref.dtype)
        lane += factor.shape[1]
    wide[:, : plan.width] = jnp.zeros((rows.shape[0], plan.width), BF)
    wide[:, plan.width : plan.width + plan.body] = hidden[0]
    pad = jnp.zeros((rows.shape[0], plan.second - plan.used), BF)
    wide[:, plan.width + plan.body :] = jnp.concatenate([hidden[1], pad], axis=1)


def return_finish(plan, rows, held, extra, outs):
    (factor_ref,), (cot, d_attn, d_both) = extra, outs
    cot[...] = rows
    total = dot(rows, held[...])
    d_attn[...] = total[:, : plan.width].astype(BF)
    begin, body, tail = plan.width, plan.body, plan.tail
    for lane, start, span in (
        (0, begin, body),
        (body, begin, body),
        (2 * body, begin + body, tail),
        (2 * body + tail, begin + body, tail),
    ):
        here = slice(lane, lane + span)
        d_both[:, here] = (total[:, start : start + span] * factor_ref[:, here]).astype(BF)


def spread_kernel(count, n_pieces, places, *refs):
    lefts, refs = refs[: count * places], refs[count * places :]
    pieces, outs, (held, sems) = refs[:n_pieces], refs[n_pieces:-2], refs[-2:]
    weight = fetch_pieces(pieces, held, sems)
    for piece in weight:
        piece.start()
    size = outs[0].shape[0]
    rows = held.shape[0] // 4
    begins = [sum(p.shape[0] for p in pieces[:i]) for i in range(n_pieces)]
    for part in range(4):
        here = slice(part * rows, (part + 1) * rows)
        for begin, piece in zip(begins, weight):
            if begin // rows == part:
                piece.wait()
        for place in range(places):
            total, lane = 0.0, 0
            for left in lefts[place * count : (place + 1) * count]:
                lanes = left.shape[1]
                total += dot_last(left[...], held[here, lane : lane + lanes])
                lane += lanes
            outs[2 * place][:, here] = total[:size].astype(BF)
            outs[2 * place + 1][:, here] = total[size:].astype(BF)


def spread(name, lefts, pieces, places, size):
    anywhere = pl.BlockSpec(memory_space=pl.ANY)
    features = sum(piece.shape[0] for piece in pieces)
    width = pieces[0].shape[1]
    tokens = 2 * size * len(places)

    def rows(left, place):
        return pl.BlockSpec((2 * size, left.shape[1]), lambda i: (place, 0))

    blocks = 2 * len(places)
    return pl.pallas_call(
        functools.partial(spread_kernel, len(lefts), len(pieces), len(places)),
        grid=(1,),
        in_specs=[rows(left, place) for place in places for left in lefts]
        + [anywhere] * len(pieces),
        out_specs=[pl.BlockSpec((size, features), lambda i: (0, 0))] * blocks,
        out_shape=[jax.ShapeDtypeStruct((size, features), BF)] * blocks,
        scratch_shapes=[
            pltpu.VMEM((features, width), BF),
            pltpu.SemaphoreType.DMA((len(pieces),)),
        ],
        compiler_params=pltpu.CompilerParams(vmem_limit_bytes=52 * 1024 * 1024),
        cost_estimate=pl.CostEstimate(
            flops=2 * tokens * features * width,
            bytes_accessed=2 * (tokens + features) * width + 2 * tokens * features,
            transcendentals=0,
        ),
        name=name,
    )(*[left for _ in places for left in lefts], *pieces)


class Layer:
    def __init__(self, n_ctx, slots, inputs, norm_gain, cotangent, lengths, units):
        self.groups, self.rows, self.features = inputs.shape
        self.tokens = self.groups * self.rows
        self.n_ctx, self.slots, self.lengths = n_ctx, slots, lengths
        self.own = norm_gain.shape[0]
        self.width = self.features // n_ctx
        self.plan = Plan(n_ctx, self.own, self.width, units)
        self.flat = inputs.reshape(self.tokens, self.features).astype(F32)
        self.cot = cotangent.reshape(self.tokens, self.features)
        self.tables = rotary_tables(n_ctx * self.rows, self.width)
        self.blocks = (n_ctx, self.groups, self.rows)

    def calls(self, lanes):
        heads = self.width // HD
        return attention_calls(self.n_ctx, self.groups, self.rows, self.width, heads, lanes)

    def standardize(self):
        center = self.flat - jnp.mean(self.flat, axis=-1, keepdims=True)
        variance = jnp.mean(center * center, axis=-1, keepdims=True)
        inverse = lax.rsqrt(variance + EPSILON)
        return center * inverse, inverse

    def norm(self, standard, scales):
        gain, bias = self.scales(scales)
        return (standard * gain + bias).astype(BF), gain

    def scales(self, scales):
        return [scales[:, i].astype(F32).reshape(1, self.features) for i in range(2)]

    def attend(self, joined, wide, tables):
        lanes = wide.shape[1]
        shape = (*self.blocks, lanes)
        joined = joined.reshape(*self.blocks, 3 * self.width)
        rotated, wide, lse = self.calls(lanes)[0](
            self.lengths, self.slots, joined, *tables, wide.reshape(shape)
        )
        return rotated, wide.reshape(-1, lanes), lse

    def attend_back(self, rotated, wide, d_attn, lse, tables):
        lanes = wide.shape[1]
        return self.calls(lanes)[1](
            self.lengths,
            self.slots,
            rotated,
            wide.reshape(*self.blocks, lanes),
            d_attn.reshape(*self.blocks, self.width),
            lse,
            *tables,
        ).reshape(-1, 3 * self.width)

    def finish_output(self, branches):
        return (self.flat + branches.astype(F32)).astype(BF)

    def norm_back(self, d_normed, standard, inverse, gain):
        d_normed = d_normed.astype(F32)
        grad = d_normed * gain
        centered = (
            grad
            - jnp.mean(grad, axis=-1, keepdims=True)
            - standard * jnp.mean(grad * standard, axis=-1, keepdims=True)
        )
        sums = [jnp.sum(d_normed * standard, axis=0), jnp.sum(d_normed, axis=0)]
        sums = jnp.concatenate([v.reshape(-1, self.own) for v in sums], axis=1)
        return (self.cot.astype(F32) + inverse * centered).astype(BF), sums


def on_any_mesh(layer, weights, scales):
    plan = layer.plan
    n, own, width = plan.n, plan.own, plan.width

    def swap(pieces):
        return lax.all_to_all(pieces, "ctx", split_axis=0, concat_axis=0, tiled=True)

    def gather(v, axis):
        return lax.all_gather(v, axis, axis=0, tiled=True)

    def scatter(v, axis):
        return lax.psum_scatter(v, axis, scatter_dimension=0, tiled=True)

    first, second = (swap(packed) for packed in pack_columns(plan, weights, scales))
    w_first = gather(unpack_columns(plan, first, False)[0], "dp")
    w_second = gather(unpack_columns(plan, second, False)[0], "dp")[:, : plan.used]
    scales = second[:, :2, plan.used :]
    standard, inverse = layer.standardize()
    normed, gain = layer.norm(standard, gather(scales, "dp"))
    normed, cot = gather(normed, "ctx"), gather(layer.cot, "ctx")
    total = dot(normed, w_first)
    hidden, factors = swiglu(plan, total[:, plan.joined :])
    empty = jnp.zeros((normed.shape[0], width), BF)
    rotated, attn, lse = layer.attend(total[:, : plan.joined], empty, layer.tables)
    wide = jnp.concatenate([attn, *hidden], axis=1)
    branches = scatter(dot_last(wide, w_second).astype(BF), "ctx")
    total = dot(cot, w_second)
    body = total[:, width : width + plan.body]
    tail = total[:, width + plan.body :]
    d_both = jnp.concatenate([body, body, tail, tail], axis=1) * jnp.concatenate(factors, axis=1)
    d_attn = total[:, :width].astype(BF)
    d_joined = layer.attend_back(rotated, attn, d_attn, lse, layer.tables)
    d_first = jnp.concatenate([d_joined, d_both.astype(BF)], axis=1)
    d_normed = scatter(dot_last(d_first, w_first).astype(BF), "ctx")
    sums = [scatter(dot_first(*v).astype(BF), "dp") for v in ((normed, d_first), (cot, wide))]
    begins = (0, plan.joined, plan.first)
    grads = unpack_rows(plan, swap(pack_rows(own, n, sums)), [0, 1, 2, 3, 4], begins)
    input_grad, norm_sums = layer.norm_back(d_normed, standard, inverse, gain)
    return layer.finish_output(branches), input_grad, scatter(norm_sums, ("dp", "ctx")), grads


def swaps(bit, n):
    return [(i, i ^ bit) for i in range(n)]


class State:
    def __init__(self, **arrays):
        self.held = arrays

    def __getitem__(self, name):
        return self.held[name]

    def drop(self, *names):
        for name in names:
            del self.held[name]

    def tick(self, before=(), sends=(), work=()):
        for action in before:
            self.held.update(action(self.held))
        view = dict(self.held)
        for name, source, axis, pairs in sends:
            view[name] = lax.ppermute(self.held[source], axis, pairs)
        for action in work:
            view.update(action(view))
        names = list(view)
        held = lax.optimization_barrier([view[name] for name in names])
        self.held = dict(zip(names, held))


def on_grid(layer, weights, scales):
    plan = layer.plan
    n, own, features = plan.n, plan.own, layer.features
    ctx, dp = lax.axis_index("ctx"), lax.axis_index("dp")
    z = ctx // 2
    inner = (z == 1) | (z == 2)
    quarter = features // 4
    side, pair = ("ctx", swaps(1, n)), ("ctx", swaps(2, n))
    middle = ("ctx", [(2, 4), (3, 5), (4, 2), (5, 3)])
    outward = ("ctx", [(2, 0), (3, 1), (4, 6), (5, 7)])
    inward = ("ctx", [(b, a) for a, b in outward[1]])
    core, across = ("dp", swaps(1, 4)), ("dp", swaps(2, 4))

    def blocks_of(v, first, steps):
        blocks = [
            lax.dynamic_slice_in_dim(v, (first ^ step) * quarter, quarter, 1) for step in steps
        ]
        return jnp.concatenate(blocks, axis=1)

    def reorder(v):
        return blocks_of(v, dp, (0, 2, 1, 3))

    def unorder(v):
        return blocks_of(v, (dp % 2) * 2 + dp // 2, (0, 2, 1, 3))

    opened = {}

    def doubled(held, axis, bit, size):
        mine = lax.axis_index(axis) // bit % 2
        got = lax.ppermute(held, axis, swaps(bit, size))
        first, second = jnp.where(mine == 0, held, got), jnp.where(mine == 0, got, held)
        return jnp.concatenate([first, second], axis=0)

    def begin(s):
        held = scales.reshape(1, 2, own)
        for bit in (1, 2, 4):
            held = doubled(held, "ctx", bit, n)
        packed, second = pack_columns(plan, weights, scales)
        packed, held, c0 = lax.optimization_barrier((packed, held, s["c0"]))
        packed = lax.all_to_all(packed, "ctx", split_axis=0, concat_axis=0, tiled=True)
        made = {"c0x": lax.ppermute(c0, *side), "c1": lax.ppermute(c0, *pair)}
        for bit in (1, 2):
            held = doubled(held, "dp", bit, 4)
        normed, gain = layer.norm(standard, held)
        n0 = reorder(normed)
        made |= {"n0": n0, "gain": gain, "n0x": lax.ppermute(n0, *side)}
        made |= {"n1": lax.ppermute(n0, *pair), "n2i": lax.ppermute(n0, *middle)}
        parts = unpack_columns(plan, packed, True)
        return made | {"second": second} | dict(zip(("a0", "b0", "ab0"), parts))

    def second_in(s):
        opened["second"] = lax.all_to_all(
            s["second"], "ctx", split_axis=0, concat_axis=0, tiled=True
        )
        return {}

    def select(name):
        return lambda s: {name: jnp.where(inner, s[name + "i"], s[name + "o"])}

    def plus(name, *parts):
        return lambda s: {name: sum(s[part].astype(F32) for part in parts).astype(BF)}

    def pieces(s, name):
        names = "a0 b0 a2 b2 ab1 a3 b3" if name == "ab" else "w0 w2 w1 w3"
        return [s[key] for key in names.split()]

    def slots(s, letter):
        return [s.get(letter + i) for i in ("0", "0x", "1", "1x", "2", "2x", "3", "3x")]

    def streamed(name, letter, weight, names, finish, widths, extra, places):
        def work(s):
            done = [s[key] for key in names] if places[0] else []
            held = (slots(s, letter), places, pieces(s, weight), [s[key] for key in extra])
            made = stream(name, *held, functools.partial(finish, plan), widths, done)
            return dict(zip(names, made))

        return work

    def project(*places):
        names = ("n", "joined", "factors", "wide")
        widths = [(plan.joined, F32), (2 * plan.units, BF), (plan.second, BF)]
        return streamed("project", "n", "ab", names, project_finish, widths, [], places)

    def bring_back(*places):
        names = ("c", "d_attn", "d_both")
        widths = [(plan.width, BF), (2 * plan.units, BF)]
        held = ("factors",)
        return streamed("bring_back", "c", "w", names, return_finish, widths, held, places)

    def tables(s):
        return {"tables": layer.tables}

    def attend(s):
        made = layer.attend(s["joined"], s["wide"], s["tables"])
        return dict(zip(("rotated", "wide", "lse"), made))

    def attend_back(s):
        d_joined = layer.attend_back(
            s["rotated"], s["wide"], s["d_attn"], s["lse"], s["tables"]
        )
        return {"d_joined": d_joined}

    def scattered(name, letter, lefts, weight, places):
        def work(s):
            size = s["c0"].shape[0]
            made = spread(name, [s[v] for v in lefts], pieces(s, weight), places, size)
            keys = [f"{letter}{place}{kind}" for place in places for kind in "ka"]
            return dict(zip(keys, made))

        return work

    def output_part(*places):
        return scattered("output_part", "o", ["wide"], "w", places)

    def normed_part(*places):
        return scattered("normed_part", "d", ["d_joined", "d_both"], "ab", places)

    factors = {"J": ("n", "d_joined"), "G": ("n", "d_both"), "W": ("c", "wide")}

    def product(s, name, begin, end):
        left, right = factors[name]
        return dot_first(s[left][:, begin * quarter : end * quarter], s[right])

    def grad_a(name):
        return lambda s: {name + "A": product(s, name, 2, 4).astype(BF)}

    def grad_b(name):
        def work(s):
            total = product(s, name, 1, 2) + s[name + "Ar"][quarter:].astype(F32)
            return {name + "B": total.astype(BF)}

        return work

    def grad_c(name):
        def work(s):
            total = product(s, name, 0, 1) + s[name + "Ar"][:quarter].astype(F32)
            return {name + "C": (total + s[name + "Br"].astype(F32)).astype(BF)}

        return work

    def to(name, source, way):
        return (name, source, *way)

    def cross(name):
        return lambda s: {name + "Ar": lax.ppermute(s[name + "A"], *core)}

    def send_a(name):
        return to(name + "Ar", name + "A", core)

    def send_b(name):
        return to(name + "Br", name + "B", across)

    def packed_rows(*names):
        return lambda s: {names: pack_rows(own, n, [s[name + "C"] for name in names])}

    def swap_packed(*names):
        def work(s):
            opened[names] = lax.all_to_all(
                s[names], "ctx", split_axis=0, concat_axis=0, tiled=True
            )
            return {}

        return work

    def norm_back(s):
        input_grad, sums = layer.norm_back(unorder(s["d"]), standard, inverse, s["gain"])

        def halved(sums, dim, axis, bit, size):
            mine = lax.axis_index(axis) // bit % 2
            first, second = jnp.split(sums, 2, axis=dim)
            give = jnp.where(mine == 0, second, first)
            return jnp.where(mine == 0, first, second) + lax.ppermute(give, axis, swaps(bit, size))

        sums = sums.reshape(4, 2, 2, 2, 2 * own)
        for dim, bit in ((3, 1), (2, 2), (1, 4)):
            sums = halved(sums, dim, "ctx", bit, n)
        names = ("J", "W")
        packed, sums = lax.optimization_barrier((s[names], sums))
        opened[names] = lax.all_to_all(packed, "ctx", split_axis=0, concat_axis=0, tiled=True)
        sums = sums.reshape(4, 2 * own)
        for bit in (2, 1):
            sums = halved(sums, 0, "dp", bit, 4)
        return {"input_grad": input_grad, "norm_sums": sums}

    def y(name):
        return to(name + "2", name + "0", across)

    def near(name):
        return to(name + "1", name + "0", core)

    def far(name):
        return to(name + "3", name + "2", core)

    standard, inverse = layer.standardize()
    st = State(c0=reorder(layer.cot))
    tick = st.tick
    tick((), (), [begin])
    tick(
        (),
        [
            to("n1x", "n1", side),
            to("n3i", "n1", middle),
            to("n2o", "n2i", outward),
            y("a"),
            near("ab"),
        ],
        [second_in, tables],
    )
    tick(
        [select("n2")],
        [
            to("n2x", "n2", side),
            to("n3o", "n3i", outward),
            to("c2i", "c0", middle),
            y("b"),
            far("a"),
        ],
    )
    tick(
        [select("n3")],
        [
            to("n3x", "n3", side),
            to("c2o", "c2i", outward),
            to("c3i", "c1", middle),
            far("b"),
        ],
        [project(0, 1)],
    )
    tick(
        [select("c2"), lambda s: {"w0": unpack_columns(plan, opened["second"], False)[0]}],
        [to("c2x", "c2", side), to("c3o", "c3i", outward), y("w"), near("w")],
        [project(2, 3)],
    )
    tick(
        [select("c3")],
        [to("c3x", "c3", side), to("c1x", "c0x", pair), far("w")],
        [attend, output_part(0, 1, 2, 3)],
    )
    tick(
        (),
        [to("o3x", "o3a", side), to("o1p", "o1a", pair)],
        [bring_back(0, 1, 2, 3), grad_a("G")],
    )
    tick(
        [plus("o3", "o3k", "o3x")],
        [to("o2x", "o2a", side), to("o3i", "o3", inward), send_a("G")],
        [attend_back, grad_b("G")],
    )
    tick(
        [plus("o2", "o2k", "o2x"), plus("o3", "o3", "o3i"), plus("o0a", "o0a", "o1p")],
        [to("o0x", "o0a", side), to("o2i", "o2", inward), to("o3m", "o3", middle), send_b("G")],
        [normed_part(1, 3)],
    )
    tick(
        [plus("o2", "o2", "o2i"), plus("o1", "o1k", "o3m")],
        [to("d3x", "d3a", side), to("o2m", "o2", middle), to("o1r", "o1", pair)],
        [normed_part(0, 2), grad_c("G"), packed_rows("G")],
    )
    tick(
        [plus("d3", "d3k", "d3x")],
        [to("d2x", "d2a", side), to("d3i", "d3", inward)],
        [
            swap_packed("G"),
            grad_a("J"),
            cross("J"),
            grad_b("J"),
            grad_a("W"),
            plus("o", "o0k", "o0x", "o2m", "o1r"),
        ],
    )
    tick(
        [plus("d2", "d2k", "d2x"), plus("d3", "d3", "d3i")],
        [
            to("d1x", "d1a", side),
            to("d2i", "d2", inward),
            to("d3m", "d3", middle),
            send_b("J"),
            send_a("W"),
        ],
        [grad_b("W"), grad_c("J")],
    )
    tick(
        [plus("d2", "d2", "d2i"), plus("d1", "d1k", "d1x", "d3m")],
        [to("d0x", "d0a", side), to("d2m", "d2", middle), to("d1r", "d1", pair), send_b("W")],
        [grad_c("W"), packed_rows("J", "W")],
    )
    tick([plus("d", "d0k", "d0x", "d2m", "d1r")], (), [norm_back])
    gate_grad, up_grad = unpack_rows(plan, opened["G",], [2, 3], (0, 0, 0))
    begins = (0, 0, plan.joined)
    joined_grad, out_grad, down_grad = unpack_rows(plan, opened["J", "W"], [0, 1, 4], begins)
    grads = [joined_grad, out_grad, gate_grad, up_grad, down_grad]
    return layer.finish_output(unorder(st["o"])), st["input_grad"], st["norm_sums"], grads


def on_device(
    n_ctx,
    n_dp,
    inputs,
    norm_gain,
    norm_bias,
    joined_weight,
    gate_weight,
    up_weight,
    out_weight,
    down_weight,
    cotangent,
    lengths,
):
    grid = (n_ctx, n_dp) == (8, 4)
    if grid:
        ctx = lax.axis_index("ctx")
        z, x = ctx // 2, ctx % 2
        high = z >= 2
        order = [z, z ^ 1, jnp.where(high, 1, 2), jnp.where(high, 0, 3)]
        natural = [2 * o + (x ^ r) for o in order for r in range(2)]
        slots = jnp.zeros((n_ctx,), jnp.int32)
        for slot, part in enumerate(natural):
            slots = jnp.where(jnp.arange(n_ctx) == part, slot, slots)
    else:
        slots = jnp.arange(n_ctx, dtype=jnp.int32)
    units = gate_weight.shape[1] // n_ctx
    layer = Layer(n_ctx, slots, inputs, norm_gain, cotangent, lengths, units)
    weights = (joined_weight, out_weight, gate_weight, up_weight, down_weight)
    scales = jnp.concatenate([norm_gain, norm_bias])
    run = on_grid if grid else on_any_mesh
    output, input_grad, norm_sums, grads = run(layer, weights, scales)
    joined_grad, out_grad, gate_grad, up_grad, down_grad = grads
    return (
        output.reshape(inputs.shape),
        input_grad.reshape(inputs.shape),
        norm_sums[0, : layer.own],
        norm_sums[0, layer.own :],
        joined_grad,
        gate_grad,
        up_grad,
        out_grad,
        down_grad,
    )


def solution(mesh):
    rows = P(("dp", "ctx"), None)
    vector = P(("dp", "ctx"))
    tokens = P("dp", "ctx", None)
    return jax.shard_map(
        functools.partial(on_device, mesh.shape["ctx"], mesh.shape["dp"]),
        mesh=mesh,
        in_specs=(tokens, vector, vector, rows, rows, rows, rows, rows, tokens, P("dp")),
        out_specs=(tokens, tokens, vector, vector, rows, rows, rows, rows, rows),
        check_vma=False,
    )
```

```python
import functools

import jax
import jax.numpy as jnp
from jax import lax
from jax.experimental import pallas as pl
from jax.experimental.pallas import tpu as pltpu
from jax.sharding import PartitionSpec as P

HD = 64
ROT = 16
ATTEND_ROWS = 512
EPSILON = 1e-05
THETA = 10000.0
NEGATIVE = -1e30
BF = jnp.bfloat16
F32 = jnp.float32
LAST = (((1,), (1,)), ((), ()))
FIRST = (((0,), (0,)), ((), ()))


def dot(left, right):
    return jnp.dot(left, right, preferred_element_type=F32)


def dot_last(left, right):
    return lax.dot_general(left, right, LAST, preferred_element_type=F32)


def dot_first(left, right):
    return lax.dot_general(left, right, FIRST, preferred_element_type=F32)


def rotary_tables(length, width):
    half = ROT // 2
    lane = jnp.arange(width, dtype=jnp.int32) % HD
    frequency = THETA ** (-(2.0 * (lane % half).astype(F32)) / ROT)
    angles = jnp.arange(length, dtype=jnp.int32).astype(F32)[:, None] * frequency[None, :]
    cosine = jnp.where(lane[None, :] < ROT, jnp.cos(angles), 1.0)
    sine = jnp.sin(angles)
    sine = jnp.where(lane[None, :] < half, -sine, jnp.where(lane[None, :] < ROT, sine, 0.0))
    return cosine, sine


def partner(x):
    half = ROT // 2
    lane = lax.broadcasted_iota(jnp.int32, x.shape, 1) % HD
    down = jnp.concatenate([x[:, half:], x[:, :half]], axis=1)
    up = jnp.concatenate([x[:, -half:], x[:, :-half]], axis=1)
    return jnp.where(lane < half, down, up)


def attend_forward(
    length_ref, slot_ref, joined_ref, cos_ref, sin_ref, wide_ref, rot_ref, attn_ref, lse_ref
):
    parts, _, rows, triple = joined_ref.shape
    width = triple // 3
    length = parts * rows
    alive_count = length_ref[pl.program_id(0)]
    per = max(1, min(ATTEND_ROWS, length) // rows)
    block = per * rows
    for part in range(parts):
        slot = slot_ref[part]
        here = slice(part * rows, (part + 1) * rows)

        def rotated(start):
            x = joined_ref[slot, 0, :, start : start + width]
            return (x * cos_ref[here, :] + partner(x) * sin_ref[here, :]).astype(BF)

        rot_ref[part, 0, :, :width] = rotated(0) * 0.125
        rot_ref[part, 0, :, width : 2 * width] = rotated(width)
        rot_ref[part, 0, :, 2 * width :] = joined_ref[slot, 0, :, 2 * width :].astype(BF)
    lse_ref[...] = jnp.zeros_like(lse_ref)
    heads = width // HD
    for step in range(length // block):
        begin, end = step * per, (step + 1) * per
        stop = end * rows
        slots = [slot_ref[part] for part in range(begin, end)]

        @pl.when(begin * rows >= alive_count)
        def _(slots=slots):
            for slot in slots:
                attn_ref[slot, 0] = jnp.zeros((rows, width), BF)

        @pl.when(begin * rows < alive_count)
        def _(begin=begin, end=end, stop=stop, slots=slots):
            q_pos = begin * rows + lax.broadcasted_iota(jnp.int32, (block, 1), 0)
            k_pos = lax.broadcasted_iota(jnp.int32, (block, stop), 1)
            allowed = k_pos <= q_pos
            alive = q_pos < alive_count
            for head in range(heads):
                lane = head * HD
                q = rot_ref[begin:end, 0, :, lane : lane + HD].reshape(block, HD)
                lane += width
                k = rot_ref[:end, 0, :, lane : lane + HD].reshape(stop, HD)
                lane += width
                v = rot_ref[:end, 0, :, lane : lane + HD].reshape(stop, HD)
                scores = jnp.where(allowed, dot_last(q, k), NEGATIVE)
                top = jnp.max(scores, axis=1, keepdims=True)
                expo = jnp.exp(scores - top)
                weight = jnp.sum(expo, axis=1, keepdims=True)
                out = jnp.where(alive, dot(expo.astype(BF), v) / weight, 0.0).astype(BF)
                for index, slot in enumerate(slots):
                    there = slice(index * rows, (index + 1) * rows)
                    attn_ref[slot, 0, :, head * HD : (head + 1) * HD] = out[there, :]
                lse = jnp.where(alive, top + jnp.log(weight), 0.0)
                lse_ref[begin:end, 0, :, head : head + 1] = lse.reshape(per, rows, 1)


def attend_backward(
    length_ref, slot_ref, rot_ref, attn_ref, grad_ref, lse_ref, cos_ref, sin_ref, out_ref, dq, dk, dv
):
    parts, _, rows, triple = rot_ref.shape
    width = triple // 3
    length = parts * rows
    seq = pl.program_id(0)
    head = pl.program_id(1)
    alive_count = length_ref[seq]
    per = max(1, min(ATTEND_ROWS, length) // rows)
    block = per * rows
    lane = lax.broadcasted_iota(jnp.int32, (1, width), 1)
    mine = (lane // HD) == head

    @pl.when(head == 0)
    def _():
        dq[...] = jnp.zeros_like(dq)
        dk[...] = jnp.zeros_like(dk)
        dv[...] = jnp.zeros_like(dv)

    for step in range(length // block):
        begin, end = step * per, (step + 1) * per
        stop = end * rows

        @pl.when(begin * rows < alive_count)
        def _(begin=begin, end=end, stop=stop):
            q_pos = begin * rows + lax.broadcasted_iota(jnp.int32, (block, 1), 0)
            alive = q_pos < alive_count
            q = rot_ref[begin:end, 0, :, :width].reshape(block, width)
            q = jnp.where(mine, q, jnp.zeros_like(q))
            k = rot_ref[:end, 0, :, width : 2 * width].reshape(stop, width)
            v = rot_ref[:end, 0, :, 2 * width :].reshape(stop, width)
            slots = [slot_ref[part] for part in range(begin, end)]
            g = jnp.concatenate([grad_ref[slot, 0] for slot in slots], axis=0)
            g = jnp.where(mine & alive, g, jnp.zeros_like(g))
            o = jnp.concatenate([attn_ref[slot, 0] for slot in slots], axis=0)
            delta = jnp.sum(g.astype(F32) * o.astype(F32), axis=1, keepdims=True)
            held = lse_ref[begin:end, 0].reshape(block, lse_ref.shape[3])
            spot = lax.broadcasted_iota(jnp.int32, (1, lse_ref.shape[3]), 1) == head
            lse = jnp.sum(jnp.where(spot, held, 0.0), axis=1, keepdims=True)
            scores = dot_last(q, k)
            k_pos = lax.broadcasted_iota(jnp.int32, (block, stop), 1)
            probs = jnp.where((k_pos <= q_pos) & alive, jnp.exp(scores - lse), 0.0)
            d_probs = dot_last(g, v)
            d_scores = (probs * (d_probs - delta)).astype(BF)
            here = slice(begin * rows, stop)
            dq[here, :] += jnp.where(mine, dot(d_scores, k), 0.0)
            dk[:stop, :] += dot_first(d_scores, q)
            dv[:stop, :] += dot_first(probs.astype(BF), g)

    @pl.when(head == pl.num_programs(1) - 1)
    def _():
        for part in range(parts):
            slot = slot_ref[part]
            here = slice(part * rows, (part + 1) * rows)

            def unrotated(x):
                return (x * cos_ref[here, :] - partner(x) * sin_ref[here, :]).astype(BF)

            out_ref[slot, 0, :, :width] = unrotated(dq[here, :] * 0.125)
            out_ref[slot, 0, :, width : 2 * width] = unrotated(dk[here, :])
            out_ref[slot, 0, :, 2 * width :] = dv[here, :].astype(BF)


def attention_calls(parts, groups, rows, width, heads, lanes):
    length = parts * rows
    smem = pl.BlockSpec(memory_space=pltpu.SMEM)

    def spec(last):
        return pl.BlockSpec((parts, 1, rows, last), lambda s, *_: (0, s, 0, 0))

    table = pl.BlockSpec((length, width), lambda *_: (0, 0))

    def shape(last, dtype):
        return jax.ShapeDtypeStruct((parts, groups, rows, last), dtype)

    pairs = groups * heads * length * length // 2
    params = pltpu.CompilerParams(vmem_limit_bytes=48 * 1024 * 1024)
    forward = pl.pallas_call(
        attend_forward,
        grid=(groups,),
        in_specs=[smem, smem, spec(3 * width), table, table, pl.BlockSpec(memory_space=pl.ANY)],
        out_specs=[spec(3 * width), spec(width), spec(heads)],
        out_shape=[shape(3 * width, BF), shape(lanes, BF), shape(heads, F32)],
        input_output_aliases={5: 1},
        compiler_params=params,
        cost_estimate=pl.CostEstimate(
            flops=pairs * 1024, bytes_accessed=16 * length * width, transcendentals=pairs
        ),
        name="attend_forward",
    )
    backward = pl.pallas_call(
        attend_backward,
        grid=(groups, heads),
        in_specs=[smem, smem, spec(3 * width), spec(width), spec(width), spec(heads), table, table],
        out_specs=spec(3 * width),
        out_shape=shape(3 * width, BF),
        scratch_shapes=[pltpu.VMEM((length, width), F32)] * 3,
        compiler_params=params,
        cost_estimate=pl.CostEstimate(
            flops=pairs * 2560, bytes_accessed=16 * length * width, transcendentals=pairs
        ),
        name="attend_backward",
    )
    return forward, backward


class Plan:
    def __init__(self, n, own, width, units):
        self.n, self.own, self.width, self.units = n, own, width, units
        self.body = units // 128 * 128
        self.tail = units - self.body
        self.joined = 3 * width
        self.first = self.joined + 2 * units
        self.used = width + units
        self.second = self.used + own
        spans = [(0, r * n * width, width, width) for r in range(3)]
        for start, span in ((0, self.body), (self.body, self.tail)):
            spans += [(w, start, units, span) for w in (2, 3)]
        self.spans = [*spans, (1, 0, width, width), (4, 0, units, units)]

    def segments(self):
        lane = 0
        for weight, start, stride, span in self.spans:
            yield weight, start, stride, lane, span
            lane += span


def pack_kernel(plan, chosen, *refs):
    scale_ref, sources, out_ref = refs[0], dict(zip(chosen, refs[1:-1])), refs[-1]
    lane = 0
    for weight, start, stride, _, span in plan.segments():
        if weight in chosen:
            for dest in range(plan.n):
                begin = start + dest * stride
                out_ref[dest, :, lane : lane + span] = sources[weight][:, begin : begin + span]
            lane += span
    if lane < out_ref.shape[2]:
        for dest in range(plan.n):
            out_ref[dest, :, lane:] = scale_ref[...]


def unpack_kernel(own, outs_of, in_ref, *outs):
    for out, (source, sources, lane, lanes) in zip(outs, outs_of):
        for index in range(sources):
            block = in_ref[source + index, :, lane : lane + lanes]
            out[index * own : (index + 1) * own, :] = block


def pack_rows_kernel(own, *refs):
    sources, out = refs[:-1], refs[-1]
    for dest in range(out.shape[0]):
        lane = 0
        for source in sources:
            lanes = source.shape[1]
            out[dest, :, lane : lane + lanes] = source[dest * own : (dest + 1) * own, :]
            lane += lanes


def unpack_rows_kernel(n, layout, held, *outs):
    for source in range(n):
        for out, start, stride, lane, span in layout:
            begin = start + source * stride
            block = held[source, :, lane : lane + span].astype(F32)
            outs[out][:, begin : begin + span] = block


def in_vmem(kernel, name, out_shape):
    def call(*operands):
        place = pl.BlockSpec(memory_space=pltpu.VMEM)
        moved = sum(o.size * o.dtype.itemsize for o in operands)
        return pl.pallas_call(
            kernel,
            in_specs=[place] * len(operands),
            out_specs=jax.tree.map(lambda _: place, out_shape),
            out_shape=out_shape,
            compiler_params=pltpu.CompilerParams(vmem_limit_bytes=48 * 1024 * 1024),
            cost_estimate=pl.CostEstimate(flops=0, bytes_accessed=3 * moved, transcendentals=0),
            name=name,
        )(*operands)

    return call


def pack_columns(plan, weights, scales):
    scales = jnp.pad(scales.reshape(2, plan.own), ((0, plan.own - 2), (0, 0)))
    packed = []
    for chosen, lanes in (((0, 2, 3), plan.first), ((1, 4), plan.second)):
        shape = jax.ShapeDtypeStruct((plan.n, plan.own, lanes), BF)
        kernel = functools.partial(pack_kernel, plan, chosen)
        packed.append(in_vmem(kernel, "pack_columns", shape)(scales, *[weights[w] for w in chosen]))
    return packed


def unpack_columns(plan, packed, parts):
    n, own, lanes = packed.shape
    outs_of = [(half * n // 2, n // 2, 0, lanes) for half in range(2)] if parts else []
    outs_of.append((0, n, 0, lanes))
    shapes = [jax.ShapeDtypeStruct((c * own, lanes), BF) for _, c, _, lanes in outs_of]
    kernel = functools.partial(unpack_kernel, own, outs_of)
    return in_vmem(kernel, "unpack_columns", shapes)(packed)


def pack_rows(own, n, gradients):
    lanes = sum(g.shape[1] for g in gradients)
    shape = jax.ShapeDtypeStruct((n, own, lanes), BF)
    return in_vmem(functools.partial(pack_rows_kernel, own), "pack_rows", shape)(*gradients)


def unpack_rows(plan, packed, chosen, begins):
    layout = []
    for weight, start, stride, lane, span in plan.segments():
        if weight in chosen:
            group = 0 if weight == 0 else 1 if weight in (2, 3) else 2
            lane += begins[group] - (0, plan.joined, plan.first)[group]
            layout.append((chosen.index(weight), start, stride, lane, span))
    widths = [3 * plan.width, plan.width, plan.units, plan.units, plan.units]
    shapes = [jax.ShapeDtypeStruct((plan.own, plan.n * widths[w]), F32) for w in chosen]
    kernel = functools.partial(unpack_rows_kernel, plan.n, layout)
    return in_vmem(kernel, "unpack_rows", shapes)(packed)


def fetch_pieces(pieces, held, sems):
    copies, row = [], 0
    for i, piece in enumerate(pieces):
        there = held.at[pl.ds(row, piece.shape[0]), :]
        copies.append(pltpu.make_async_copy(piece, there, sems.at[i]))
        row += piece.shape[0]
    return copies


def stream_kernel(n, n_pieces, n_extra, n_into, finish, *refs):
    blocks, refs = refs[:n], refs[n:]
    pieces, refs = refs[:n_pieces], refs[n_pieces + n_into :]
    extra, outs, (held, rows_ref, rows_sem, weight_sem) = refs[:n_extra], refs[n_extra:-4], refs[-4:]
    size = blocks[0].shape[0]
    step = pl.program_id(0)
    steps = n // 2
    weight = fetch_pieces(pieces, held, weight_sem)

    def copy(block, buffer, half):
        there = rows_ref.at[buffer, pl.ds(half * size, size), :]
        return pltpu.make_async_copy(block, there, rows_sem.at[buffer, half])

    def fetch(index):
        for place in range(steps):

            @pl.when(index == place)
            def _(place=place):
                for half in range(2):
                    copy(blocks[2 * place + half], place % 2, half).start()

    @pl.when(step == 0)
    def _():
        fetch(0)
        for piece in weight:
            piece.start()

    @pl.when(step + 1 < steps)
    def _():
        fetch(step + 1)

    buffer = lax.rem(step, 2)
    for half in range(2):
        copy(blocks[half], buffer, half).wait()

    @pl.when(step == 0)
    def _():
        for piece in weight:
            piece.wait()

    finish(rows_ref[buffer], held, extra, outs)


def stream(name, slots, places, pieces, extra, finish, outs, into):
    size, features = slots[0].shape
    blocks = [slots[2 * place + half] for place in places for half in range(2)]
    n = len(blocks)
    first, stride = places[0], places[-1] - places[-2] if len(places) > 1 else 1
    anywhere = pl.BlockSpec(memory_space=pl.ANY)

    def rows(width):
        return pl.BlockSpec((2 * size, width), lambda i: (first + stride * i, 0))

    outs = [(features, BF), *outs]
    width = pieces[0].shape[1]
    begin = n + len(pieces)
    return pl.pallas_call(
        functools.partial(stream_kernel, n, len(pieces), len(extra), len(into), finish),
        grid=(n // 2,),
        in_specs=[anywhere] * (begin + len(into)) + [rows(e.shape[1]) for e in extra],
        out_specs=[rows(w) for w, _ in outs],
        out_shape=[jax.ShapeDtypeStruct((len(slots) * size, w), dtype) for w, dtype in outs],
        input_output_aliases={begin + i: i for i in range(len(into))},
        scratch_shapes=[
            pltpu.VMEM((features, width), BF),
            pltpu.VMEM((2, 2 * size, features), BF),
            pltpu.SemaphoreType.DMA((2, 2)),
            pltpu.SemaphoreType.DMA((len(pieces),)),
        ],
        compiler_params=pltpu.CompilerParams(vmem_limit_bytes=52 * 1024 * 1024),
        cost_estimate=pl.CostEstimate(
            flops=2 * n * size * features * width,
            bytes_accessed=2 * (n * size + width) * features * 2,
            transcendentals=0,
        ),
        name=name,
    )(*blocks, *pieces, *into, *extra)


def swiglu(plan, both):
    body, tail = plan.body, plan.tail
    hidden, factors = [], []
    for start, span in ((0, body), (2 * body, tail)):
        gate, up = both[:, start : start + span], both[:, start + span : start + 2 * span]
        sigmoid = jax.nn.sigmoid(gate)
        silu = gate * sigmoid
        hidden.append((silu * up).astype(BF))
        factors += [up * sigmoid * (1.0 + gate * (1.0 - sigmoid)), silu]
    return hidden, factors


def project_finish(plan, rows, held, extra, outs):
    normed, joined, factor_ref, wide = outs
    normed[...] = rows
    joined[...] = dot(rows, held[:, : plan.joined])
    hidden, factors = swiglu(plan, dot(rows, held[:, plan.joined :]))
    lane = 0
    for factor in factors:
        factor_ref[:, lane : lane + factor.shape[1]] = factor.astype(factor_ref.dtype)
        lane += factor.shape[1]
    wide[:, : plan.width] = jnp.zeros((rows.shape[0], plan.width), BF)
    wide[:, plan.width : plan.width + plan.body] = hidden[0]
    pad = jnp.zeros((rows.shape[0], plan.second - plan.used), BF)
    wide[:, plan.width + plan.body :] = jnp.concatenate([hidden[1], pad], axis=1)


def return_finish(plan, rows, held, extra, outs):
    (factor_ref,), (cot, d_attn, d_both) = extra, outs
    cot[...] = rows
    total = dot(rows, held[...])
    d_attn[...] = total[:, : plan.width].astype(BF)
    begin, body, tail = plan.width, plan.body, plan.tail
    for lane, start, span in (
        (0, begin, body),
        (body, begin, body),
        (2 * body, begin + body, tail),
        (2 * body + tail, begin + body, tail),
    ):
        here = slice(lane, lane + span)
        d_both[:, here] = (total[:, start : start + span] * factor_ref[:, here]).astype(BF)


def spread_kernel(count, n_pieces, places, *refs):
    lefts, refs = refs[: count * places], refs[count * places :]
    pieces, outs, (held, sems) = refs[:n_pieces], refs[n_pieces:-2], refs[-2:]
    weight = fetch_pieces(pieces, held, sems)
    for piece in weight:
        piece.start()
    size = outs[0].shape[0]
    rows = held.shape[0] // 4
    begins = [sum(p.shape[0] for p in pieces[:i]) for i in range(n_pieces)]
    for part in range(4):
        here = slice(part * rows, (part + 1) * rows)
        for begin, piece in zip(begins, weight):
            if begin // rows == part:
                piece.wait()
        for place in range(places):
            total, lane = 0.0, 0
            for left in lefts[place * count : (place + 1) * count]:
                lanes = left.shape[1]
                total += dot_last(left[...], held[here, lane : lane + lanes])
                lane += lanes
            outs[2 * place][:, here] = total[:size].astype(BF)
            outs[2 * place + 1][:, here] = total[size:].astype(BF)


def spread(name, lefts, pieces, places, size):
    anywhere = pl.BlockSpec(memory_space=pl.ANY)
    features = sum(piece.shape[0] for piece in pieces)
    width = pieces[0].shape[1]
    tokens = 2 * size * len(places)

    def rows(left, place):
        return pl.BlockSpec((2 * size, left.shape[1]), lambda i: (place, 0))

    blocks = 2 * len(places)
    return pl.pallas_call(
        functools.partial(spread_kernel, len(lefts), len(pieces), len(places)),
        grid=(1,),
        in_specs=[rows(left, place) for place in places for left in lefts]
        + [anywhere] * len(pieces),
        out_specs=[pl.BlockSpec((size, features), lambda i: (0, 0))] * blocks,
        out_shape=[jax.ShapeDtypeStruct((size, features), BF)] * blocks,
        scratch_shapes=[
            pltpu.VMEM((features, width), BF),
            pltpu.SemaphoreType.DMA((len(pieces),)),
        ],
        compiler_params=pltpu.CompilerParams(vmem_limit_bytes=52 * 1024 * 1024),
        cost_estimate=pl.CostEstimate(
            flops=2 * tokens * features * width,
            bytes_accessed=2 * (tokens + features) * width + 2 * tokens * features,
            transcendentals=0,
        ),
        name=name,
    )(*[left for _ in places for left in lefts], *pieces)


class Layer:
    def __init__(self, n_ctx, slots, inputs, norm_gain, cotangent, lengths, units):
        self.groups, self.rows, self.features = inputs.shape
        self.tokens = self.groups * self.rows
        self.n_ctx, self.slots, self.lengths = n_ctx, slots, lengths
        self.own = norm_gain.shape[0]
        self.width = self.features // n_ctx
        self.plan = Plan(n_ctx, self.own, self.width, units)
        self.flat = inputs.reshape(self.tokens, self.features).astype(F32)
        self.cot = cotangent.reshape(self.tokens, self.features)
        self.tables = rotary_tables(n_ctx * self.rows, self.width)
        self.blocks = (n_ctx, self.groups, self.rows)

    def calls(self, lanes):
        heads = self.width // HD
        return attention_calls(self.n_ctx, self.groups, self.rows, self.width, heads, lanes)

    def standardize(self):
        center = self.flat - jnp.mean(self.flat, axis=-1, keepdims=True)
        variance = jnp.mean(center * center, axis=-1, keepdims=True)
        inverse = lax.rsqrt(variance + EPSILON)
        return center * inverse, inverse

    def norm(self, standard, scales):
        gain, bias = self.scales(scales)
        return (standard * gain + bias).astype(BF), gain

    def scales(self, scales):
        return [scales[:, i].astype(F32).reshape(1, self.features) for i in range(2)]

    def attend(self, joined, wide, tables):
        lanes = wide.shape[1]
        shape = (*self.blocks, lanes)
        joined = joined.reshape(*self.blocks, 3 * self.width)
        rotated, wide, lse = self.calls(lanes)[0](
            self.lengths, self.slots, joined, *tables, wide.reshape(shape)
        )
        return rotated, wide.reshape(-1, lanes), lse

    def attend_back(self, rotated, wide, d_attn, lse, tables):
        lanes = wide.shape[1]
        return self.calls(lanes)[1](
            self.lengths,
            self.slots,
            rotated,
            wide.reshape(*self.blocks, lanes),
            d_attn.reshape(*self.blocks, self.width),
            lse,
            *tables,
        ).reshape(-1, 3 * self.width)

    def finish_output(self, branches):
        return (self.flat + branches.astype(F32)).astype(BF)

    def norm_back(self, d_normed, standard, inverse, gain):
        d_normed = d_normed.astype(F32)
        grad = d_normed * gain
        centered = (
            grad
            - jnp.mean(grad, axis=-1, keepdims=True)
            - standard * jnp.mean(grad * standard, axis=-1, keepdims=True)
        )
        sums = [jnp.sum(d_normed * standard, axis=0), jnp.sum(d_normed, axis=0)]
        sums = jnp.concatenate([v.reshape(-1, self.own) for v in sums], axis=1)
        return (self.cot.astype(F32) + inverse * centered).astype(BF), sums


def on_any_mesh(layer, weights, scales):
    plan = layer.plan
    n, own, width = plan.n, plan.own, plan.width

    def swap(pieces):
        return lax.all_to_all(pieces, "ctx", split_axis=0, concat_axis=0, tiled=True)

    def gather(v, axis):
        return lax.all_gather(v, axis, axis=0, tiled=True)

    def scatter(v, axis):
        return lax.psum_scatter(v, axis, scatter_dimension=0, tiled=True)

    first, second = (swap(packed) for packed in pack_columns(plan, weights, scales))
    w_first = gather(unpack_columns(plan, first, False)[0], "dp")
    w_second = gather(unpack_columns(plan, second, False)[0], "dp")[:, : plan.used]
    scales = second[:, :2, plan.used :]
    standard, inverse = layer.standardize()
    normed, gain = layer.norm(standard, gather(scales, "dp"))
    normed, cot = gather(normed, "ctx"), gather(layer.cot, "ctx")
    total = dot(normed, w_first)
    hidden, factors = swiglu(plan, total[:, plan.joined :])
    empty = jnp.zeros((normed.shape[0], width), BF)
    rotated, attn, lse = layer.attend(total[:, : plan.joined], empty, layer.tables)
    wide = jnp.concatenate([attn, *hidden], axis=1)
    branches = scatter(dot_last(wide, w_second).astype(BF), "ctx")
    total = dot(cot, w_second)
    body = total[:, width : width + plan.body]
    tail = total[:, width + plan.body :]
    d_both = jnp.concatenate([body, body, tail, tail], axis=1) * jnp.concatenate(factors, axis=1)
    d_attn = total[:, :width].astype(BF)
    d_joined = layer.attend_back(rotated, attn, d_attn, lse, layer.tables)
    d_first = jnp.concatenate([d_joined, d_both.astype(BF)], axis=1)
    d_normed = scatter(dot_last(d_first, w_first).astype(BF), "ctx")
    sums = [scatter(dot_first(*v).astype(BF), "dp") for v in ((normed, d_first), (cot, wide))]
    begins = (0, plan.joined, plan.first)
    grads = unpack_rows(plan, swap(pack_rows(own, n, sums)), [0, 1, 2, 3, 4], begins)
    input_grad, norm_sums = layer.norm_back(d_normed, standard, inverse, gain)
    return layer.finish_output(branches), input_grad, scatter(norm_sums, ("dp", "ctx")), grads


def swaps(bit, n):
    return [(i, i ^ bit) for i in range(n)]


class State:
    def __init__(self, **arrays):
        self.held = arrays

    def __getitem__(self, name):
        return self.held[name]

    def drop(self, *names):
        for name in names:
            del self.held[name]

    def tick(self, before=(), sends=(), work=()):
        for action in before:
            self.held.update(action(self.held))
        view = dict(self.held)
        for name, source, axis, pairs in sends:
            view[name] = lax.ppermute(self.held[source], axis, pairs)
        for action in work:
            view.update(action(view))
        names = list(view)
        held = lax.optimization_barrier([view[name] for name in names])
        self.held = dict(zip(names, held))


def on_grid(layer, weights, scales):
    plan = layer.plan
    n, own, features = plan.n, plan.own, layer.features
    ctx, dp = lax.axis_index("ctx"), lax.axis_index("dp")
    z = ctx // 2
    inner = (z == 1) | (z == 2)
    quarter = features // 4
    side, pair = ("ctx", swaps(1, n)), ("ctx", swaps(2, n))
    middle = ("ctx", [(2, 4), (3, 5), (4, 2), (5, 3)])
    outward = ("ctx", [(2, 0), (3, 1), (4, 6), (5, 7)])
    inward = ("ctx", [(b, a) for a, b in outward[1]])
    core, across = ("dp", swaps(1, 4)), ("dp", swaps(2, 4))

    def blocks_of(v, first, steps):
        blocks = [
            lax.dynamic_slice_in_dim(v, (first ^ step) * quarter, quarter, 1) for step in steps
        ]
        return jnp.concatenate(blocks, axis=1)

    def reorder(v):
        return blocks_of(v, dp, (0, 2, 1, 3))

    def unorder(v):
        return blocks_of(v, (dp % 2) * 2 + dp // 2, (0, 2, 1, 3))

    opened = {}

    def doubled(held, axis, bit, size):
        mine = lax.axis_index(axis) // bit % 2
        got = lax.ppermute(held, axis, swaps(bit, size))
        first, second = jnp.where(mine == 0, held, got), jnp.where(mine == 0, got, held)
        return jnp.concatenate([first, second], axis=0)

    def begin(s):
        held = scales.reshape(1, 2, own)
        for bit in (1, 2, 4):
            held = doubled(held, "ctx", bit, n)
        packed, second = pack_columns(plan, weights, scales)
        packed, held, c0 = lax.optimization_barrier((packed, held, s["c0"]))
        packed = lax.all_to_all(packed, "ctx", split_axis=0, concat_axis=0, tiled=True)
        made = {"c0x": lax.ppermute(c0, *side), "c1": lax.ppermute(c0, *pair)}
        for bit in (1, 2):
            held = doubled(held, "dp", bit, 4)
        normed, gain = layer.norm(standard, held)
        n0 = reorder(normed)
        made |= {"n0": n0, "gain": gain, "n0x": lax.ppermute(n0, *side)}
        made |= {"n1": lax.ppermute(n0, *pair), "n2i": lax.ppermute(n0, *middle)}
        parts = unpack_columns(plan, packed, True)
        return made | {"second": second} | dict(zip(("a0", "b0", "ab0"), parts))

    def second_in(s):
        opened["second"] = lax.all_to_all(
            s["second"], "ctx", split_axis=0, concat_axis=0, tiled=True
        )
        return {}

    def select(name):
        return lambda s: {name: jnp.where(inner, s[name + "i"], s[name + "o"])}

    def plus(name, *parts):
        return lambda s: {name: sum(s[part].astype(F32) for part in parts).astype(BF)}

    def pieces(s, name):
        names = "a0 b0 a2 b2 ab1 a3 b3" if name == "ab" else "w0 w2 w1 w3"
        return [s[key] for key in names.split()]

    def slots(s, letter):
        return [s.get(letter + i) for i in ("0", "0x", "1", "1x", "2", "2x", "3", "3x")]

    def streamed(name, letter, weight, names, finish, widths, extra, places):
        def work(s):
            done = [s[key] for key in names] if places[0] else []
            held = (slots(s, letter), places, pieces(s, weight), [s[key] for key in extra])
            made = stream(name, *held, functools.partial(finish, plan), widths, done)
            return dict(zip(names, made))

        return work

    def project(*places):
        names = ("n", "joined", "factors", "wide")
        widths = [(plan.joined, F32), (2 * plan.units, BF), (plan.second, BF)]
        return streamed("project", "n", "ab", names, project_finish, widths, [], places)

    def bring_back(*places):
        names = ("c", "d_attn", "d_both")
        widths = [(plan.width, BF), (2 * plan.units, BF)]
        held = ("factors",)
        return streamed("bring_back", "c", "w", names, return_finish, widths, held, places)

    def tables(s):
        return {"tables": layer.tables}

    def attend(s):
        made = layer.attend(s["joined"], s["wide"], s["tables"])
        return dict(zip(("rotated", "wide", "lse"), made))

    def attend_back(s):
        d_joined = layer.attend_back(
            s["rotated"], s["wide"], s["d_attn"], s["lse"], s["tables"]
        )
        return {"d_joined": d_joined}

    def scattered(name, letter, lefts, weight, places):
        def work(s):
            size = s["c0"].shape[0]
            made = spread(name, [s[v] for v in lefts], pieces(s, weight), places, size)
            keys = [f"{letter}{place}{kind}" for place in places for kind in "ka"]
            return dict(zip(keys, made))

        return work

    def output_part(*places):
        return scattered("output_part", "o", ["wide"], "w", places)

    def normed_part(*places):
        return scattered("normed_part", "d", ["d_joined", "d_both"], "ab", places)

    factors = {"J": ("n", "d_joined"), "G": ("n", "d_both"), "W": ("c", "wide")}

    def product(s, name, begin, end):
        left, right = factors[name]
        return dot_first(s[left][:, begin * quarter : end * quarter], s[right])

    def grad_a(name):
        return lambda s: {name + "A": product(s, name, 2, 4).astype(BF)}

    def grad_b(name):
        def work(s):
            total = product(s, name, 1, 2) + s[name + "Ar"][quarter:].astype(F32)
            return {name + "B": total.astype(BF)}

        return work

    def grad_c(name):
        def work(s):
            total = product(s, name, 0, 1) + s[name + "Ar"][:quarter].astype(F32)
            return {name + "C": (total + s[name + "Br"].astype(F32)).astype(BF)}

        return work

    def to(name, source, way):
        return (name, source, *way)

    def cross(name):
        return lambda s: {name + "Ar": lax.ppermute(s[name + "A"], *core)}

    def send_a(name):
        return to(name + "Ar", name + "A", core)

    def send_b(name):
        return to(name + "Br", name + "B", across)

    def packed_rows(*names):
        return lambda s: {names: pack_rows(own, n, [s[name + "C"] for name in names])}

    def swap_packed(*names):
        def work(s):
            opened[names] = lax.all_to_all(
                s[names], "ctx", split_axis=0, concat_axis=0, tiled=True
            )
            return {}

        return work

    def norm_back(s):
        input_grad, sums = layer.norm_back(unorder(s["d"]), standard, inverse, s["gain"])

        def halved(sums, dim, axis, bit, size):
            mine = lax.axis_index(axis) // bit % 2
            first, second = jnp.split(sums, 2, axis=dim)
            give = jnp.where(mine == 0, second, first)
            return jnp.where(mine == 0, first, second) + lax.ppermute(give, axis, swaps(bit, size))

        sums = sums.reshape(4, 2, 2, 2, 2 * own)
        for dim, bit in ((3, 1), (2, 2), (1, 4)):
            sums = halved(sums, dim, "ctx", bit, n)
        names = ("J", "W")
        packed, sums = lax.optimization_barrier((s[names], sums))
        opened[names] = lax.all_to_all(packed, "ctx", split_axis=0, concat_axis=0, tiled=True)
        sums = sums.reshape(4, 2 * own)
        for bit in (2, 1):
            sums = halved(sums, 0, "dp", bit, 4)
        return {"input_grad": input_grad, "norm_sums": sums}

    def y(name):
        return to(name + "2", name + "0", across)

    def near(name):
        return to(name + "1", name + "0", core)

    def far(name):
        return to(name + "3", name + "2", core)

    standard, inverse = layer.standardize()
    st = State(c0=reorder(layer.cot))
    tick = st.tick
    tick((), (), [begin])
    tick(
        (),
        [
            to("n1x", "n1", side),
            to("n3i", "n1", middle),
            to("n2o", "n2i", outward),
            y("a"),
            near("ab"),
        ],
        [second_in, tables],
    )
    tick(
        [select("n2")],
        [
            to("n2x", "n2", side),
            to("n3o", "n3i", outward),
            to("c2i", "c0", middle),
            y("b"),
            far("a"),
        ],
    )
    tick(
        [select("n3")],
        [
            to("n3x", "n3", side),
            to("c2o", "c2i", outward),
            to("c3i", "c1", middle),
            far("b"),
        ],
        [project(0, 1, 2)],
    )
    tick(
        [select("c2"), lambda s: {"w0": unpack_columns(plan, opened["second"], False)[0]}],
        [to("c2x", "c2", side), to("c3o", "c3i", outward), y("w"), near("w")],
        [project(3), attend],
    )
    tick(
        [select("c3")],
        [to("c3x", "c3", side), to("c1x", "c0x", pair), far("w")],
        [output_part(0, 1, 2, 3)],
    )
    tick(
        (),
        [to("o3x", "o3a", side), to("o1p", "o1a", pair)],
        [bring_back(0, 1, 2, 3), grad_a("G")],
    )
    tick(
        [plus("o3", "o3k", "o3x")],
        [to("o2x", "o2a", side), to("o3i", "o3", inward), send_a("G")],
        [attend_back, grad_b("G")],
    )
    tick(
        [plus("o2", "o2k", "o2x"), plus("o3", "o3", "o3i"), plus("o0a", "o0a", "o1p")],
        [to("o0x", "o0a", side), to("o2i", "o2", inward), to("o3m", "o3", middle), send_b("G")],
        [normed_part(1, 3)],
    )
    tick(
        [plus("o2", "o2", "o2i"), plus("o1", "o1k", "o3m")],
        [to("d3x", "d3a", side), to("o2m", "o2", middle), to("o1r", "o1", pair)],
        [normed_part(0, 2), grad_c("G"), packed_rows("G")],
    )
    tick(
        [plus("d3", "d3k", "d3x")],
        [to("d2x", "d2a", side), to("d3i", "d3", inward)],
        [
            swap_packed("G"),
            grad_a("J"),
            cross("J"),
            grad_b("J"),
            grad_a("W"),
            plus("o", "o0k", "o0x", "o2m", "o1r"),
        ],
    )
    tick(
        [plus("d2", "d2k", "d2x"), plus("d3", "d3", "d3i")],
        [
            to("d1x", "d1a", side),
            to("d2i", "d2", inward),
            to("d3m", "d3", middle),
            send_b("J"),
            send_a("W"),
        ],
        [grad_b("W"), grad_c("J")],
    )
    tick(
        [plus("d2", "d2", "d2i"), plus("d1", "d1k", "d1x", "d3m")],
        [to("d0x", "d0a", side), to("d2m", "d2", middle), to("d1r", "d1", pair), send_b("W")],
        [grad_c("W"), packed_rows("J", "W")],
    )
    tick([plus("d", "d0k", "d0x", "d2m", "d1r")], (), [norm_back])
    gate_grad, up_grad = unpack_rows(plan, opened["G",], [2, 3], (0, 0, 0))
    begins = (0, 0, plan.joined)
    joined_grad, out_grad, down_grad = unpack_rows(plan, opened["J", "W"], [0, 1, 4], begins)
    grads = [joined_grad, out_grad, gate_grad, up_grad, down_grad]
    return layer.finish_output(unorder(st["o"])), st["input_grad"], st["norm_sums"], grads


def on_device(
    n_ctx,
    n_dp,
    inputs,
    norm_gain,
    norm_bias,
    joined_weight,
    gate_weight,
    up_weight,
    out_weight,
    down_weight,
    cotangent,
    lengths,
):
    grid = (n_ctx, n_dp) == (8, 4)
    if grid:
        ctx = lax.axis_index("ctx")
        z, x = ctx // 2, ctx % 2
        high = z >= 2
        order = [z, z ^ 1, jnp.where(high, 1, 2), jnp.where(high, 0, 3)]
        natural = [2 * o + (x ^ r) for o in order for r in range(2)]
        slots = jnp.zeros((n_ctx,), jnp.int32)
        for slot, part in enumerate(natural):
            slots = jnp.where(jnp.arange(n_ctx) == part, slot, slots)
    else:
        slots = jnp.arange(n_ctx, dtype=jnp.int32)
    units = gate_weight.shape[1] // n_ctx
    layer = Layer(n_ctx, slots, inputs, norm_gain, cotangent, lengths, units)
    weights = (joined_weight, out_weight, gate_weight, up_weight, down_weight)
    scales = jnp.concatenate([norm_gain, norm_bias])
    run = on_grid if grid else on_any_mesh
    output, input_grad, norm_sums, grads = run(layer, weights, scales)
    joined_grad, out_grad, gate_grad, up_grad, down_grad = grads
    return (
        output.reshape(inputs.shape),
        input_grad.reshape(inputs.shape),
        norm_sums[0, : layer.own],
        norm_sums[0, layer.own :],
        joined_grad,
        gate_grad,
        up_grad,
        out_grad,
        down_grad,
    )


def solution(mesh):
    rows = P(("dp", "ctx"), None)
    vector = P(("dp", "ctx"))
    tokens = P("dp", "ctx", None)
    return jax.shard_map(
        functools.partial(on_device, mesh.shape["ctx"], mesh.shape["dp"]),
        mesh=mesh,
        in_specs=(tokens, vector, vector, rows, rows, rows, rows, rows, tokens, P("dp")),
        out_specs=(tokens, tokens, vector, vector, rows, rows, rows, rows, rows),
        check_vma=False,
    )
```

```python
import functools

import jax
import jax.numpy as jnp
from jax import lax
from jax.experimental import pallas as pl
from jax.experimental.pallas import tpu as pltpu
from jax.sharding import PartitionSpec as P

HD = 64
ROT = 16
ATTEND_ROWS = 512
EPSILON = 1e-05
THETA = 10000.0
NEGATIVE = -1e30
BF = jnp.bfloat16
F32 = jnp.float32
LAST = (((1,), (1,)), ((), ()))
FIRST = (((0,), (0,)), ((), ()))


def dot(left, right):
    return jnp.dot(left, right, preferred_element_type=F32)


def dot_last(left, right):
    return lax.dot_general(left, right, LAST, preferred_element_type=F32)


def dot_first(left, right):
    return lax.dot_general(left, right, FIRST, preferred_element_type=F32)


def rotary_tables(length, width):
    half = ROT // 2
    lane = jnp.arange(width, dtype=jnp.int32) % HD
    frequency = THETA ** (-(2.0 * (lane % half).astype(F32)) / ROT)
    angles = jnp.arange(length, dtype=jnp.int32).astype(F32)[:, None] * frequency[None, :]
    cosine = jnp.where(lane[None, :] < ROT, jnp.cos(angles), 1.0)
    sine = jnp.sin(angles)
    sine = jnp.where(lane[None, :] < half, -sine, jnp.where(lane[None, :] < ROT, sine, 0.0))
    return cosine, sine


def partner(x):
    half = ROT // 2
    lane = lax.broadcasted_iota(jnp.int32, x.shape, 1) % HD
    down = jnp.concatenate([x[:, half:], x[:, :half]], axis=1)
    up = jnp.concatenate([x[:, -half:], x[:, :-half]], axis=1)
    return jnp.where(lane < half, down, up)


def attend_forward(
    length_ref, slot_ref, joined_ref, cos_ref, sin_ref, wide_ref, rot_ref, attn_ref, lse_ref
):
    parts, _, rows, triple = joined_ref.shape
    width = triple // 3
    length = parts * rows
    alive_count = length_ref[pl.program_id(0)]
    per = max(1, min(ATTEND_ROWS, length) // rows)
    block = per * rows
    for part in range(parts):
        slot = slot_ref[part]
        here = slice(part * rows, (part + 1) * rows)

        def rotated(start):
            x = joined_ref[slot, 0, :, start : start + width]
            return (x * cos_ref[here, :] + partner(x) * sin_ref[here, :]).astype(BF)

        rot_ref[part, 0, :, :width] = rotated(0) * 0.125
        rot_ref[part, 0, :, width : 2 * width] = rotated(width)
        rot_ref[part, 0, :, 2 * width :] = joined_ref[slot, 0, :, 2 * width :].astype(BF)
    lse_ref[...] = jnp.zeros_like(lse_ref)
    heads = width // HD
    for step in range(length // block):
        begin, end = step * per, (step + 1) * per
        stop = end * rows
        slots = [slot_ref[part] for part in range(begin, end)]

        @pl.when(begin * rows >= alive_count)
        def _(slots=slots):
            for slot in slots:
                attn_ref[slot, 0] = jnp.zeros((rows, width), BF)

        @pl.when(begin * rows < alive_count)
        def _(begin=begin, end=end, stop=stop, slots=slots):
            q_pos = begin * rows + lax.broadcasted_iota(jnp.int32, (block, 1), 0)
            k_pos = lax.broadcasted_iota(jnp.int32, (block, stop), 1)
            allowed = k_pos <= q_pos
            alive = q_pos < alive_count
            for head in range(heads):
                lane = head * HD
                q = rot_ref[begin:end, 0, :, lane : lane + HD].reshape(block, HD)
                lane += width
                k = rot_ref[:end, 0, :, lane : lane + HD].reshape(stop, HD)
                lane += width
                v = rot_ref[:end, 0, :, lane : lane + HD].reshape(stop, HD)
                scores = jnp.where(allowed, dot_last(q, k), NEGATIVE)
                top = jnp.max(scores, axis=1, keepdims=True)
                expo = jnp.exp(scores - top)
                weight = jnp.sum(expo, axis=1, keepdims=True)
                out = jnp.where(alive, dot(expo.astype(BF), v) / weight, 0.0).astype(BF)
                for index, slot in enumerate(slots):
                    there = slice(index * rows, (index + 1) * rows)
                    attn_ref[slot, 0, :, head * HD : (head + 1) * HD] = out[there, :]
                lse = jnp.where(alive, top + jnp.log(weight), 0.0)
                lse_ref[begin:end, 0, :, head : head + 1] = lse.reshape(per, rows, 1)


def attend_backward(
    length_ref, slot_ref, rot_ref, attn_ref, grad_ref, lse_ref, cos_ref, sin_ref, out_ref, dq, dk, dv
):
    parts, _, rows, triple = rot_ref.shape
    width = triple // 3
    length = parts * rows
    seq = pl.program_id(0)
    head = pl.program_id(1)
    alive_count = length_ref[seq]
    per = max(1, min(ATTEND_ROWS, length) // rows)
    block = per * rows
    lane = lax.broadcasted_iota(jnp.int32, (1, width), 1)
    mine = (lane // HD) == head

    @pl.when(head == 0)
    def _():
        dq[...] = jnp.zeros_like(dq)
        dk[...] = jnp.zeros_like(dk)
        dv[...] = jnp.zeros_like(dv)

    for step in range(length // block):
        begin, end = step * per, (step + 1) * per
        stop = end * rows

        @pl.when(begin * rows < alive_count)
        def _(begin=begin, end=end, stop=stop):
            q_pos = begin * rows + lax.broadcasted_iota(jnp.int32, (block, 1), 0)
            alive = q_pos < alive_count
            q = rot_ref[begin:end, 0, :, :width].reshape(block, width)
            q = jnp.where(mine, q, jnp.zeros_like(q))
            k = rot_ref[:end, 0, :, width : 2 * width].reshape(stop, width)
            v = rot_ref[:end, 0, :, 2 * width :].reshape(stop, width)
            slots = [slot_ref[part] for part in range(begin, end)]
            g = jnp.concatenate([grad_ref[slot, 0] for slot in slots], axis=0)
            g = jnp.where(mine & alive, g, jnp.zeros_like(g))
            o = jnp.concatenate([attn_ref[slot, 0] for slot in slots], axis=0)
            delta = jnp.sum(g.astype(F32) * o.astype(F32), axis=1, keepdims=True)
            held = lse_ref[begin:end, 0].reshape(block, lse_ref.shape[3])
            spot = lax.broadcasted_iota(jnp.int32, (1, lse_ref.shape[3]), 1) == head
            lse = jnp.sum(jnp.where(spot, held, 0.0), axis=1, keepdims=True)
            scores = dot_last(q, k)
            k_pos = lax.broadcasted_iota(jnp.int32, (block, stop), 1)
            probs = jnp.where((k_pos <= q_pos) & alive, jnp.exp(scores - lse), 0.0)
            d_probs = dot_last(g, v)
            d_scores = (probs * (d_probs - delta)).astype(BF)
            here = slice(begin * rows, stop)
            dq[here, :] += jnp.where(mine, dot(d_scores, k), 0.0)
            dk[:stop, :] += dot_first(d_scores, q)
            dv[:stop, :] += dot_first(probs.astype(BF), g)

    @pl.when(head == pl.num_programs(1) - 1)
    def _():
        for part in range(parts):
            slot = slot_ref[part]
            here = slice(part * rows, (part + 1) * rows)

            def unrotated(x):
                return (x * cos_ref[here, :] - partner(x) * sin_ref[here, :]).astype(BF)

            out_ref[slot, 0, :, :width] = unrotated(dq[here, :] * 0.125)
            out_ref[slot, 0, :, width : 2 * width] = unrotated(dk[here, :])
            out_ref[slot, 0, :, 2 * width :] = dv[here, :].astype(BF)


def attention_calls(parts, groups, rows, width, heads, lanes):
    length = parts * rows
    smem = pl.BlockSpec(memory_space=pltpu.SMEM)

    def spec(last):
        return pl.BlockSpec((parts, 1, rows, last), lambda s, *_: (0, s, 0, 0))

    table = pl.BlockSpec((length, width), lambda *_: (0, 0))

    def shape(last, dtype):
        return jax.ShapeDtypeStruct((parts, groups, rows, last), dtype)

    pairs = groups * heads * length * length // 2
    params = pltpu.CompilerParams(vmem_limit_bytes=48 * 1024 * 1024)
    forward = pl.pallas_call(
        attend_forward,
        grid=(groups,),
        in_specs=[smem, smem, spec(3 * width), table, table, pl.BlockSpec(memory_space=pl.ANY)],
        out_specs=[spec(3 * width), spec(width), spec(heads)],
        out_shape=[shape(3 * width, BF), shape(lanes, BF), shape(heads, F32)],
        input_output_aliases={5: 1},
        compiler_params=params,
        cost_estimate=pl.CostEstimate(
            flops=pairs * 1024, bytes_accessed=16 * length * width, transcendentals=pairs
        ),
        name="attend_forward",
    )
    backward = pl.pallas_call(
        attend_backward,
        grid=(groups, heads),
        in_specs=[smem, smem, spec(3 * width), spec(width), spec(width), spec(heads), table, table],
        out_specs=spec(3 * width),
        out_shape=shape(3 * width, BF),
        scratch_shapes=[pltpu.VMEM((length, width), F32)] * 3,
        compiler_params=params,
        cost_estimate=pl.CostEstimate(
            flops=pairs * 2560, bytes_accessed=16 * length * width, transcendentals=pairs
        ),
        name="attend_backward",
    )
    return forward, backward


class Plan:
    def __init__(self, n, own, width, units):
        self.n, self.own, self.width, self.units = n, own, width, units
        self.body = units // 128 * 128
        self.tail = units - self.body
        self.joined = 3 * width
        self.first = self.joined + 2 * units
        self.used = width + units
        self.second = self.used + own
        spans = [(0, r * n * width, width, width) for r in range(3)]
        for start, span in ((0, self.body), (self.body, self.tail)):
            spans += [(w, start, units, span) for w in (2, 3)]
        self.spans = [*spans, (1, 0, width, width), (4, 0, units, units)]

    def segments(self):
        lane = 0
        for weight, start, stride, span in self.spans:
            yield weight, start, stride, lane, span
            lane += span


def pack_kernel(plan, chosen, *refs):
    scale_ref, sources, out_ref = refs[0], dict(zip(chosen, refs[1:-1])), refs[-1]
    lane = 0
    for weight, start, stride, _, span in plan.segments():
        if weight in chosen:
            for dest in range(plan.n):
                begin = start + dest * stride
                out_ref[dest, :, lane : lane + span] = sources[weight][:, begin : begin + span]
            lane += span
    if lane < out_ref.shape[2]:
        for dest in range(plan.n):
            out_ref[dest, :, lane:] = scale_ref[...]


def unpack_kernel(own, outs_of, in_ref, *outs):
    for out, (source, sources, lane, lanes) in zip(outs, outs_of):
        for index in range(sources):
            block = in_ref[source + index, :, lane : lane + lanes]
            out[index * own : (index + 1) * own, :] = block


def pack_rows_kernel(own, counts, *refs):
    sources, out = refs[:-1], refs[-1]
    lane = 0
    for count in counts:
        chunks, sources = sources[:count], sources[count:]
        lanes = chunks[0].shape[1]
        for dest in range(out.shape[0]):
            chunk, row = divmod(dest * own, chunks[0].shape[0])
            out[dest, :, lane : lane + lanes] = chunks[chunk][row : row + own, :]
        lane += lanes


def unpack_rows_kernel(n, layout, held, *outs):
    for source in range(n):
        for out, start, stride, lane, span in layout:
            begin = start + source * stride
            block = held[source, :, lane : lane + span].astype(F32)
            outs[out][:, begin : begin + span] = block


def in_vmem(kernel, name, out_shape):
    def call(*operands):
        place = pl.BlockSpec(memory_space=pltpu.VMEM)
        moved = sum(o.size * o.dtype.itemsize for o in operands)
        return pl.pallas_call(
            kernel,
            in_specs=[place] * len(operands),
            out_specs=jax.tree.map(lambda _: place, out_shape),
            out_shape=out_shape,
            compiler_params=pltpu.CompilerParams(vmem_limit_bytes=48 * 1024 * 1024),
            cost_estimate=pl.CostEstimate(flops=0, bytes_accessed=3 * moved, transcendentals=0),
            name=name,
        )(*operands)

    return call


def pack_columns(plan, weights, scales):
    scales = jnp.pad(scales.reshape(2, plan.own), ((0, plan.own - 2), (0, 0)))
    packed = []
    for chosen, lanes in (((0, 2, 3), plan.first), ((1, 4), plan.second)):
        shape = jax.ShapeDtypeStruct((plan.n, plan.own, lanes), BF)
        kernel = functools.partial(pack_kernel, plan, chosen)
        packed.append(in_vmem(kernel, "pack_columns", shape)(scales, *[weights[w] for w in chosen]))
    return packed


def unpack_columns(plan, packed, parts):
    n, own, lanes = packed.shape
    outs_of = [(half * n // 2, n // 2, 0, lanes) for half in range(2)] if parts else []
    outs_of.append((0, n, 0, lanes))
    shapes = [jax.ShapeDtypeStruct((c * own, lanes), BF) for _, c, _, lanes in outs_of]
    kernel = functools.partial(unpack_kernel, own, outs_of)
    return in_vmem(kernel, "unpack_columns", shapes)(packed)


def pack_rows(own, n, gradients):
    lanes = sum(chunks[0].shape[1] for chunks in gradients)
    shape = jax.ShapeDtypeStruct((n, own, lanes), BF)
    kernel = functools.partial(pack_rows_kernel, own, [len(chunks) for chunks in gradients])
    return in_vmem(kernel, "pack_rows", shape)(*[c for chunks in gradients for c in chunks])


def unpack_rows(plan, packed, chosen, begins):
    layout = []
    for weight, start, stride, lane, span in plan.segments():
        if weight in chosen:
            group = 0 if weight == 0 else 1 if weight in (2, 3) else 2
            lane += begins[group] - (0, plan.joined, plan.first)[group]
            layout.append((chosen.index(weight), start, stride, lane, span))
    widths = [3 * plan.width, plan.width, plan.units, plan.units, plan.units]
    shapes = [jax.ShapeDtypeStruct((plan.own, plan.n * widths[w]), F32) for w in chosen]
    kernel = functools.partial(unpack_rows_kernel, plan.n, layout)
    return in_vmem(kernel, "unpack_rows", shapes)(packed)


def fetch_pieces(pieces, held, sems):
    copies, row = [], 0
    for i, piece in enumerate(pieces):
        there = held.at[pl.ds(row, piece.shape[0]), :]
        copies.append(pltpu.make_async_copy(piece, there, sems.at[i]))
        row += piece.shape[0]
    return copies


def stream_kernel(n, n_pieces, n_extra, n_into, finish, *refs):
    blocks, refs = refs[:n], refs[n:]
    pieces, refs = refs[:n_pieces], refs[n_pieces + n_into :]
    extra, outs, (held, rows_ref, rows_sem, weight_sem) = refs[:n_extra], refs[n_extra:-4], refs[-4:]
    size = blocks[0].shape[0]
    step = pl.program_id(0)
    steps = n // 2
    weight = fetch_pieces(pieces, held, weight_sem)

    def copy(block, buffer, half):
        there = rows_ref.at[buffer, pl.ds(half * size, size), :]
        return pltpu.make_async_copy(block, there, rows_sem.at[buffer, half])

    def fetch(index):
        for place in range(steps):

            @pl.when(index == place)
            def _(place=place):
                for half in range(2):
                    copy(blocks[2 * place + half], place % 2, half).start()

    @pl.when(step == 0)
    def _():
        fetch(0)
        for piece in weight:
            piece.start()

    @pl.when(step + 1 < steps)
    def _():
        fetch(step + 1)

    buffer = lax.rem(step, 2)
    for half in range(2):
        copy(blocks[half], buffer, half).wait()

    @pl.when(step == 0)
    def _():
        for piece in weight:
            piece.wait()

    finish(rows_ref[buffer], held, extra, outs)


def stream(name, slots, places, pieces, extra, finish, outs, into):
    size, features = slots[0].shape
    blocks = [slots[2 * place + half] for place in places for half in range(2)]
    n = len(blocks)
    first, stride = places[0], places[-1] - places[-2] if len(places) > 1 else 1
    anywhere = pl.BlockSpec(memory_space=pl.ANY)

    def rows(width):
        return pl.BlockSpec((2 * size, width), lambda i: (first + stride * i, 0))

    outs = [(features, BF), *outs]
    width = pieces[0].shape[1]
    begin = n + len(pieces)
    return pl.pallas_call(
        functools.partial(stream_kernel, n, len(pieces), len(extra), len(into), finish),
        grid=(n // 2,),
        in_specs=[anywhere] * (begin + len(into)) + [rows(e.shape[1]) for e in extra],
        out_specs=[rows(w) for w, _ in outs],
        out_shape=[jax.ShapeDtypeStruct((len(slots) * size, w), dtype) for w, dtype in outs],
        input_output_aliases={begin + i: i for i in range(len(into))},
        scratch_shapes=[
            pltpu.VMEM((features, width), BF),
            pltpu.VMEM((2, 2 * size, features), BF),
            pltpu.SemaphoreType.DMA((2, 2)),
            pltpu.SemaphoreType.DMA((len(pieces),)),
        ],
        compiler_params=pltpu.CompilerParams(vmem_limit_bytes=52 * 1024 * 1024),
        cost_estimate=pl.CostEstimate(
            flops=2 * n * size * features * width,
            bytes_accessed=2 * (n * size + width) * features * 2,
            transcendentals=0,
        ),
        name=name,
    )(*blocks, *pieces, *into, *extra)


def swiglu(plan, both):
    body, tail = plan.body, plan.tail
    hidden, factors = [], []
    for start, span in ((0, body), (2 * body, tail)):
        gate, up = both[:, start : start + span], both[:, start + span : start + 2 * span]
        sigmoid = jax.nn.sigmoid(gate)
        silu = gate * sigmoid
        hidden.append((silu * up).astype(BF))
        factors += [up * sigmoid * (1.0 + gate * (1.0 - sigmoid)), silu]
    return hidden, factors


def project_finish(plan, rows, held, extra, outs):
    normed, joined, factor_ref, wide = outs
    normed[...] = rows
    joined[...] = dot(rows, held[:, : plan.joined])
    hidden, factors = swiglu(plan, dot(rows, held[:, plan.joined :]))
    lane = 0
    for factor in factors:
        factor_ref[:, lane : lane + factor.shape[1]] = factor.astype(factor_ref.dtype)
        lane += factor.shape[1]
    wide[:, : plan.width] = jnp.zeros((rows.shape[0], plan.width), BF)
    wide[:, plan.width : plan.width + plan.body] = hidden[0]
    pad = jnp.zeros((rows.shape[0], plan.second - plan.used), BF)
    wide[:, plan.width + plan.body :] = jnp.concatenate([hidden[1], pad], axis=1)


def return_finish(plan, rows, held, extra, outs):
    (factor_ref,), (cot, d_attn, d_both) = extra, outs
    cot[...] = rows
    total = dot(rows, held[...])
    d_attn[...] = total[:, : plan.width].astype(BF)
    begin, body, tail = plan.width, plan.body, plan.tail
    for lane, start, span in (
        (0, begin, body),
        (body, begin, body),
        (2 * body, begin + body, tail),
        (2 * body + tail, begin + body, tail),
    ):
        here = slice(lane, lane + span)
        d_both[:, here] = (total[:, start : start + span] * factor_ref[:, here]).astype(BF)


def spread_kernel(count, n_pieces, places, *refs):
    lefts, refs = refs[: count * places], refs[count * places :]
    pieces, outs, (held, sems) = refs[:n_pieces], refs[n_pieces:-2], refs[-2:]
    weight = fetch_pieces(pieces, held, sems)
    for piece in weight:
        piece.start()
    size = outs[0].shape[0]
    rows = held.shape[0] // 4
    begins = [sum(p.shape[0] for p in pieces[:i]) for i in range(n_pieces)]
    for part in range(4):
        here = slice(part * rows, (part + 1) * rows)
        for begin, piece in zip(begins, weight):
            if begin // rows == part:
                piece.wait()
        for place in range(places):
            total, lane = 0.0, 0
            for left in lefts[place * count : (place + 1) * count]:
                lanes = left.shape[1]
                total += dot_last(left[...], held[here, lane : lane + lanes])
                lane += lanes
            outs[2 * place][:, here] = total[:size].astype(BF)
            outs[2 * place + 1][:, here] = total[size:].astype(BF)


def spread(name, lefts, pieces, places, size):
    anywhere = pl.BlockSpec(memory_space=pl.ANY)
    features = sum(piece.shape[0] for piece in pieces)
    width = pieces[0].shape[1]
    tokens = 2 * size * len(places)

    def rows(left, place):
        return pl.BlockSpec((2 * size, left.shape[1]), lambda i: (place, 0))

    blocks = 2 * len(places)
    return pl.pallas_call(
        functools.partial(spread_kernel, len(lefts), len(pieces), len(places)),
        grid=(1,),
        in_specs=[rows(left, place) for place in places for left in lefts]
        + [anywhere] * len(pieces),
        out_specs=[pl.BlockSpec((size, features), lambda i: (0, 0))] * blocks,
        out_shape=[jax.ShapeDtypeStruct((size, features), BF)] * blocks,
        scratch_shapes=[
            pltpu.VMEM((features, width), BF),
            pltpu.SemaphoreType.DMA((len(pieces),)),
        ],
        compiler_params=pltpu.CompilerParams(vmem_limit_bytes=52 * 1024 * 1024),
        cost_estimate=pl.CostEstimate(
            flops=2 * tokens * features * width,
            bytes_accessed=2 * (tokens + features) * width + 2 * tokens * features,
            transcendentals=0,
        ),
        name=name,
    )(*[left for _ in places for left in lefts], *pieces)


class Layer:
    def __init__(self, n_ctx, slots, inputs, norm_gain, cotangent, lengths, units):
        self.groups, self.rows, self.features = inputs.shape
        self.tokens = self.groups * self.rows
        self.n_ctx, self.slots, self.lengths = n_ctx, slots, lengths
        self.own = norm_gain.shape[0]
        self.width = self.features // n_ctx
        self.plan = Plan(n_ctx, self.own, self.width, units)
        self.flat = inputs.reshape(self.tokens, self.features).astype(F32)
        self.cot = cotangent.reshape(self.tokens, self.features)
        self.tables = rotary_tables(n_ctx * self.rows, self.width)
        self.blocks = (n_ctx, self.groups, self.rows)

    def calls(self, lanes):
        heads = self.width // HD
        return attention_calls(self.n_ctx, self.groups, self.rows, self.width, heads, lanes)

    def standardize(self):
        center = self.flat - jnp.mean(self.flat, axis=-1, keepdims=True)
        variance = jnp.mean(center * center, axis=-1, keepdims=True)
        inverse = lax.rsqrt(variance + EPSILON)
        return center * inverse, inverse

    def norm(self, standard, scales):
        gain, bias = self.scales(scales)
        return (standard * gain + bias).astype(BF), gain

    def scales(self, scales):
        return [scales[:, i].astype(F32).reshape(1, self.features) for i in range(2)]

    def attend(self, joined, wide, tables):
        lanes = wide.shape[1]
        shape = (*self.blocks, lanes)
        joined = joined.reshape(*self.blocks, 3 * self.width)
        rotated, wide, lse = self.calls(lanes)[0](
            self.lengths, self.slots, joined, *tables, wide.reshape(shape)
        )
        return rotated, wide.reshape(-1, lanes), lse

    def attend_back(self, rotated, wide, d_attn, lse, tables):
        lanes = wide.shape[1]
        return self.calls(lanes)[1](
            self.lengths,
            self.slots,
            rotated,
            wide.reshape(*self.blocks, lanes),
            d_attn.reshape(*self.blocks, self.width),
            lse,
            *tables,
        ).reshape(-1, 3 * self.width)

    def finish_output(self, branches):
        return (self.flat + branches.astype(F32)).astype(BF)

    def norm_back(self, d_normed, standard, inverse, gain):
        d_normed = d_normed.astype(F32)
        grad = d_normed * gain
        centered = (
            grad
            - jnp.mean(grad, axis=-1, keepdims=True)
            - standard * jnp.mean(grad * standard, axis=-1, keepdims=True)
        )
        sums = [jnp.sum(d_normed * standard, axis=0), jnp.sum(d_normed, axis=0)]
        sums = jnp.concatenate([v.reshape(-1, self.own) for v in sums], axis=1)
        return (self.cot.astype(F32) + inverse * centered).astype(BF), sums


def on_any_mesh(layer, weights, scales):
    plan = layer.plan
    n, own, width = plan.n, plan.own, plan.width

    def swap(pieces):
        return lax.all_to_all(pieces, "ctx", split_axis=0, concat_axis=0, tiled=True)

    def gather(v, axis):
        return lax.all_gather(v, axis, axis=0, tiled=True)

    def scatter(v, axis):
        return lax.psum_scatter(v, axis, scatter_dimension=0, tiled=True)

    first, second = (swap(packed) for packed in pack_columns(plan, weights, scales))
    w_first = gather(unpack_columns(plan, first, False)[0], "dp")
    w_second = gather(unpack_columns(plan, second, False)[0], "dp")[:, : plan.used]
    scales = second[:, :2, plan.used :]
    standard, inverse = layer.standardize()
    normed, gain = layer.norm(standard, gather(scales, "dp"))
    normed, cot = gather(normed, "ctx"), gather(layer.cot, "ctx")
    total = dot(normed, w_first)
    hidden, factors = swiglu(plan, total[:, plan.joined :])
    empty = jnp.zeros((normed.shape[0], width), BF)
    rotated, attn, lse = layer.attend(total[:, : plan.joined], empty, layer.tables)
    wide = jnp.concatenate([attn, *hidden], axis=1)
    branches = scatter(dot_last(wide, w_second).astype(BF), "ctx")
    total = dot(cot, w_second)
    body = total[:, width : width + plan.body]
    tail = total[:, width + plan.body :]
    d_both = jnp.concatenate([body, body, tail, tail], axis=1) * jnp.concatenate(factors, axis=1)
    d_attn = total[:, :width].astype(BF)
    d_joined = layer.attend_back(rotated, attn, d_attn, lse, layer.tables)
    d_first = jnp.concatenate([d_joined, d_both.astype(BF)], axis=1)
    d_normed = scatter(dot_last(d_first, w_first).astype(BF), "ctx")
    sums = [scatter(dot_first(*v).astype(BF), "dp") for v in ((normed, d_first), (cot, wide))]
    begins = (0, plan.joined, plan.first)
    grads = unpack_rows(plan, swap(pack_rows(own, n, [[v] for v in sums])), [0, 1, 2, 3, 4], begins)
    input_grad, norm_sums = layer.norm_back(d_normed, standard, inverse, gain)
    return layer.finish_output(branches), input_grad, scatter(norm_sums, ("dp", "ctx")), grads


def swaps(bit, n):
    return [(i, i ^ bit) for i in range(n)]


class State:
    def __init__(self, **arrays):
        self.held = arrays

    def __getitem__(self, name):
        return self.held[name]

    def drop(self, *names):
        for name in names:
            del self.held[name]

    def tick(self, before=(), sends=(), work=()):
        for action in before:
            self.held.update(action(self.held))
        view = dict(self.held)
        for name, source, axis, pairs in sends:
            view[name] = lax.ppermute(self.held[source], axis, pairs)
        for action in work:
            view.update(action(view))
        names = list(view)
        held = lax.optimization_barrier([view[name] for name in names])
        self.held = dict(zip(names, held))


def on_grid(layer, weights, scales):
    plan = layer.plan
    n, own, features = plan.n, plan.own, layer.features
    ctx, dp = lax.axis_index("ctx"), lax.axis_index("dp")
    z = ctx // 2
    inner = (z == 1) | (z == 2)
    quarter = features // 4
    side, pair = ("ctx", swaps(1, n)), ("ctx", swaps(2, n))
    middle = ("ctx", [(2, 4), (3, 5), (4, 2), (5, 3)])
    outward = ("ctx", [(2, 0), (3, 1), (4, 6), (5, 7)])
    inward = ("ctx", [(b, a) for a, b in outward[1]])
    core, across = ("dp", swaps(1, 4)), ("dp", swaps(2, 4))

    def blocks_of(v, first, steps):
        blocks = [
            lax.dynamic_slice_in_dim(v, (first ^ step) * quarter, quarter, 1) for step in steps
        ]
        return jnp.concatenate(blocks, axis=1)

    def reorder(v):
        return blocks_of(v, dp, (0, 2, 1, 3))

    def unorder(v):
        return blocks_of(v, (dp % 2) * 2 + dp // 2, (0, 2, 1, 3))

    opened = {}

    def doubled(held, axis, bit, size):
        mine = lax.axis_index(axis) // bit % 2
        got = lax.ppermute(held, axis, swaps(bit, size))
        first, second = jnp.where(mine == 0, held, got), jnp.where(mine == 0, got, held)
        return jnp.concatenate([first, second], axis=0)

    def begin(s):
        held = scales.reshape(1, 2, own)
        for bit in (1, 2, 4):
            held = doubled(held, "ctx", bit, n)
        packed, second = pack_columns(plan, weights, scales)
        packed, held, c0 = lax.optimization_barrier((packed, held, s["c0"]))
        packed = lax.all_to_all(packed, "ctx", split_axis=0, concat_axis=0, tiled=True)
        made = {"c0x": lax.ppermute(c0, *side), "c1": lax.ppermute(c0, *pair)}
        for bit in (1, 2):
            held = doubled(held, "dp", bit, 4)
        normed, gain = layer.norm(standard, held)
        n0 = reorder(normed)
        made |= {"n0": n0, "gain": gain, "n0x": lax.ppermute(n0, *side)}
        made |= {"n1": lax.ppermute(n0, *pair), "n2i": lax.ppermute(n0, *middle)}
        parts = unpack_columns(plan, packed, True)
        return made | {"second": second} | dict(zip(("a0", "b0", "ab0"), parts))

    def second_in(s):
        opened["second"] = lax.all_to_all(
            s["second"], "ctx", split_axis=0, concat_axis=0, tiled=True
        )
        return {}

    def select(name):
        return lambda s: {name: jnp.where(inner, s[name + "i"], s[name + "o"])}

    def plus(name, *parts):
        return lambda s: {name: sum(s[part].astype(F32) for part in parts).astype(BF)}

    def pieces(s, name):
        names = "a0 b0 a2 b2 ab1 a3 b3" if name == "ab" else "w0 w2 w1 w3"
        return [s[key] for key in names.split()]

    def slots(s, letter):
        return [s.get(letter + i) for i in ("0", "0x", "1", "1x", "2", "2x", "3", "3x")]

    def streamed(name, letter, weight, names, finish, widths, extra, places):
        def work(s):
            done = [s[key] for key in names] if places[0] else []
            held = (slots(s, letter), places, pieces(s, weight), [s[key] for key in extra])
            made = stream(name, *held, functools.partial(finish, plan), widths, done)
            return dict(zip(names, made))

        return work

    def project(*places):
        names = ("n", "joined", "factors", "wide")
        widths = [(plan.joined, F32), (2 * plan.units, BF), (plan.second, BF)]
        return streamed("project", "n", "ab", names, project_finish, widths, [], places)

    def bring_back(*places):
        names = ("c", "d_attn", "d_both")
        widths = [(plan.width, BF), (2 * plan.units, BF)]
        held = ("factors",)
        return streamed("bring_back", "c", "w", names, return_finish, widths, held, places)

    def tables(s):
        return {"tables": layer.tables}

    def attend(s):
        made = layer.attend(s["joined"], s["wide"], s["tables"])
        return dict(zip(("rotated", "wide", "lse"), made))

    def attend_back(s):
        d_joined = layer.attend_back(
            s["rotated"], s["wide"], s["d_attn"], s["lse"], s["tables"]
        )
        return {"d_joined": d_joined}

    def scattered(name, letter, lefts, weight, places):
        def work(s):
            size = s["c0"].shape[0]
            made = spread(name, [s[v] for v in lefts], pieces(s, weight), places, size)
            keys = [f"{letter}{place}{kind}" for place in places for kind in "ka"]
            return dict(zip(keys, made))

        return work

    def output_part(*places):
        return scattered("output_part", "o", ["wide"], "w", places)

    def normed_part(*places):
        return scattered("normed_part", "d", ["d_joined", "d_both"], "ab", places)

    factors = {"J": ("n", "d_joined"), "G": ("n", "d_both"), "W": ("c", "wide")}

    def product(s, name, begin, end):
        left, right = factors[name]
        rows = slice(int(begin * quarter), int(end * quarter))
        return dot_first(s[left][:, rows], s[right])

    def grad_a(name):
        return lambda s: {name + "A": product(s, name, 2, 4).astype(BF)}

    def grad_b(name):
        def work(s):
            total = product(s, name, 1, 2) + s[name + "Ar"][quarter:].astype(F32)
            return {name + "B": total.astype(BF)}

        return work

    def grad_c(name):
        def work(s):
            total = product(s, name, 0, 1) + s[name + "Ar"][:quarter].astype(F32)
            return {name + "C": (total + s[name + "Br"].astype(F32)).astype(BF)}

        return work

    def half_b(step):
        def work(s):
            rows = slice((2 + step) * quarter // 2, (3 + step) * quarter // 2)
            total = product(s, "G", 1 + step / 2, 1.5 + step / 2) + s["GAr"][rows].astype(F32)
            return {f"GB{step + 1}": total.astype(BF)}

        return work

    def half_c(step):
        def work(s):
            rows = slice(step * quarter // 2, (step + 1) * quarter // 2)
            total = product(s, "G", step / 2, (step + 1) / 2) + s["GAr"][rows].astype(F32)
            return {f"GC{step + 1}": (total + s[f"GB{step + 1}r"].astype(F32)).astype(BF)}

        return work

    def to(name, source, way):
        return (name, source, *way)

    def cross(name):
        return lambda s: {name + "Ar": lax.ppermute(s[name + "A"], *core)}

    def send_a(name):
        return to(name + "Ar", name + "A", core)

    def send_b(name):
        return to(name + "Br", name + "B", across)

    def packed_rows(*names):
        def work(s):
            chunks = [[s[name + "C"]] if name != "G" else [s["GC1"], s["GC2"]] for name in names]
            return {names: pack_rows(own, n, chunks)}

        return work

    def swap_packed(*names):
        def work(s):
            opened[names] = lax.all_to_all(
                s[names], "ctx", split_axis=0, concat_axis=0, tiled=True
            )
            return {}

        return work

    def norm_back(s):
        input_grad, sums = layer.norm_back(unorder(s["d"]), standard, inverse, s["gain"])

        def halved(sums, dim, axis, bit, size):
            mine = lax.axis_index(axis) // bit % 2
            first, second = jnp.split(sums, 2, axis=dim)
            give = jnp.where(mine == 0, second, first)
            return jnp.where(mine == 0, first, second) + lax.ppermute(give, axis, swaps(bit, size))

        sums = sums.reshape(4, 2, 2, 2, 2 * own)
        for dim, bit in ((3, 1), (2, 2), (1, 4)):
            sums = halved(sums, dim, "ctx", bit, n)
        names = ("J", "W")
        packed, sums = lax.optimization_barrier((s[names], sums))
        opened[names] = lax.all_to_all(packed, "ctx", split_axis=0, concat_axis=0, tiled=True)
        sums = sums.reshape(4, 2 * own)
        for bit in (2, 1):
            sums = halved(sums, 0, "dp", bit, 4)
        return {"input_grad": input_grad, "norm_sums": sums}

    def y(name):
        return to(name + "2", name + "0", across)

    def near(name):
        return to(name + "1", name + "0", core)

    def far(name):
        return to(name + "3", name + "2", core)

    standard, inverse = layer.standardize()
    st = State(c0=reorder(layer.cot))
    tick = st.tick
    tick((), (), [begin])
    tick(
        (),
        [
            to("n1x", "n1", side),
            to("n3i", "n1", middle),
            to("n2o", "n2i", outward),
            y("a"),
            near("ab"),
        ],
        [second_in, tables],
    )
    tick(
        [select("n2")],
        [
            to("n2x", "n2", side),
            to("n3o", "n3i", outward),
            to("c2i", "c0", middle),
            y("b"),
            far("a"),
        ],
    )
    tick(
        [select("n3")],
        [
            to("n3x", "n3", side),
            to("c2o", "c2i", outward),
            to("c3i", "c1", middle),
            far("b"),
        ],
        [project(0, 1, 2)],
    )
    tick(
        [select("c2"), lambda s: {"w0": unpack_columns(plan, opened["second"], False)[0]}],
        [to("c2x", "c2", side), to("c3o", "c3i", outward), y("w"), near("w")],
        [project(3), attend],
    )
    tick(
        [select("c3")],
        [to("c3x", "c3", side), to("c1x", "c0x", pair), far("w")],
        [output_part(0, 1, 2, 3), bring_back(0, 2)],
    )
    tick(
        (),
        [to("o3x", "o3a", side), to("o1p", "o1a", pair)],
        [bring_back(1, 3), grad_a("G")],
    )
    tick(
        [plus("o3", "o3k", "o3x")],
        [to("o2x", "o2a", side), to("o3i", "o3", inward), send_a("G")],
        [attend_back, half_b(0), half_b(1)],
    )
    tick(
        [plus("o2", "o2k", "o2x"), plus("o3", "o3", "o3i"), plus("o0a", "o0a", "o1p")],
        [to("o0x", "o0a", side), to("o2i", "o2", inward), to("o3m", "o3", middle), to("GB1r", "GB1", across)],
        [normed_part(1, 3)],
    )
    tick(
        [plus("o2", "o2", "o2i"), plus("o1", "o1k", "o3m")],
        [to("d3x", "d3a", side), to("o2m", "o2", middle), to("o1r", "o1", pair), to("GB2r", "GB2", across)],
        [normed_part(0, 2), half_c(0), half_c(1), packed_rows("G")],
    )
    tick(
        [plus("d3", "d3k", "d3x")],
        [to("d2x", "d2a", side), to("d3i", "d3", inward)],
        [
            swap_packed("G"),
            grad_a("J"),
            cross("J"),
            grad_b("J"),
            grad_a("W"),
            plus("o", "o0k", "o0x", "o2m", "o1r"),
        ],
    )
    tick(
        [plus("d2", "d2k", "d2x"), plus("d3", "d3", "d3i")],
        [
            to("d1x", "d1a", side),
            to("d2i", "d2", inward),
            to("d3m", "d3", middle),
            send_b("J"),
            send_a("W"),
        ],
        [grad_b("W"), grad_c("J")],
    )
    tick(
        [plus("d2", "d2", "d2i"), plus("d1", "d1k", "d1x", "d3m")],
        [to("d0x", "d0a", side), to("d2m", "d2", middle), to("d1r", "d1", pair), send_b("W")],
        [grad_c("W"), packed_rows("J", "W")],
    )
    tick([plus("d", "d0k", "d0x", "d2m", "d1r")], (), [norm_back])
    gate_grad, up_grad = unpack_rows(plan, opened["G",], [2, 3], (0, 0, 0))
    begins = (0, 0, plan.joined)
    joined_grad, out_grad, down_grad = unpack_rows(plan, opened["J", "W"], [0, 1, 4], begins)
    grads = [joined_grad, out_grad, gate_grad, up_grad, down_grad]
    return layer.finish_output(unorder(st["o"])), st["input_grad"], st["norm_sums"], grads


def on_device(
    n_ctx,
    n_dp,
    inputs,
    norm_gain,
    norm_bias,
    joined_weight,
    gate_weight,
    up_weight,
    out_weight,
    down_weight,
    cotangent,
    lengths,
):
    grid = (n_ctx, n_dp) == (8, 4)
    if grid:
        ctx = lax.axis_index("ctx")
        z, x = ctx // 2, ctx % 2
        high = z >= 2
        order = [z, z ^ 1, jnp.where(high, 1, 2), jnp.where(high, 0, 3)]
        natural = [2 * o + (x ^ r) for o in order for r in range(2)]
        slots = jnp.zeros((n_ctx,), jnp.int32)
        for slot, part in enumerate(natural):
            slots = jnp.where(jnp.arange(n_ctx) == part, slot, slots)
    else:
        slots = jnp.arange(n_ctx, dtype=jnp.int32)
    units = gate_weight.shape[1] // n_ctx
    layer = Layer(n_ctx, slots, inputs, norm_gain, cotangent, lengths, units)
    weights = (joined_weight, out_weight, gate_weight, up_weight, down_weight)
    scales = jnp.concatenate([norm_gain, norm_bias])
    run = on_grid if grid else on_any_mesh
    output, input_grad, norm_sums, grads = run(layer, weights, scales)
    joined_grad, out_grad, gate_grad, up_grad, down_grad = grads
    return (
        output.reshape(inputs.shape),
        input_grad.reshape(inputs.shape),
        norm_sums[0, : layer.own],
        norm_sums[0, layer.own :],
        joined_grad,
        gate_grad,
        up_grad,
        out_grad,
        down_grad,
    )


def solution(mesh):
    rows = P(("dp", "ctx"), None)
    vector = P(("dp", "ctx"))
    tokens = P("dp", "ctx", None)
    return jax.shard_map(
        functools.partial(on_device, mesh.shape["ctx"], mesh.shape["dp"]),
        mesh=mesh,
        in_specs=(tokens, vector, vector, rows, rows, rows, rows, rows, tokens, P("dp")),
        out_specs=(tokens, tokens, vector, vector, rows, rows, rows, rows, rows),
        check_vma=False,
    )
```

```python
import functools

import jax
import jax.numpy as jnp
from jax import lax
from jax.experimental import pallas as pl
from jax.experimental.pallas import tpu as pltpu
from jax.sharding import PartitionSpec as P

HD = 64
ROT = 16
ATTEND_ROWS = 512
EPSILON = 1e-05
THETA = 10000.0
NEGATIVE = -1e30
BF = jnp.bfloat16
F32 = jnp.float32
LAST = (((1,), (1,)), ((), ()))
FIRST = (((0,), (0,)), ((), ()))


def dot(left, right):
    return jnp.dot(left, right, preferred_element_type=F32)


def dot_last(left, right):
    return lax.dot_general(left, right, LAST, preferred_element_type=F32)


def dot_first(left, right):
    return lax.dot_general(left, right, FIRST, preferred_element_type=F32)


def rotary_tables(length, width):
    half = ROT // 2
    lane = jnp.arange(width, dtype=jnp.int32) % HD
    frequency = THETA ** (-(2.0 * (lane % half).astype(F32)) / ROT)
    angles = jnp.arange(length, dtype=jnp.int32).astype(F32)[:, None] * frequency[None, :]
    cosine = jnp.where(lane[None, :] < ROT, jnp.cos(angles), 1.0)
    sine = jnp.sin(angles)
    sine = jnp.where(lane[None, :] < half, -sine, jnp.where(lane[None, :] < ROT, sine, 0.0))
    return cosine, sine


def partner(x):
    half = ROT // 2
    lane = lax.broadcasted_iota(jnp.int32, x.shape, 1) % HD
    down = jnp.concatenate([x[:, half:], x[:, :half]], axis=1)
    up = jnp.concatenate([x[:, -half:], x[:, :-half]], axis=1)
    return jnp.where(lane < half, down, up)


def attend_forward(
    length_ref, slot_ref, joined_ref, cos_ref, sin_ref, wide_ref, rot_ref, attn_ref, lse_ref
):
    parts, _, rows, triple = joined_ref.shape
    width = triple // 3
    length = parts * rows
    alive_count = length_ref[pl.program_id(0)]
    per = max(1, min(ATTEND_ROWS, length) // rows)
    block = per * rows
    for part in range(parts):
        slot = slot_ref[part]
        here = slice(part * rows, (part + 1) * rows)

        def rotated(start):
            x = joined_ref[slot, 0, :, start : start + width]
            return (x * cos_ref[here, :] + partner(x) * sin_ref[here, :]).astype(BF)

        rot_ref[part, 0, :, :width] = rotated(0) * 0.125
        rot_ref[part, 0, :, width : 2 * width] = rotated(width)
        rot_ref[part, 0, :, 2 * width :] = joined_ref[slot, 0, :, 2 * width :].astype(BF)
    lse_ref[...] = jnp.zeros_like(lse_ref)
    heads = width // HD
    for step in range(length // block):
        begin, end = step * per, (step + 1) * per
        stop = end * rows
        slots = [slot_ref[part] for part in range(begin, end)]

        @pl.when(begin * rows >= alive_count)
        def _(slots=slots):
            for slot in slots:
                attn_ref[slot, 0] = jnp.zeros((rows, width), BF)

        @pl.when(begin * rows < alive_count)
        def _(begin=begin, end=end, stop=stop, slots=slots):
            q_pos = begin * rows + lax.broadcasted_iota(jnp.int32, (block, 1), 0)
            k_pos = lax.broadcasted_iota(jnp.int32, (block, stop), 1)
            allowed = k_pos <= q_pos
            alive = q_pos < alive_count
            for head in range(heads):
                lane = head * HD
                q = rot_ref[begin:end, 0, :, lane : lane + HD].reshape(block, HD)
                lane += width
                k = rot_ref[:end, 0, :, lane : lane + HD].reshape(stop, HD)
                lane += width
                v = rot_ref[:end, 0, :, lane : lane + HD].reshape(stop, HD)
                scores = jnp.where(allowed, dot_last(q, k), NEGATIVE)
                top = jnp.max(scores, axis=1, keepdims=True)
                expo = jnp.exp(scores - top)
                weight = jnp.sum(expo, axis=1, keepdims=True)
                out = jnp.where(alive, dot(expo.astype(BF), v) / weight, 0.0).astype(BF)
                for index, slot in enumerate(slots):
                    there = slice(index * rows, (index + 1) * rows)
                    attn_ref[slot, 0, :, head * HD : (head + 1) * HD] = out[there, :]
                lse = jnp.where(alive, top + jnp.log(weight), 0.0)
                lse_ref[begin:end, 0, :, head : head + 1] = lse.reshape(per, rows, 1)


def attend_backward(
    length_ref, slot_ref, rot_ref, attn_ref, grad_ref, lse_ref, cos_ref, sin_ref, out_ref, dq, dk, dv
):
    parts, _, rows, triple = rot_ref.shape
    width = triple // 3
    length = parts * rows
    seq = pl.program_id(0)
    head = pl.program_id(1)
    alive_count = length_ref[seq]
    per = max(1, min(ATTEND_ROWS, length) // rows)
    block = per * rows
    lane = lax.broadcasted_iota(jnp.int32, (1, width), 1)
    mine = (lane // HD) == head

    @pl.when(head == 0)
    def _():
        dq[...] = jnp.zeros_like(dq)
        dk[...] = jnp.zeros_like(dk)
        dv[...] = jnp.zeros_like(dv)

    for step in range(length // block):
        begin, end = step * per, (step + 1) * per
        stop = end * rows

        @pl.when(begin * rows < alive_count)
        def _(begin=begin, end=end, stop=stop):
            q_pos = begin * rows + lax.broadcasted_iota(jnp.int32, (block, 1), 0)
            alive = q_pos < alive_count
            q = rot_ref[begin:end, 0, :, :width].reshape(block, width)
            q = jnp.where(mine, q, jnp.zeros_like(q))
            k = rot_ref[:end, 0, :, width : 2 * width].reshape(stop, width)
            v = rot_ref[:end, 0, :, 2 * width :].reshape(stop, width)
            slots = [slot_ref[part] for part in range(begin, end)]
            g = jnp.concatenate([grad_ref[slot, 0] for slot in slots], axis=0)
            g = jnp.where(mine & alive, g, jnp.zeros_like(g))
            o = jnp.concatenate([attn_ref[slot, 0] for slot in slots], axis=0)
            delta = jnp.sum(g.astype(F32) * o.astype(F32), axis=1, keepdims=True)
            held = lse_ref[begin:end, 0].reshape(block, lse_ref.shape[3])
            spot = lax.broadcasted_iota(jnp.int32, (1, lse_ref.shape[3]), 1) == head
            lse = jnp.sum(jnp.where(spot, held, 0.0), axis=1, keepdims=True)
            scores = dot_last(q, k)
            k_pos = lax.broadcasted_iota(jnp.int32, (block, stop), 1)
            probs = jnp.where((k_pos <= q_pos) & alive, jnp.exp(scores - lse), 0.0)
            d_probs = dot_last(g, v)
            d_scores = (probs * (d_probs - delta)).astype(BF)
            here = slice(begin * rows, stop)
            dq[here, :] += jnp.where(mine, dot(d_scores, k), 0.0)
            dk[:stop, :] += dot_first(d_scores, q)
            dv[:stop, :] += dot_first(probs.astype(BF), g)

    @pl.when(head == pl.num_programs(1) - 1)
    def _():
        for part in range(parts):
            slot = slot_ref[part]
            here = slice(part * rows, (part + 1) * rows)

            def unrotated(x):
                return (x * cos_ref[here, :] - partner(x) * sin_ref[here, :]).astype(BF)

            out_ref[slot, 0, :, :width] = unrotated(dq[here, :] * 0.125)
            out_ref[slot, 0, :, width : 2 * width] = unrotated(dk[here, :])
            out_ref[slot, 0, :, 2 * width :] = dv[here, :].astype(BF)


def attention_calls(parts, groups, rows, width, heads, lanes):
    length = parts * rows
    smem = pl.BlockSpec(memory_space=pltpu.SMEM)

    def spec(last):
        return pl.BlockSpec((parts, 1, rows, last), lambda s, *_: (0, s, 0, 0))

    table = pl.BlockSpec((length, width), lambda *_: (0, 0))

    def shape(last, dtype):
        return jax.ShapeDtypeStruct((parts, groups, rows, last), dtype)

    pairs = groups * heads * length * length // 2
    params = pltpu.CompilerParams(vmem_limit_bytes=48 * 1024 * 1024)
    forward = pl.pallas_call(
        attend_forward,
        grid=(groups,),
        in_specs=[smem, smem, spec(3 * width), table, table, pl.BlockSpec(memory_space=pl.ANY)],
        out_specs=[spec(3 * width), spec(width), spec(heads)],
        out_shape=[shape(3 * width, BF), shape(lanes, BF), shape(heads, F32)],
        input_output_aliases={5: 1},
        compiler_params=params,
        cost_estimate=pl.CostEstimate(
            flops=pairs * 1024, bytes_accessed=16 * length * width, transcendentals=pairs
        ),
        name="attend_forward",
    )
    backward = pl.pallas_call(
        attend_backward,
        grid=(groups, heads),
        in_specs=[smem, smem, spec(3 * width), spec(width), spec(width), spec(heads), table, table],
        out_specs=spec(3 * width),
        out_shape=shape(3 * width, BF),
        scratch_shapes=[pltpu.VMEM((length, width), F32)] * 3,
        compiler_params=params,
        cost_estimate=pl.CostEstimate(
            flops=pairs * 2560, bytes_accessed=16 * length * width, transcendentals=pairs
        ),
        name="attend_backward",
    )
    return forward, backward


class Plan:
    def __init__(self, n, own, width, units):
        self.n, self.own, self.width, self.units = n, own, width, units
        self.body = units // 128 * 128
        self.tail = units - self.body
        self.joined = 3 * width
        self.first = self.joined + 2 * units
        self.used = width + units
        self.second = self.used + own
        spans = [(0, r * n * width, width, width) for r in range(3)]
        for start, span in ((0, self.body), (self.body, self.tail)):
            spans += [(w, start, units, span) for w in (2, 3)]
        self.spans = [*spans, (1, 0, width, width), (4, 0, units, units)]

    def segments(self):
        lane = 0
        for weight, start, stride, span in self.spans:
            yield weight, start, stride, lane, span
            lane += span


def pack_kernel(plan, chosen, *refs):
    scale_ref, sources, out_ref = refs[0], dict(zip(chosen, refs[1:-1])), refs[-1]
    lane = 0
    for weight, start, stride, _, span in plan.segments():
        if weight in chosen:
            for dest in range(plan.n):
                begin = start + dest * stride
                out_ref[dest, :, lane : lane + span] = sources[weight][:, begin : begin + span]
            lane += span
    if lane < out_ref.shape[2]:
        for dest in range(plan.n):
            out_ref[dest, :, lane:] = scale_ref[...]


def unpack_kernel(own, outs_of, in_ref, *outs):
    for out, (source, sources, lane, lanes) in zip(outs, outs_of):
        for index in range(sources):
            block = in_ref[source + index, :, lane : lane + lanes]
            out[index * own : (index + 1) * own, :] = block


def pack_rows_kernel(own, counts, *refs):
    sources, out = refs[:-1], refs[-1]
    lane = 0
    for count in counts:
        chunks, sources = sources[:count], sources[count:]
        lanes = chunks[0].shape[1]
        for dest in range(out.shape[0]):
            chunk, row = divmod(dest * own, chunks[0].shape[0])
            out[dest, :, lane : lane + lanes] = chunks[chunk][row : row + own, :]
        lane += lanes


def unpack_rows_kernel(n, layout, held, *outs):
    for source in range(n):
        for out, start, stride, lane, span in layout:
            begin = start + source * stride
            block = held[source, :, lane : lane + span].astype(F32)
            outs[out][:, begin : begin + span] = block


def in_vmem(kernel, name, out_shape):
    def call(*operands):
        place = pl.BlockSpec(memory_space=pltpu.VMEM)
        moved = sum(o.size * o.dtype.itemsize for o in operands)
        return pl.pallas_call(
            kernel,
            in_specs=[place] * len(operands),
            out_specs=jax.tree.map(lambda _: place, out_shape),
            out_shape=out_shape,
            compiler_params=pltpu.CompilerParams(vmem_limit_bytes=48 * 1024 * 1024),
            cost_estimate=pl.CostEstimate(flops=0, bytes_accessed=3 * moved, transcendentals=0),
            name=name,
        )(*operands)

    return call


def pack_columns(plan, weights, scales):
    scales = jnp.pad(scales.reshape(2, plan.own), ((0, plan.own - 2), (0, 0)))
    packed = []
    for chosen, lanes in (((0, 2, 3), plan.first), ((1, 4), plan.second)):
        shape = jax.ShapeDtypeStruct((plan.n, plan.own, lanes), BF)
        kernel = functools.partial(pack_kernel, plan, chosen)
        packed.append(in_vmem(kernel, "pack_columns", shape)(scales, *[weights[w] for w in chosen]))
    return packed


def unpack_columns(plan, packed, parts):
    n, own, lanes = packed.shape
    outs_of = [(half * n // 2, n // 2, 0, lanes) for half in range(2)] if parts else []
    outs_of.append((0, n, 0, lanes))
    shapes = [jax.ShapeDtypeStruct((c * own, lanes), BF) for _, c, _, lanes in outs_of]
    kernel = functools.partial(unpack_kernel, own, outs_of)
    return in_vmem(kernel, "unpack_columns", shapes)(packed)


def pack_rows(own, n, gradients):
    lanes = sum(chunks[0].shape[1] for chunks in gradients)
    shape = jax.ShapeDtypeStruct((n, own, lanes), BF)
    kernel = functools.partial(pack_rows_kernel, own, [len(chunks) for chunks in gradients])
    return in_vmem(kernel, "pack_rows", shape)(*[c for chunks in gradients for c in chunks])


def unpack_rows(plan, packed, chosen, begins):
    layout = []
    for weight, start, stride, lane, span in plan.segments():
        if weight in chosen:
            group = 0 if weight == 0 else 1 if weight in (2, 3) else 2
            lane += begins[group] - (0, plan.joined, plan.first)[group]
            layout.append((chosen.index(weight), start, stride, lane, span))
    widths = [3 * plan.width, plan.width, plan.units, plan.units, plan.units]
    shapes = [jax.ShapeDtypeStruct((plan.own, plan.n * widths[w]), F32) for w in chosen]
    kernel = functools.partial(unpack_rows_kernel, plan.n, layout)
    return in_vmem(kernel, "unpack_rows", shapes)(packed)


def fetch_pieces(pieces, held, sems):
    copies, row = [], 0
    for i, piece in enumerate(pieces):
        there = held.at[pl.ds(row, piece.shape[0]), :]
        copies.append(pltpu.make_async_copy(piece, there, sems.at[i]))
        row += piece.shape[0]
    return copies


def stream_kernel(n, n_pieces, n_extra, n_into, finish, *refs):
    blocks, refs = refs[:n], refs[n:]
    pieces, refs = refs[:n_pieces], refs[n_pieces + n_into :]
    extra, outs, (held, rows_ref, rows_sem, weight_sem) = refs[:n_extra], refs[n_extra:-4], refs[-4:]
    size = blocks[0].shape[0]
    step = pl.program_id(0)
    steps = n // 2
    weight = fetch_pieces(pieces, held, weight_sem)

    def copy(block, buffer, half):
        there = rows_ref.at[buffer, pl.ds(half * size, size), :]
        return pltpu.make_async_copy(block, there, rows_sem.at[buffer, half])

    def fetch(index):
        for place in range(steps):

            @pl.when(index == place)
            def _(place=place):
                for half in range(2):
                    copy(blocks[2 * place + half], place % 2, half).start()

    @pl.when(step == 0)
    def _():
        fetch(0)
        for piece in weight:
            piece.start()

    @pl.when(step + 1 < steps)
    def _():
        fetch(step + 1)

    buffer = lax.rem(step, 2)
    for half in range(2):
        copy(blocks[half], buffer, half).wait()

    @pl.when(step == 0)
    def _():
        for piece in weight:
            piece.wait()

    finish(rows_ref[buffer], held, extra, outs)


def stream(name, slots, places, pieces, extra, finish, outs, into):
    size, features = slots[0].shape
    blocks = [slots[2 * place + half] for place in places for half in range(2)]
    n = len(blocks)
    first, stride = places[0], places[-1] - places[-2] if len(places) > 1 else 1
    anywhere = pl.BlockSpec(memory_space=pl.ANY)

    def rows(width):
        return pl.BlockSpec((2 * size, width), lambda i: (first + stride * i, 0))

    outs = [(features, BF), *outs]
    width = pieces[0].shape[1]
    begin = n + len(pieces)
    return pl.pallas_call(
        functools.partial(stream_kernel, n, len(pieces), len(extra), len(into), finish),
        grid=(n // 2,),
        in_specs=[anywhere] * (begin + len(into)) + [rows(e.shape[1]) for e in extra],
        out_specs=[rows(w) for w, _ in outs],
        out_shape=[jax.ShapeDtypeStruct((len(slots) * size, w), dtype) for w, dtype in outs],
        input_output_aliases={begin + i: i for i in range(len(into))},
        scratch_shapes=[
            pltpu.VMEM((features, width), BF),
            pltpu.VMEM((2, 2 * size, features), BF),
            pltpu.SemaphoreType.DMA((2, 2)),
            pltpu.SemaphoreType.DMA((len(pieces),)),
        ],
        compiler_params=pltpu.CompilerParams(vmem_limit_bytes=52 * 1024 * 1024),
        cost_estimate=pl.CostEstimate(
            flops=2 * n * size * features * width,
            bytes_accessed=2 * (n * size + width) * features * 2,
            transcendentals=0,
        ),
        name=name,
    )(*blocks, *pieces, *into, *extra)


def swiglu(plan, both):
    body, tail = plan.body, plan.tail
    hidden, factors = [], []
    for start, span in ((0, body), (2 * body, tail)):
        gate, up = both[:, start : start + span], both[:, start + span : start + 2 * span]
        sigmoid = jax.nn.sigmoid(gate)
        silu = gate * sigmoid
        hidden.append((silu * up).astype(BF))
        factors += [up * sigmoid * (1.0 + gate * (1.0 - sigmoid)), silu]
    return hidden, factors


def project_finish(plan, rows, held, extra, outs):
    normed, joined, factor_ref, wide = outs
    normed[...] = rows
    joined[...] = dot(rows, held[:, : plan.joined])
    hidden, factors = swiglu(plan, dot(rows, held[:, plan.joined :]))
    lane = 0
    for factor in factors:
        factor_ref[:, lane : lane + factor.shape[1]] = factor.astype(factor_ref.dtype)
        lane += factor.shape[1]
    wide[:, : plan.width] = jnp.zeros((rows.shape[0], plan.width), BF)
    wide[:, plan.width : plan.width + plan.body] = hidden[0]
    pad = jnp.zeros((rows.shape[0], plan.second - plan.used), BF)
    wide[:, plan.width + plan.body :] = jnp.concatenate([hidden[1], pad], axis=1)


def return_finish(plan, rows, held, extra, outs):
    (factor_ref,), (cot, d_attn, d_both) = extra, outs
    cot[...] = rows
    total = dot(rows, held[...])
    d_attn[...] = total[:, : plan.width].astype(BF)
    begin, body, tail = plan.width, plan.body, plan.tail
    for lane, start, span in (
        (0, begin, body),
        (body, begin, body),
        (2 * body, begin + body, tail),
        (2 * body + tail, begin + body, tail),
    ):
        here = slice(lane, lane + span)
        d_both[:, here] = (total[:, start : start + span] * factor_ref[:, here]).astype(BF)


def spread_kernel(count, n_pieces, places, *refs):
    lefts, refs = refs[: count * places], refs[count * places :]
    pieces, outs, (held, sems) = refs[:n_pieces], refs[n_pieces:-2], refs[-2:]
    weight = fetch_pieces(pieces, held, sems)
    for piece in weight:
        piece.start()
    size = outs[0].shape[0]
    rows = held.shape[0] // 4
    begins = [sum(p.shape[0] for p in pieces[:i]) for i in range(n_pieces)]
    for part in range(4):
        here = slice(part * rows, (part + 1) * rows)
        for begin, piece in zip(begins, weight):
            if begin // rows == part:
                piece.wait()
        for place in range(places):
            total, lane = 0.0, 0
            for left in lefts[place * count : (place + 1) * count]:
                lanes = left.shape[1]
                total += dot_last(left[...], held[here, lane : lane + lanes])
                lane += lanes
            outs[2 * place][:, here] = total[:size].astype(BF)
            outs[2 * place + 1][:, here] = total[size:].astype(BF)


def spread(name, lefts, pieces, places, size):
    anywhere = pl.BlockSpec(memory_space=pl.ANY)
    features = sum(piece.shape[0] for piece in pieces)
    width = pieces[0].shape[1]
    tokens = 2 * size * len(places)

    def rows(left, place):
        return pl.BlockSpec((2 * size, left.shape[1]), lambda i: (place, 0))

    blocks = 2 * len(places)
    return pl.pallas_call(
        functools.partial(spread_kernel, len(lefts), len(pieces), len(places)),
        grid=(1,),
        in_specs=[rows(left, place) for place in places for left in lefts]
        + [anywhere] * len(pieces),
        out_specs=[pl.BlockSpec((size, features), lambda i: (0, 0))] * blocks,
        out_shape=[jax.ShapeDtypeStruct((size, features), BF)] * blocks,
        scratch_shapes=[
            pltpu.VMEM((features, width), BF),
            pltpu.SemaphoreType.DMA((len(pieces),)),
        ],
        compiler_params=pltpu.CompilerParams(vmem_limit_bytes=52 * 1024 * 1024),
        cost_estimate=pl.CostEstimate(
            flops=2 * tokens * features * width,
            bytes_accessed=2 * (tokens + features) * width + 2 * tokens * features,
            transcendentals=0,
        ),
        name=name,
    )(*[left for _ in places for left in lefts], *pieces)


class Layer:
    def __init__(self, n_ctx, slots, inputs, norm_gain, cotangent, lengths, units):
        self.groups, self.rows, self.features = inputs.shape
        self.tokens = self.groups * self.rows
        self.n_ctx, self.slots, self.lengths = n_ctx, slots, lengths
        self.own = norm_gain.shape[0]
        self.width = self.features // n_ctx
        self.plan = Plan(n_ctx, self.own, self.width, units)
        self.flat = inputs.reshape(self.tokens, self.features).astype(F32)
        self.cot = cotangent.reshape(self.tokens, self.features)
        self.tables = rotary_tables(n_ctx * self.rows, self.width)
        self.blocks = (n_ctx, self.groups, self.rows)

    def calls(self, lanes):
        heads = self.width // HD
        return attention_calls(self.n_ctx, self.groups, self.rows, self.width, heads, lanes)

    def standardize(self):
        center = self.flat - jnp.mean(self.flat, axis=-1, keepdims=True)
        variance = jnp.mean(center * center, axis=-1, keepdims=True)
        inverse = lax.rsqrt(variance + EPSILON)
        return center * inverse, inverse

    def norm(self, standard, scales):
        gain, bias = self.scales(scales)
        return (standard * gain + bias).astype(BF), gain

    def scales(self, scales):
        return [scales[:, i].astype(F32).reshape(1, self.features) for i in range(2)]

    def attend(self, joined, wide, tables):
        lanes = wide.shape[1]
        shape = (*self.blocks, lanes)
        joined = joined.reshape(*self.blocks, 3 * self.width)
        rotated, wide, lse = self.calls(lanes)[0](
            self.lengths, self.slots, joined, *tables, wide.reshape(shape)
        )
        return rotated, wide.reshape(-1, lanes), lse

    def attend_back(self, rotated, wide, d_attn, lse, tables):
        lanes = wide.shape[1]
        return self.calls(lanes)[1](
            self.lengths,
            self.slots,
            rotated,
            wide.reshape(*self.blocks, lanes),
            d_attn.reshape(*self.blocks, self.width),
            lse,
            *tables,
        ).reshape(-1, 3 * self.width)

    def finish_output(self, branches):
        return (self.flat + branches.astype(F32)).astype(BF)

    def norm_back(self, d_normed, standard, inverse, gain):
        d_normed = d_normed.astype(F32)
        grad = d_normed * gain
        centered = (
            grad
            - jnp.mean(grad, axis=-1, keepdims=True)
            - standard * jnp.mean(grad * standard, axis=-1, keepdims=True)
        )
        sums = [jnp.sum(d_normed * standard, axis=0), jnp.sum(d_normed, axis=0)]
        sums = jnp.concatenate([v.reshape(-1, self.own) for v in sums], axis=1)
        return (self.cot.astype(F32) + inverse * centered).astype(BF), sums


def on_any_mesh(layer, weights, scales):
    plan = layer.plan
    n, own, width = plan.n, plan.own, plan.width

    def swap(pieces):
        return lax.all_to_all(pieces, "ctx", split_axis=0, concat_axis=0, tiled=True)

    def gather(v, axis):
        return lax.all_gather(v, axis, axis=0, tiled=True)

    def scatter(v, axis):
        return lax.psum_scatter(v, axis, scatter_dimension=0, tiled=True)

    first, second = (swap(packed) for packed in pack_columns(plan, weights, scales))
    w_first = gather(unpack_columns(plan, first, False)[0], "dp")
    w_second = gather(unpack_columns(plan, second, False)[0], "dp")[:, : plan.used]
    scales = second[:, :2, plan.used :]
    standard, inverse = layer.standardize()
    normed, gain = layer.norm(standard, gather(scales, "dp"))
    normed, cot = gather(normed, "ctx"), gather(layer.cot, "ctx")
    total = dot(normed, w_first)
    hidden, factors = swiglu(plan, total[:, plan.joined :])
    empty = jnp.zeros((normed.shape[0], width), BF)
    rotated, attn, lse = layer.attend(total[:, : plan.joined], empty, layer.tables)
    wide = jnp.concatenate([attn, *hidden], axis=1)
    branches = scatter(dot_last(wide, w_second).astype(BF), "ctx")
    total = dot(cot, w_second)
    body = total[:, width : width + plan.body]
    tail = total[:, width + plan.body :]
    d_both = jnp.concatenate([body, body, tail, tail], axis=1) * jnp.concatenate(factors, axis=1)
    d_attn = total[:, :width].astype(BF)
    d_joined = layer.attend_back(rotated, attn, d_attn, lse, layer.tables)
    d_first = jnp.concatenate([d_joined, d_both.astype(BF)], axis=1)
    d_normed = scatter(dot_last(d_first, w_first).astype(BF), "ctx")
    sums = [scatter(dot_first(*v).astype(BF), "dp") for v in ((normed, d_first), (cot, wide))]
    begins = (0, plan.joined, plan.first)
    grads = unpack_rows(plan, swap(pack_rows(own, n, [[v] for v in sums])), [0, 1, 2, 3, 4], begins)
    input_grad, norm_sums = layer.norm_back(d_normed, standard, inverse, gain)
    return layer.finish_output(branches), input_grad, scatter(norm_sums, ("dp", "ctx")), grads


def swaps(bit, n):
    return [(i, i ^ bit) for i in range(n)]


class State:
    def __init__(self, **arrays):
        self.held = arrays

    def __getitem__(self, name):
        return self.held[name]

    def drop(self, *names):
        for name in names:
            del self.held[name]

    def tick(self, before=(), sends=(), work=()):
        for action in before:
            self.held.update(action(self.held))
        view = dict(self.held)
        for name, source, axis, pairs in sends:
            view[name] = lax.ppermute(self.held[source], axis, pairs)
        for action in work:
            view.update(action(view))
        names = list(view)
        held = lax.optimization_barrier([view[name] for name in names])
        self.held = dict(zip(names, held))


def on_grid(layer, weights, scales):
    plan = layer.plan
    n, own, features = plan.n, plan.own, layer.features
    ctx, dp = lax.axis_index("ctx"), lax.axis_index("dp")
    z = ctx // 2
    inner = (z == 1) | (z == 2)
    quarter = features // 4
    side, pair = ("ctx", swaps(1, n)), ("ctx", swaps(2, n))
    middle = ("ctx", [(2, 4), (3, 5), (4, 2), (5, 3)])
    outward = ("ctx", [(2, 0), (3, 1), (4, 6), (5, 7)])
    inward = ("ctx", [(b, a) for a, b in outward[1]])
    core, across = ("dp", swaps(1, 4)), ("dp", swaps(2, 4))

    def blocks_of(v, first, steps):
        blocks = [
            lax.dynamic_slice_in_dim(v, (first ^ step) * quarter, quarter, 1) for step in steps
        ]
        return jnp.concatenate(blocks, axis=1)

    def reorder(v):
        return blocks_of(v, dp, (0, 2, 1, 3))

    def unorder(v):
        return blocks_of(v, (dp % 2) * 2 + dp // 2, (0, 2, 1, 3))

    opened = {}

    def doubled(held, axis, bit, size):
        mine = lax.axis_index(axis) // bit % 2
        got = lax.ppermute(held, axis, swaps(bit, size))
        first, second = jnp.where(mine == 0, held, got), jnp.where(mine == 0, got, held)
        return jnp.concatenate([first, second], axis=0)

    def begin(s):
        held = scales.reshape(1, 2, own)
        for bit in (1, 2, 4):
            held = doubled(held, "ctx", bit, n)
        packed, second = pack_columns(plan, weights, scales)
        packed, held, c0 = lax.optimization_barrier((packed, held, s["c0"]))
        packed = lax.all_to_all(packed, "ctx", split_axis=0, concat_axis=0, tiled=True)
        made = {"c0x": lax.ppermute(c0, *side), "c1": lax.ppermute(c0, *pair)}
        for bit in (1, 2):
            held = doubled(held, "dp", bit, 4)
        normed, gain = layer.norm(standard, held)
        n0 = reorder(normed)
        made |= {"n0": n0, "gain": gain, "n0x": lax.ppermute(n0, *side)}
        made |= {"n1": lax.ppermute(n0, *pair), "n2i": lax.ppermute(n0, *middle)}
        parts = unpack_columns(plan, packed, True)
        return made | {"second": second} | dict(zip(("a0", "b0", "ab0"), parts))

    def second_in(s):
        opened["second"] = lax.all_to_all(
            s["second"], "ctx", split_axis=0, concat_axis=0, tiled=True
        )
        return {}

    def select(name):
        return lambda s: {name: jnp.where(inner, s[name + "i"], s[name + "o"])}

    def plus(name, *parts):
        return lambda s: {name: sum(s[part].astype(F32) for part in parts).astype(BF)}

    def pieces(s, name):
        names = "a0 b0 a2 b2 ab1 a3 b3" if name == "ab" else "w0 w2 w1 w3"
        return [s[key] for key in names.split()]

    def slots(s, letter):
        return [s.get(letter + i) for i in ("0", "0x", "1", "1x", "2", "2x", "3", "3x")]

    def streamed(name, letter, weight, names, finish, widths, extra, places):
        def work(s):
            done = [s[key] for key in names] if places[0] else []
            held = (slots(s, letter), places, pieces(s, weight), [s[key] for key in extra])
            made = stream(name, *held, functools.partial(finish, plan), widths, done)
            return dict(zip(names, made))

        return work

    def project(*places):
        names = ("n", "joined", "factors", "wide")
        widths = [(plan.joined, F32), (2 * plan.units, BF), (plan.second, BF)]
        return streamed("project", "n", "ab", names, project_finish, widths, [], places)

    def bring_back(*places):
        names = ("c", "d_attn", "d_both")
        widths = [(plan.width, BF), (2 * plan.units, BF)]
        held = ("factors",)
        return streamed("bring_back", "c", "w", names, return_finish, widths, held, places)

    def tables(s):
        return {"tables": layer.tables}

    def attend(s):
        made = layer.attend(s["joined"], s["wide"], s["tables"])
        return dict(zip(("rotated", "wide", "lse"), made))

    def attend_back(s):
        d_joined = layer.attend_back(
            s["rotated"], s["wide"], s["d_attn"], s["lse"], s["tables"]
        )
        return {"d_joined": d_joined}

    def scattered(name, letter, lefts, weight, places):
        def work(s):
            size = s["c0"].shape[0]
            made = spread(name, [s[v] for v in lefts], pieces(s, weight), places, size)
            keys = [f"{letter}{place}{kind}" for place in places for kind in "ka"]
            return dict(zip(keys, made))

        return work

    def output_part(*places):
        return scattered("output_part", "o", ["wide"], "w", places)

    def normed_part(*places):
        return scattered("normed_part", "d", ["d_joined", "d_both"], "ab", places)

    factors = {"J": ("n", "d_joined"), "G": ("n", "d_both"), "W": ("c", "wide")}

    def product(s, name, begin, end):
        left, right = factors[name]
        rows = slice(int(begin * quarter), int(end * quarter))
        return dot_first(s[left][:, rows], s[right])

    def grad_a(name):
        return lambda s: {name + "A": product(s, name, 2, 4).astype(BF)}

    def grad_b(name):
        def work(s):
            total = product(s, name, 1, 2) + s[name + "Ar"][quarter:].astype(F32)
            return {name + "B": total.astype(BF)}

        return work

    def grad_c(name):
        def work(s):
            total = product(s, name, 0, 1) + s[name + "Ar"][:quarter].astype(F32)
            return {name + "C": (total + s[name + "Br"].astype(F32)).astype(BF)}

        return work

    def half_b(step):
        def work(s):
            rows = slice((2 + step) * quarter // 2, (3 + step) * quarter // 2)
            total = product(s, "G", 1 + step / 2, 1.5 + step / 2) + s["GAr"][rows].astype(F32)
            return {f"GB{step + 1}": total.astype(BF)}

        return work

    def half_c(step):
        def work(s):
            rows = slice(step * quarter // 2, (step + 1) * quarter // 2)
            total = product(s, "G", step / 2, (step + 1) / 2) + s["GAr"][rows].astype(F32)
            return {f"GC{step + 1}": (total + s[f"GB{step + 1}r"].astype(F32)).astype(BF)}

        return work

    def to(name, source, way):
        return (name, source, *way)

    def cross(name):
        return lambda s: {name + "Ar": lax.ppermute(s[name + "A"], *core)}

    def send_a(name):
        return to(name + "Ar", name + "A", core)

    def send_b(name):
        return to(name + "Br", name + "B", across)

    def packed_rows(*names):
        def work(s):
            chunks = [[s[name + "C"]] if name != "G" else [s["GC1"], s["GC2"]] for name in names]
            return {names: pack_rows(own, n, chunks)}

        return work

    def swap_packed(*names):
        def work(s):
            opened[names] = lax.all_to_all(
                s[names], "ctx", split_axis=0, concat_axis=0, tiled=True
            )
            return {}

        return work

    def norm_back(s):
        input_grad, sums = layer.norm_back(unorder(s["d"]), standard, inverse, s["gain"])

        def halved(sums, dim, axis, bit, size):
            mine = lax.axis_index(axis) // bit % 2
            first, second = jnp.split(sums, 2, axis=dim)
            give = jnp.where(mine == 0, second, first)
            return jnp.where(mine == 0, first, second) + lax.ppermute(give, axis, swaps(bit, size))

        sums = sums.reshape(4, 2, 2, 2, 2 * own)
        for dim, bit in ((3, 1), (2, 2), (1, 4)):
            sums = halved(sums, dim, "ctx", bit, n)
        names = ("J", "W")
        packed, sums = lax.optimization_barrier((s[names], sums))
        opened[names] = lax.all_to_all(packed, "ctx", split_axis=0, concat_axis=0, tiled=True)
        sums = sums.reshape(4, 2 * own)
        for bit in (2, 1):
            sums = halved(sums, 0, "dp", bit, 4)
        return {"input_grad": input_grad, "norm_sums": sums}

    def y(name):
        return to(name + "2", name + "0", across)

    def near(name):
        return to(name + "1", name + "0", core)

    def far(name):
        return to(name + "3", name + "2", core)

    standard, inverse = layer.standardize()
    st = State(c0=reorder(layer.cot))
    tick = st.tick
    tick((), (), [begin])
    tick(
        (),
        [
            to("n1x", "n1", side),
            to("n3i", "n1", middle),
            to("n2o", "n2i", outward),
            y("a"),
            near("ab"),
        ],
        [second_in, tables],
    )
    tick(
        [select("n2")],
        [
            to("n2x", "n2", side),
            to("n3o", "n3i", outward),
            to("c2i", "c0", middle),
            y("b"),
            far("a"),
        ],
    )
    tick(
        [select("n3")],
        [
            to("n3x", "n3", side),
            to("c2o", "c2i", outward),
            to("c3i", "c1", middle),
            far("b"),
        ],
        [project(0, 1, 2)],
    )
    tick(
        [select("c2"), lambda s: {"w0": unpack_columns(plan, opened["second"], False)[0]}],
        [to("c2x", "c2", side), to("c3o", "c3i", outward), y("w"), near("w")],
        [project(3), attend],
    )
    tick(
        [select("c3")],
        [to("c3x", "c3", side), to("c1x", "c0x", pair), far("w")],
        [output_part(0, 1, 2, 3), bring_back(0, 2)],
    )
    tick(
        (),
        [to("o3x", "o3a", side), to("o1p", "o1a", pair)],
        [bring_back(1, 3), grad_a("G")],
    )
    tick(
        [plus("o3", "o3k", "o3x")],
        [to("o2x", "o2a", side), to("o3i", "o3", inward), send_a("G")],
        [attend_back, half_b(0)],
    )
    tick(
        [plus("o2", "o2k", "o2x"), plus("o3", "o3", "o3i"), plus("o0a", "o0a", "o1p")],
        [to("o0x", "o0a", side), to("o2i", "o2", inward), to("o3m", "o3", middle), to("GB1r", "GB1", across)],
        [normed_part(1, 3), half_b(1)],
    )
    tick(
        [plus("o2", "o2", "o2i"), plus("o1", "o1k", "o3m")],
        [to("d3x", "d3a", side), to("o2m", "o2", middle), to("o1r", "o1", pair), to("GB2r", "GB2", across)],
        [normed_part(0, 2), half_c(0), half_c(1), packed_rows("G")],
    )
    tick(
        [plus("d3", "d3k", "d3x")],
        [to("d2x", "d2a", side), to("d3i", "d3", inward)],
        [
            swap_packed("G"),
            grad_a("J"),
            cross("J"),
            grad_b("J"),
            grad_a("W"),
            plus("o", "o0k", "o0x", "o2m", "o1r"),
        ],
    )
    tick(
        [plus("d2", "d2k", "d2x"), plus("d3", "d3", "d3i")],
        [
            to("d1x", "d1a", side),
            to("d2i", "d2", inward),
            to("d3m", "d3", middle),
            send_b("J"),
            send_a("W"),
        ],
        [grad_b("W"), grad_c("J")],
    )
    tick(
        [plus("d2", "d2", "d2i"), plus("d1", "d1k", "d1x", "d3m")],
        [to("d0x", "d0a", side), to("d2m", "d2", middle), to("d1r", "d1", pair), send_b("W")],
        [grad_c("W"), packed_rows("J", "W")],
    )
    tick([plus("d", "d0k", "d0x", "d2m", "d1r")], (), [norm_back])
    gate_grad, up_grad = unpack_rows(plan, opened["G",], [2, 3], (0, 0, 0))
    begins = (0, 0, plan.joined)
    joined_grad, out_grad, down_grad = unpack_rows(plan, opened["J", "W"], [0, 1, 4], begins)
    grads = [joined_grad, out_grad, gate_grad, up_grad, down_grad]
    return layer.finish_output(unorder(st["o"])), st["input_grad"], st["norm_sums"], grads


def on_device(
    n_ctx,
    n_dp,
    inputs,
    norm_gain,
    norm_bias,
    joined_weight,
    gate_weight,
    up_weight,
    out_weight,
    down_weight,
    cotangent,
    lengths,
):
    grid = (n_ctx, n_dp) == (8, 4)
    if grid:
        ctx = lax.axis_index("ctx")
        z, x = ctx // 2, ctx % 2
        high = z >= 2
        order = [z, z ^ 1, jnp.where(high, 1, 2), jnp.where(high, 0, 3)]
        natural = [2 * o + (x ^ r) for o in order for r in range(2)]
        slots = jnp.zeros((n_ctx,), jnp.int32)
        for slot, part in enumerate(natural):
            slots = jnp.where(jnp.arange(n_ctx) == part, slot, slots)
    else:
        slots = jnp.arange(n_ctx, dtype=jnp.int32)
    units = gate_weight.shape[1] // n_ctx
    layer = Layer(n_ctx, slots, inputs, norm_gain, cotangent, lengths, units)
    weights = (joined_weight, out_weight, gate_weight, up_weight, down_weight)
    scales = jnp.concatenate([norm_gain, norm_bias])
    run = on_grid if grid else on_any_mesh
    output, input_grad, norm_sums, grads = run(layer, weights, scales)
    joined_grad, out_grad, gate_grad, up_grad, down_grad = grads
    return (
        output.reshape(inputs.shape),
        input_grad.reshape(inputs.shape),
        norm_sums[0, : layer.own],
        norm_sums[0, layer.own :],
        joined_grad,
        gate_grad,
        up_grad,
        out_grad,
        down_grad,
    )


def solution(mesh):
    rows = P(("dp", "ctx"), None)
    vector = P(("dp", "ctx"))
    tokens = P("dp", "ctx", None)
    return jax.shard_map(
        functools.partial(on_device, mesh.shape["ctx"], mesh.shape["dp"]),
        mesh=mesh,
        in_specs=(tokens, vector, vector, rows, rows, rows, rows, rows, tokens, P("dp")),
        out_specs=(tokens, tokens, vector, vector, rows, rows, rows, rows, rows),
        check_vma=False,
    )
```
